128 devices in a mesh: comp: 2 (over y_lo), lat: 8 (over y_hi, z), lon: 8 (over x, core).
Axes of the slice: x: 4, y: 4 (y_hi: 2, y_lo: 2; y = y_hi * 2 + y_lo), z: 4, core: 2. Of those that a mesh axis runs over, the one named last changes fastest.
Arguments:
- adjoint_state: float32 [2, 32, 256, 1024], P('comp', None, 'lat', 'lon'), may hold values from -6 to 6
- winds: float32 [2, 2, 32, 256, 1024], P(None, 'comp', None, 'lat', 'lon'), may hold values from -0.3 to 0.3
- block_inverse: float32 [2, 8, 4, 4, 256, 1024], P('comp', None, None, None, 'lat', 'lon'), may hold values from -0.5 to 1.5
- flux_coef: float32 [2, 4, 256, 1024], P('comp', None, 'lat', 'lon'), may hold values from 0.2 to 1
- sea_mask: int32 [256, 1024], P('lat', 'lon'), may hold values 0 or 1
- intersection_cell: int32 [2, 4, 256, 1024], P(None, None, 'lat', 'lon'), may hold values from 0 to 1023, as said below
- intersection_weight: float32 [4, 256, 1024], P(None, 'lat', 'lon'), may hold values from 0.1 to 1
- fold_map: int32 [1024], replicated, may hold values from 0 to 1023, as said below
Outputs:
- adjoint_final: float32 [2, 32, 256, 1024], P('comp', None, 'lat', 'lon')
The draws below stay inside these ranges and needn't reach their ends.
Inputs may be any that keep to these rules, and one draw needn't show every extreme that they name: intersection_cell[0, k, i, j] lies within one row of i, intersection_cell[1, k, i, j] within one column of j counted periodically; entry k = 0 is the cell (i, j) itself. fold_map[j] = (o - j) mod 1024 for one offset o of 0 to 1023, the same for every j; so fold_map[fold_map[j]] = j.
All inputs are finite; a program needn't handle non-finite values. No bound on the sum of `sea_mask` on one device may be relied on, other than what follows from the above.
Results may differ from the reference program's by a relative error of at most 0.0001.
Values sent between devices are 32-bit elements; how exact they have to be, the bound alone decides.
No kernel may reach another device: no remote copies, remote signals or barrier semaphores. Data moves between devices by JAX's collectives and lax.ppermute only.
A program may use at most 128 MiB of HBM per device.

```python
import math
import jax
import jax.numpy as jnp

LEV = 32
BLK = 4
NBLK = 8
NLAT = 256
NLON = 1024
NINT = 2
SUB = 3
KOV = 4


def draw_block_inverse(key, part):
    key = jax.random.fold_in(key, 11)
    key_diag, key_off = jax.random.split(key)
    shape = (2, NBLK, BLK, BLK, NLAT, NLON)
    diagonal = jax.random.uniform(key_diag, shape, jnp.float32, 0.7, 1.3)
    offdiag = jnp.clip(0.2 * jax.random.normal(key_off, shape, jnp.float32), -0.45, 0.45)
    identity = jnp.eye(BLK, dtype=jnp.float32)[None, None, :, :, None, None]
    return identity * diagonal + (1.0 - identity) * offdiag


def draw_intersection_cell(key, part):
    key = jax.random.fold_in(key, 23)
    key_row, key_col = jax.random.split(key)
    shape = (KOV, NLAT, NLON)
    row_step = jax.random.randint(key_row, shape, -1, 2)
    col_step = jax.random.randint(key_col, shape, -1, 2)
    first = (jnp.arange(KOV) == 0)[:, None, None]
    row_step = jnp.where(first, 0, row_step)
    col_step = jnp.where(first, 0, col_step)
    row_base = jnp.arange(NLAT, dtype=jnp.int32)[None, :, None]
    col_base = jnp.arange(NLON, dtype=jnp.int32)[None, None, :]
    rows_out = jnp.clip(row_base + row_step, 0, NLAT - 1)
    cols_out = (col_base + col_step) % NLON
    return jnp.stack([rows_out, cols_out]).astype(jnp.int32)


def draw_fold_map(key, part):
    key = jax.random.fold_in(key, 37)
    offset = jax.random.randint(key, (), 0, NLON)
    return ((offset - jnp.arange(NLON, dtype=jnp.int32)) % NLON).astype(jnp.int32)


def place_ends(array, rng, low, high):
    dims = array.shape
    place = [jax.random.randint(jax.random.fold_in(rng, axis), (), 0, dims[axis]) for axis in range(len(dims))]
    array = array.at[tuple(place)].set(low)
    longest = dims.index(max(dims))
    place[longest] = (place[longest] + 1) % dims[longest]
    return array.at[tuple(place)].set(high)


def steps_of(rng, shape, cuts, low, top_value):
    loudness = 1.0
    for axis_at, shards_of in cuts:
        steps = jax.random.uniform(jax.random.fold_in(jax.random.fold_in(rng, 6), axis_at), (shards_of,), jnp.float32, low / len(cuts), top_value / len(cuts))
        loudness = loudness * jnp.repeat(jnp.exp(steps), shape[axis_at] // shards_of).reshape((-1,) + (1,) * (len(shape) - 1 - axis_at))
    return loudness


def bell_draw(own_key, extent, deviation, limit, cuts=(), kind=jnp.bfloat16):
    values = jax.random.normal(own_key, extent, jnp.float32) * deviation
    if len(cuts) > 0:
        values = steps_of(own_key, extent, cuts, -0.22, 0.18) * values
    return jnp.clip(values, min=-limit, max=limit).astype(kind)


def setup_inputs(seed: int = 0) -> dict:
    seeds = jax.random.split(jax.random.key(seed), 9)
    return {
        "adjoint_state": bell_draw(seeds[0], (2, LEV, NLAT, NLON), 1.0, 6.0, ((0, 2), (2, 8), (3, 8)), jnp.float32),
        "winds": jnp.clip(jax.random.uniform(seeds[1], (2, 2, LEV, NLAT, NLON), jnp.float32, -0.3, 0.3) * steps_of(seeds[1], (2, 2, LEV, NLAT, NLON), ((1, 2), (3, 8), (4, 8)), -0.4, 0.0), -0.3, 0.3),
        "block_inverse": draw_block_inverse(jax.random.fold_in(seeds[8], 71), 0),
        "flux_coef": jnp.clip(jnp.exp(math.log(1.0) - 1.609438 * jax.random.uniform(seeds[3], (2, 4, NLAT, NLON), jnp.float32) ** steps_of(seeds[3], (2, 4, NLAT, NLON), ((0, 2), (2, 8), (3, 8)), -0.2, 0.2)), 0.2, 1.0),
        "sea_mask": place_ends((jax.random.randint(seeds[4], (NLAT, NLON), 0, 4) < 3).astype(jnp.int32), jax.random.fold_in(seeds[4], 1), 0, 1),
        "intersection_cell": draw_intersection_cell(jax.random.fold_in(seeds[8], 71), 0),
        "intersection_weight": jnp.clip(jnp.exp(math.log(1.0) - 2.3025851 * jax.random.uniform(seeds[6], (KOV, NLAT, NLON), jnp.float32) ** steps_of(seeds[6], (KOV, NLAT, NLON), ((1, 8), (2, 8)), -0.2, 0.2)), 0.1, 1.0),
        "fold_map": draw_fold_map(jax.random.fold_in(seeds[8], 71), 0),
    }


DIFFUSE = 0.15


def pad_field(field, fold_map, top_sign):
    wrapped = jnp.concatenate([field[:, :, -1:], field, field[:, :, :1]], axis=2)
    north_row = top_sign * jnp.take(field[:, -1, :], fold_map, axis=1)
    north_row = jnp.pad(north_row, ((0, 0), (1, 1)))[:, None, :]
    south_row = jnp.zeros_like(north_row)
    return jnp.concatenate([south_row, wrapped, north_row], axis=1)


def advect(tracer, wind_u, wind_v, fold_map, top_sign):
    zonal = wind_u * tracer
    merid = wind_v * tracer
    tracer_pad = pad_field(tracer, fold_map, top_sign)
    zonal_pad = pad_field(zonal, fold_map, -top_sign)
    merid_pad = pad_field(merid, fold_map, -top_sign)
    result = tracer + 0.5 * (zonal_pad[:, 1:-1, 2:] - zonal_pad[:, 1:-1, :-2])
    result = result + 0.5 * (merid_pad[:, 2:, 1:-1] - merid_pad[:, :-2, 1:-1])
    beside_all = tracer_pad[:, 2:, 1:-1] + tracer_pad[:, :-2, 1:-1] + tracer_pad[:, 1:-1, 2:] + tracer_pad[:, 1:-1, :-2]
    return result + DIFFUSE * (beside_all - 4.0 * tracer)


def vertical(tracer, inverse):
    blocks = inverse.shape[0]
    width = inverse.shape[1]
    column = tracer.reshape(blocks, width, tracer.shape[1], tracer.shape[2])
    result = jnp.zeros_like(column)
    for inner in range(width):
        result = result + inverse[:, :, inner] * column[:, None, inner]
    return result.reshape(tracer.shape)


def remap_all(fluxes, intersection_cell, intersection_weight):
    gathered = fluxes[:, intersection_cell[0], intersection_cell[1]]
    return jnp.sum(intersection_weight[None] * gathered, axis=1)


def reference(adjoint_state, winds, block_inverse, flux_coef, sea_mask, intersection_cell, intersection_weight, fold_map):
    atmosphere = adjoint_state[0]
    ocean_field = adjoint_state[1]
    wet = sea_mask.astype(jnp.float32)
    for window in range(NINT):
        for sweep in range(SUB):
            atmosphere = advect(atmosphere, winds[0, 0], winds[1, 0], fold_map, jnp.float32(0.0))
            ocean_field = advect(ocean_field, winds[0, 1], winds[1, 1], fold_map, jnp.float32(1.0)) * wet
        atmosphere = vertical(atmosphere, block_inverse[0])
        ocean_field = vertical(ocean_field, block_inverse[1])
        air_flux = flux_coef[0] * (atmosphere[0] * wet)[None]
        sea_flux = flux_coef[1] * (ocean_field[0] * wet)[None]
        to_air = remap_all(sea_flux, intersection_cell, intersection_weight)
        to_sea = remap_all(air_flux, intersection_cell, intersection_weight)
        atmosphere = atmosphere.at[0].add(jnp.sum(flux_coef[0] * to_air, axis=0))
        ocean_field = ocean_field.at[0].add(jnp.sum(flux_coef[1] * to_sea, axis=0) * wet)
    return jnp.stack([atmosphere, ocean_field])
```

```python
import functools

import jax
import jax.numpy as jnp
from jax import lax
from jax.experimental import pallas as pl
from jax.experimental.pallas import tpu as pltpu
from jax.sharding import PartitionSpec as P

DIFFUSE = 0.15
ROWS = 32
EXT = 48
COLS = 128
BLOCKS = 8
F32 = jnp.float32
AXES = ("comp", "lat", "lon")
LAT, LON = 8, 8
SLABS = 9
SLAB = 120
VMEM = pl.BlockSpec(memory_space=pltpu.VMEM)
SMEM = pl.BlockSpec(memory_space=pltpu.SMEM)
PARAMS = pltpu.CompilerParams(vmem_limit_bytes=48 * 1024 * 1024)


def block_pieces(n_is_zero):
    pieces = []
    if n_is_zero:
        for a in range(4):
            pieces.append((0, a, 0, 8 * a, 8))
            pieces.append((1, a, 0, 32 + 8 * a, 8))
            pieces.append((2, a, 0, 64 + 7 * a, 7))
        for b in range(4):
            pieces.append((3 + b, 0, 0, 92 + 5 * b, 5))
            for a in range(1, 4):
                pieces.append((3 + b, a, 1, 4 * (4 * (a - 1) + b), 4))
    else:
        for a in range(4):
            pieces.append((0, a, 0, 6 * a, 6))
            pieces.append((1, a, 0, 24 + 6 * a, 6))
            pieces.append((2, a, 0, 48 + 5 * a, 5))
            for b in range(4):
                pieces.append((3 + b, a, 0, 68 + 3 * (4 * a + b), 3))
    return pieces


SINGLES = (
    [(0, f, 1, 48 + 5 * f, 5) for f in range(4)]
    + [(1 + s // 4, s % 4, 1, 68 + 4 * s, 4) for s in range(9)]
    + [(3, 1, 0, 112, 8), (3, 2, 1, 104, 8)]
)


def mirrored_single(quad, member):
    if quad in (1, 2) or (quad == 3 and member == 0):
        s = 8 - (4 * (quad - 1) + member)
        return 1 + s // 4, s % 4
    return quad, member


def pack_rows_kernel(pos, lam, winds, inv, fc, mask, cell, weight, x_out, top_out, bottom_out, mirror_out):
    is_ocean, lat_pos, lon_pos = pos[0], pos[1], pos[2]
    wet = mask[...].astype(F32)
    x_out[3, 1] = wet
    x_out[3, 2] = jnp.where(is_ocean == 1, wet, jnp.ones_like(wet))
    x_out[3, 3] = jnp.zeros_like(wet)
    for f in range(4):
        x_out[0, f] = fc[f]
    rows = lat_pos * ROWS + lax.broadcasted_iota(jnp.int32, (ROWS, COLS), 0)
    cols = lon_pos * COLS + lax.broadcasted_iota(jnp.int32, (ROWS, COLS), 1)
    row_shift = [cell[0, k] - rows for k in range(4)]
    col_shift = []
    for k in range(4):
        d = cell[1, k] - cols
        d = jnp.where(d > 1, d - LON * COLS, d)
        col_shift.append(jnp.where(d < -1, d + LON * COLS, d))
    for s in range(9):
        total = jnp.zeros((ROWS, COLS), F32)
        for k in range(4):
            hit = (row_shift[k] == s // 3 - 1) & (col_shift[k] == s % 3 - 1)
            total = total + jnp.where(hit, weight[k], 0.0)
        x_out[1 + s // 4, s % 4] = total

    flip = 7 - lax.broadcasted_iota(jnp.int32, (8, COLS), 0)

    def reverse(tile):
        return jnp.take_along_axis(tile, flip, axis=0, mode="promise_in_bounds")

    def field_ref(field, n, a):
        if field == 0:
            return lam.at[4 * n + a]
        if field <= 2:
            return winds.at[2 - field, 4 * n + a]
        return inv.at[n, a, field - 3]

    def put(ref, other, slab, at, count, sign):
        top_out[slab, at : at + count, :] = ref[ROWS - count : ROWS, :]
        bottom_out[slab, at : at + count, :] = ref[0:count, :]
        turned = reverse(other[ROWS - 8 : ROWS, :])
        if sign < 0:
            turned = -turned
        mirror_out[slab, at : at + count, :] = turned[0:count, :]

    for field, a, slab, at, count in block_pieces(True):
        ref = field_ref(field, 0, a)
        put(ref, ref, slab, at, count, -1 if field in (1, 2) else 1)
    for quad, member, slab, at, count in SINGLES:
        put(x_out.at[quad, member], x_out.at[mirrored_single(quad, member)], slab, at, count, 1)

    def step(n, carry):
        for field, a, slab, at, count in block_pieces(False):
            ref = field_ref(field, n, a)
            put(ref, ref, n + 1, at, count, -1 if field in (1, 2) else 1)
        return carry

    lax.fori_loop(1, BLOCKS, step, 0)


def lanes():
    return lax.broadcasted_iota(jnp.int32, (8, COLS), 1)


def roll_lanes(x, by):
    by = by % COLS
    return x if by == 0 else pltpu.roll(x, by, axis=1)


def roll_rows(x, by):
    by = by % x.shape[0]
    return x if by == 0 else pltpu.roll(x, by, axis=0)


def pack_cols_kernel(
    pos, south_in, north_in, fold_a, fold_b, lam, winds, inv, x_in,
    hs, hn, hxs, hxn, own, to_west, to_east, north,
):
    is_top, turn = pos[3], pos[4]

    @pl.when(is_top == 0)
    def _():
        north[...] = north_in[...]

    @pl.when(is_top == 1)
    def _():
        lane = lanes()
        source = jnp.where(turn >= lane, turn - lane, turn - lane + COLS)
        first = lane <= turn

        def step(i, carry):
            for t in range(SLAB // 8):
                here = (i, slice(8 * t, 8 * t + 8), slice(None))
                a = jnp.take_along_axis(fold_a[here], source, axis=1, mode="promise_in_bounds")
                b = jnp.take_along_axis(fold_b[here], source, axis=1, mode="promise_in_bounds")
                north[here] = jnp.where(first, a, b)
            return carry

        lax.fori_loop(0, SLABS, step, 0)

    for field, a, slab, at, count in block_pieces(True):
        hs[0, field, a, 8 - count : 8, :] = south_in[slab, at : at + count, :]
        hn[0, field, a, 0:count, :] = north[slab, at : at + count, :]
    for quad, member, slab, at, count in SINGLES:
        hxs[quad, member, 8 - count : 8, :] = south_in[slab, at : at + count, :]
        hxn[quad, member, 0:count, :] = north[slab, at : at + count, :]

    def unpack(n, carry):
        for field, a, slab, at, count in block_pieces(False):
            hs[n, field, a, 8 - count : 8, :] = south_in[n + 1, at : at + count, :]
            hn[n, field, a, 0:count, :] = north[n + 1, at : at + count, :]
        return carry

    lax.fori_loop(1, BLOCKS, unpack, 0)

    lane = lanes()
    group = lane % 32

    def edge_pair(members):
        pair = jnp.zeros((8, COLS), F32)
        for a, x in enumerate(members):
            if x is not None:
                pair = jnp.where((lane >= 32 * a) & (lane < 32 * a + 16), roll_lanes(x, 32 * a + 8), pair)
        return pair

    def dense(n, which, quads, t, old=None):
        rows = slice(8 * t, 8 * t + 8)
        west = jnp.zeros((8, COLS), F32) if old is None else old[0]
        east = jnp.zeros((8, COLS), F32) if old is None else old[1]
        for slot, members in quads.items():
            pair = edge_pair(members)
            own[n, 4 * which + slot, rows, :] = jnp.where(group < 16, pair, roll_lanes(pair, 16))
            here = (group >= 8 * slot) & (group < 8 * slot + 8)
            west = jnp.where(here, roll_lanes(pair, 8 * slot - 8), west)
            east = jnp.where(here, roll_lanes(pair, 8 * slot), east)
        to_west[2 * n + which, rows, :] = west
        to_east[2 * n + which, rows, :] = east

    def member(field, n, a, t):
        if t == 0:
            return hs[n, field, a]
        if t == 5:
            return hn[n, field, a]
        rows = slice(8 * t - 8, 8 * t)
        if field == 0:
            return lam[4 * n + a, rows, :]
        if field <= 2:
            return winds[2 - field, 4 * n + a, rows, :]
        return inv[n, a, field - 3, rows, :]

    def block(n, carry):
        for t in range(6):
            dense(n, 0, {s: [member(s, n, a, t) for a in range(4)] for s in range(3)}, t)
            dense(n, 1, {d: [member(3 + (a + d) % 4, n, a, t) for a in range(4)] for d in range(4)}, t)
        return carry

    lax.fori_loop(0, BLOCKS, block, 0)

    for quad in range(4):
        for t in range(6):
            rows = slice(8 * t, 8 * t + 8)
            members = []
            for a in range(4):
                if quad == 3 and a == 3:
                    members.append(None)
                elif t == 0:
                    members.append(hxs[quad, a])
                elif t == 5:
                    members.append(hxn[quad, a])
                else:
                    members.append(x_in[quad, a, 8 * t - 8 : 8 * t, :])
            dense(quad, 0, {3: members}, t, (to_west[2 * quad, rows, :], to_east[2 * quad, rows, :]))


def ext_lanes():
    return lax.broadcasted_iota(jnp.int32, (EXT, COLS), 1)


class Fields:
    def __init__(self, pos, lam, winds, inv, x_in, hs, hn, hxs, hxn, own, from_west, from_east):
        self.pos, self.lam, self.winds, self.inv, self.x_in = pos, lam, winds, inv, x_in
        self.hs, self.hn, self.hxs, self.hxn = hs, hn, hxs, hxn
        self.own, self.from_west, self.from_east = own, from_west, from_east

    def main(self, field, n, a):
        if field == 0:
            mid = self.lam[4 * n + a]
        elif field <= 2:
            mid = self.winds[2 - field, 4 * n + a]
        else:
            mid = self.inv[n, a, field - 3]
        return jnp.concatenate([self.hs[n, field, a], mid, self.hn[n, field, a]], axis=0)

    def single(self, quad, a):
        return jnp.concatenate([self.hxs[quad, a], self.x_in[quad, a], self.hxn[quad, a]], axis=0)

    def strip(self, n, which, slot):
        group = ext_lanes() % 32
        west = roll_lanes(self.from_west[2 * n + which], -8 * slot)
        east = roll_lanes(self.from_east[2 * n + which], 24 - 8 * slot)
        return jnp.where(group < 8, west, jnp.where(group < 24, self.own[n, 4 * which + slot], east))

    def barrier_masks(self):
        row = lax.broadcasted_iota(jnp.int32, (EXT, COLS), 0)
        apart = self.pos[5] == 1
        keep_c = jnp.where(apart & (row == 40), 0.0, 1.0).astype(F32)
        keep_d = jnp.where(apart & (row == 39), 0.0, 1.0).astype(F32)
        return keep_c, keep_d


def replicate(strip, a):
    lane = ext_lanes()
    out = roll_lanes(strip, -32 * a)
    base = jnp.where(lane < 32, out, 0.0)
    for g in range(1, 4):
        base = jnp.where((lane >= 32 * g) & (lane < 32 * g + 32), roll_lanes(out, 32 * g), base)
    return base


def advect(tracer, merid, zonal, land, masks):
    to_south = (DIFFUSE + 0.5 * merid) * masks[0]
    to_north = (DIFFUSE - 0.5 * merid) * masks[1]
    to_west = DIFFUSE + 0.5 * zonal
    for _ in range(3):
        a = to_west * tracer
        b = (2 * DIFFUSE) * tracer - a
        rest = (1.0 - 4 * DIFFUSE) * tracer
        new = rest + roll_lanes(a, -1) + roll_lanes(b, 1)
        new = new + roll_rows(to_south * tracer, -1) + roll_rows(to_north * tracer, 1)
        tracer = new * land
    return tracer


def advect_block(fields, n, state, land, land_strip, masks):
    for a in range(4):
        state[a] = advect(state[a], fields.main(1, n, a), fields.main(2, n, a), land, masks)
    state[4] = advect(state[4], fields.strip(n, 0, 1), fields.strip(n, 0, 2), land_strip, masks)


def solve_block(fields, n, state):
    old = [state[a] for a in range(5)]
    for a in range(4):
        total = fields.main(3, n, a) * old[0]
        for b in range(1, 4):
            total = total + fields.main(3 + b, n, a) * old[b]
        state[a] = total
    total = fields.strip(n, 1, 0) * old[4]
    for d in range(1, 4):
        total = total + fields.strip(n, 1, d) * roll_lanes(old[4], -32 * d)
    state[4] = total


def main_from_strip(main, strip, a, width):
    lane = ext_lanes()
    main = jnp.where(lane < width, roll_lanes(strip, -(32 * a + 8)), main)
    return jnp.where(lane >= COLS - width, roll_lanes(strip, 104 - 32 * a), main)


def merge(state):
    lane = ext_lanes()
    strip = state[4]
    new_strip = strip
    for a in range(4):
        main = state[a]
        west = (lane >= 32 * a + 11) & (lane < 32 * a + 16)
        east = (lane >= 32 * a + 16) & (lane < 32 * a + 21)
        new_strip = jnp.where(west, roll_lanes(main, 32 * a + 8), new_strip)
        new_strip = jnp.where(east, roll_lanes(main, 32 * a + 24), new_strip)
        state[a] = main_from_strip(main, strip, a, 3)
    state[4] = new_strip


def load_block(fields, n, state):
    for a in range(4):
        state[a] = fields.main(0, n, a)
    state[4] = fields.strip(n, 0, 0)


def fluxes_out(fields, state, payload):
    surface = state[0] * fields.single(3, 1)
    for f in range(4):
        payload[f] = fields.single(0, f) * surface
    wet_strip = roll_lanes(fields.strip(3, 0, 3), -32)
    payload[4] = fields.strip(0, 0, 3) * replicate(state[4] * wet_strip, 0)


def couple(fields, received):
    total = jnp.zeros((EXT, COLS), F32)
    total_strip = jnp.zeros((EXT, COLS), F32)
    weights = [fields.single(1 + s // 4, s % 4) for s in range(9)]
    quads = [fields.strip(q, 0, 3) for q in range(4)]
    strip_weights = [roll_lanes(quads[1 + s // 4], -32 * (s % 4)) for s in range(9)]
    for f in range(4):
        for source, table, coef, is_main in (
            (received[f], weights, fields.single(0, f), True),
            (roll_lanes(received[4], -32 * f), strip_weights, roll_lanes(quads[0], -32 * f), False),
        ):
            part = jnp.zeros((EXT, COLS), F32)
            for dc in (-1, 0, 1):
                moved = roll_lanes(source, -dc)
                for dr in (-1, 0, 1):
                    part = part + table[3 * (dr + 1) + dc + 1] * roll_rows(moved, -dr)
            if is_main:
                total = total + coef * part
            else:
                total_strip = total_strip + coef * part
    land = fields.single(3, 2)
    land_strip = roll_lanes(quads[3], -64)
    return total * land, total_strip * land_strip


def lands(fields):
    return fields.single(3, 2), replicate(fields.strip(3, 0, 3), 2)


def first_kernel(*refs):
    fields = Fields(*refs[:12])
    payload, state = refs[12:]
    land, land_strip = lands(fields)
    load_block(fields, 0, state)
    advect_block(fields, 0, state, land, land_strip, fields.barrier_masks())
    solve_block(fields, 0, state)
    merge(state)
    fluxes_out(fields, state, payload)


def rest_kernel(*refs):
    fields = Fields(*refs[:12])
    out, state = refs[12:]
    land, land_strip = lands(fields)
    masks = fields.barrier_masks()

    def block(n, carry):
        load_block(fields, n, state)
        advect_block(fields, n, state, land, land_strip, masks)
        solve_block(fields, n, state)
        merge(state)
        advect_block(fields, n, state, land, land_strip, masks)
        solve_block(fields, n, state)
        for a in range(4):
            out[4 * n + a] = main_from_strip(state[a], state[4], a, 3)[8:40]
        return carry

    lax.fori_loop(1, BLOCKS, block, 0)


def second_kernel(*refs):
    fields = Fields(*refs[:12])
    received, state_in, payload, state = refs[12:]
    land, land_strip = lands(fields)
    added, added_strip = couple(fields, received)
    lane = ext_lanes()
    strip = state_in[4] + jnp.where(lane < 32, added_strip, 0.0)
    state[0] = main_from_strip(state_in[0] + added, strip, 0, 1)
    for a in range(1, 4):
        state[a] = state_in[a]
    state[4] = strip
    advect_block(fields, 0, state, land, land_strip, fields.barrier_masks())
    solve_block(fields, 0, state)
    for a in range(4):
        state[a] = main_from_strip(state[a], state[4], a, 3)
    fluxes_out(fields, state, payload)


def last_kernel(*refs):
    fields = Fields(*refs[:12])
    received, state, rest, out = refs[12:]
    added, added_strip = couple(fields, received)
    strip = state[4] + added_strip
    out[0] = main_from_strip(state[0] + added, strip, 0, 1)[8:40]
    for a in range(1, 4):
        out[a] = state[a][8:40]
    out[4:32] = rest[4:32]


def call(kernel, out_shapes, args, scratch=(), smem=1, **more):
    return pl.pallas_call(
        kernel,
        out_shape=[jax.ShapeDtypeStruct(s, F32) for s in out_shapes],
        in_specs=[SMEM] * smem + [VMEM] * (len(args) - smem),
        out_specs=[VMEM] * len(out_shapes),
        scratch_shapes=list(scratch),
        compiler_params=PARAMS,
        **more,
    )(*args)


def index(c, a, o):
    return (c * LAT + a) * LON + o % LON


def shift_pairs(da, do):
    return [
        (index(c, a, o), index(c, a + da, o + do))
        for c in range(2)
        for a in range(LAT)
        for o in range(LON)
        if 0 <= a + da < LAT
    ]


def fold_pairs(total):
    return [(index(c, LAT - 1, o), index(c, LAT - 1, total - o)) for c in range(2) for o in range(LON)]


def body(
    adjoint_state,
    winds,
    block_inverse,
    flux_coef,
    sea_mask,
    intersection_cell,
    intersection_weight,
    fold_map,
):
    lam = adjoint_state[0]
    wind = winds[:, 0]
    inv = block_inverse[0]
    comp, lat, lon = (lax.axis_index(name).astype(jnp.int32) for name in AXES)
    offset = fold_map[0]
    top = (lat == LAT - 1).astype(jnp.int32)
    pos = jnp.stack([comp, lat, lon, top, offset % COLS, top * (1 - comp)])

    x, top_rows, bottom_rows, mirror_rows = call(
        pack_rows_kernel,
        [(4, 4, ROWS, COLS)] + [(SLABS, SLAB, COLS)] * 3,
        (pos, lam, wind, inv, flux_coef[0], sea_mask, intersection_cell, intersection_weight),
    )

    def exchange(turn):
        def run(top_rows, bottom_rows, mirror_rows):
            south = lax.ppermute(top_rows, AXES, shift_pairs(1, 0))
            north = lax.ppermute(bottom_rows, AXES, shift_pairs(-1, 0))
            fold_a = lax.ppermute(mirror_rows, AXES, fold_pairs(turn))
            fold_b = lax.ppermute(mirror_rows, AXES, fold_pairs(turn - 1))
            return south, north, fold_a, fold_b

        return run

    south, north, fold_a, fold_b = lax.switch(
        offset // COLS, [exchange(turn) for turn in range(LON)], top_rows, bottom_rows, mirror_rows
    )
    halo = (BLOCKS, 7, 4, 8, COLS)
    halo_x = (4, 4, 8, COLS)
    cols = (2 * BLOCKS, EXT, COLS)
    hs, hn, hxs, hxn, own, to_west, to_east = call(
        pack_cols_kernel,
        [halo, halo, halo_x, halo_x, (BLOCKS, 8, EXT, COLS), cols, cols],
        (pos, south, north, fold_a, fold_b, lam, wind, inv, x),
        [pltpu.VMEM((SLABS, SLAB, COLS), F32)],
    )
    from_west = lax.ppermute(to_east, AXES, shift_pairs(0, 1))
    from_east = lax.ppermute(to_west, AXES, shift_pairs(0, -1))
    args = (pos, lam, wind, inv, x, hs, hn, hxs, hxn, own, from_west, from_east)
    five = (5, EXT, COLS)

    def across(value):
        return lax.ppermute(value, "comp", [(0, 1), (1, 0)])

    payload, state = call(first_kernel, [five, five], args)
    received = across(payload)
    (rest,) = call(rest_kernel, [(32, ROWS, COLS)], args, [pltpu.VMEM(five, F32)])
    payload, state = call(second_kernel, [five, five], args + (received, state))
    received = across(payload)
    (out,) = call(last_kernel, [(32, ROWS, COLS)], args + (received, state, rest))
    return out[None]


def solution(mesh):
    return jax.shard_map(
        body,
        mesh=mesh,
        in_specs=(
            P("comp", None, "lat", "lon"),
            P(None, "comp", None, "lat", "lon"),
            P("comp", None, None, None, "lat", "lon"),
            P("comp", None, "lat", "lon"),
            P("lat", "lon"),
            P(None, None, "lat", "lon"),
            P(None, "lat", "lon"),
            P(),
        ),
        out_specs=P("comp", None, "lat", "lon"),
        check_vma=False,
    )
```

```python
import functools

import jax
import jax.numpy as jnp
from jax import lax
from jax.experimental import pallas as pl
from jax.experimental.pallas import tpu as pltpu
from jax.sharding import PartitionSpec as P

DIFFUSE = 0.15
ROWS = 32
EXT = 48
COLS = 128
BLOCKS = 8
F32 = jnp.float32
AXES = ("comp", "lat", "lon")
LAT, LON = 8, 8
VMEM = pl.BlockSpec(memory_space=pltpu.VMEM)
ANY = pl.BlockSpec(memory_space=pl.ANY)
HBM = pl.BlockSpec(memory_space=pltpu.HBM)
SMEM = pl.BlockSpec(memory_space=pltpu.SMEM)
PARAMS = pltpu.CompilerParams(vmem_limit_bytes=16 * 1024 * 1024)
FULL = pltpu.CompilerParams(vmem_limit_bytes=63 * 1024 * 1024)


def places():
    comp, lat, lon = (lax.axis_index(name) for name in AXES)
    return comp, lat, lon, lat == LAT - 1


def first_pieces():
    pieces = []
    for a in range(4):
        pieces.append((0, 0, a, 8 * a, 8))
        pieces.append((1, 0, a, 32 + 8 * a, 8))
        pieces.append((2, 0, a, 64 + 7 * a, 7))
    for b in range(4):
        pieces.append((3 + b, 0, 0, 92 + 5 * b, 5))
        for a in range(1, 4):
            pieces.append((3 + b, 0, a, 120 + 4 * (4 * (a - 1) + b), 4))
    return pieces


def rest_pieces():
    pieces = []
    for n in range(1, BLOCKS):
        at = 240 + 32 * (n - 1)
        for a in range(4):
            pieces.append((0, n, a, at + 3 * a, 3))
            pieces.append((1, n, a, at + 12 + 3 * a, 3))
            pieces.append((2, n, a, at + 24 + 2 * a, 2))
    return pieces


ROW_BUFFER = 240 + 32 * (BLOCKS - 1)
SINGLES = (
    [(0, f, 168 + 5 * f, 5) for f in range(4)]
    + [(1 + s // 4, s % 4, 188 + 4 * s, 4) for s in range(9)]
    + [(3, 1, 112, 8), (3, 2, 224, 8)]
)


def mirrored_single(quad, member):
    if quad in (1, 2) or (quad == 3 and member == 0):
        s = 8 - (4 * (quad - 1) + member)
        return 1 + s // 4, s % 4
    return quad, member


def copy_all(pairs, sem):
    copies = [pltpu.make_async_copy(a, b, sem.at[k]) for k, (a, b) in enumerate(pairs)]
    for copy in copies:
        copy.start()
    for copy in copies:
        copy.wait()


def reverse(tile):
    flip = 7 - lax.broadcasted_iota(jnp.int32, (8, COLS), 0)
    return jnp.take_along_axis(tile, flip, axis=0, mode="promise_in_bounds")


def put_piece(store, ref, other, at, count, mirrored_sign):
    end = ref.shape[0]
    store[0, at : at + count, :] = ref[end - count : end, :]
    store[1, at : at + count, :] = ref[0:count, :]
    turned = reverse(other[end - 8 : end, :])
    if mirrored_sign < 0:
        turned = -turned
    store[2, at : at + count, :] = turned[0:count, :]


def field_ref(lam, winds, inv, field, n, a):
    if field == 0:
        return lam.at[4 * n + a]
    if field <= 2:
        return winds.at[2 - field, 4 * n + a]
    return inv.at[n, a, field - 3]


def sign_of(field):
    return -1 if field in (1, 2) else 1


def hand_over(store, first_out, second_out, mirror_out):
    _, lat, _, _ = places()
    odd = lat % 2
    first_out[...] = store[odd]
    second_out[...] = store[1 - odd]
    mirror_out[...] = store[2]


def start_rows_kernel(
    fold, lam_in, winds_in, inv_in, fc_in, mask_in, cell_in, weight_in,
    x_out, first_out, second_out, mirror_out, turn_out,
    store, lam, winds, inv, fc, mask, cell, weight, sem,
):
    comp, lat_pos, lon_pos, _ = places()
    turn_out[0] = fold[0] // COLS
    pairs = [(fc_in, fc), (mask_in, mask), (cell_in, cell), (weight_in, weight)]
    for half, rows in enumerate((pl.ds(0, 8), pl.ds(ROWS - 8, 8))):
        at = pl.ds(8 * half, 8)
        pairs.append((lam_in.at[:, rows], lam.at[:, at]))
        pairs.append((winds_in.at[:, :, rows], winds.at[:, :, at]))
        pairs.append((inv_in.at[pl.ds(0, 1), :, :, rows], inv.at[:, :, :, at]))
    copy_all(pairs, sem)
    wet = mask[...].astype(F32)
    x_out[3, 1] = wet
    x_out[3, 2] = jnp.where(comp == 1, wet, jnp.ones_like(wet))
    x_out[3, 3] = jnp.zeros_like(wet)
    for f in range(4):
        x_out[0, f] = fc[f]
    rows = lat_pos * ROWS + lax.broadcasted_iota(jnp.int32, (ROWS, COLS), 0)
    cols = lon_pos * COLS + lax.broadcasted_iota(jnp.int32, (ROWS, COLS), 1)
    row_shift = [cell[0, k] - rows for k in range(4)]
    col_shift = []
    for k in range(4):
        d = cell[1, k] - cols
        d = jnp.where(d > 1, d - LON * COLS, d)
        col_shift.append(jnp.where(d < -1, d + LON * COLS, d))
    code = [3 * row_shift[k] + col_shift[k] + 4 for k in range(4)]
    weights = [weight[k] for k in range(4)]
    for s in range(9):
        total = jnp.where(code[0] == s, weights[0], 0.0)
        for k in range(1, 4):
            total = total + jnp.where(code[k] == s, weights[k], 0.0)
        x_out[1 + s // 4, s % 4] = total
    for field, n, a, at, count in first_pieces() + rest_pieces():
        ref = field_ref(lam, winds, inv, field, n, a)
        put_piece(store, ref, ref, at, count, sign_of(field))
    for quad, member, at, count in SINGLES:
        put_piece(store, x_out.at[quad, member], x_out.at[mirrored_single(quad, member)], at, count, 1)
    hand_over(store, first_out, second_out, mirror_out)


def lanes():
    return lax.broadcasted_iota(jnp.int32, (8, COLS), 1)


def roll_lanes(x, by):
    by = by % COLS
    return x if by == 0 else pltpu.roll(x, by, axis=1)


def roll_rows(x, by):
    by = by % x.shape[0]
    return x if by == 0 else pltpu.roll(x, by, axis=0)


def pack_columns(slots, own, own_at, to_west, to_east, buffer_at, row_count):
    rows = row_count
    used = [k for k, members in enumerate(slots) if members is not None]
    zero = jnp.zeros((rows, COLS), F32)
    lane = lax.broadcasted_iota(jnp.int32, (len(used) * rows, COLS), 1)
    pair = jnp.zeros((len(used) * rows, COLS), F32)
    for a in range(4):
        values = [zero if slots[k][a] is None else slots[k][a] for k in used]
        moved = roll_lanes(jnp.concatenate(values, axis=0), 32 * a + 8)
        pair = jnp.where((lane >= 32 * a) & (lane < 32 * a + 16), moved, pair)
    strips = jnp.where(lane % 32 < 16, pair, roll_lanes(pair, 16))
    group = lax.broadcasted_iota(jnp.int32, (rows, COLS), 1) % 32
    buffers = -(-len(slots) // 4)
    west, east = [zero] * buffers, [zero] * buffers
    for i, k in enumerate(used):
        own[own_at + k] = strips[i * rows : (i + 1) * rows]
        mine = pair[i * rows : (i + 1) * rows]
        buffer, slot = k // 4, k % 4
        here = (group >= 8 * slot) & (group < 8 * slot + 8)
        west[buffer] = jnp.where(here, roll_lanes(mine, 8 * slot - 8), west[buffer])
        east[buffer] = jnp.where(here, roll_lanes(mine, 8 * slot), east[buffer])
    for buffer in range(buffers):
        to_west[buffer_at + buffer, 0:rows, :] = west[buffer]
        to_east[buffer_at + buffer, 0:rows, :] = east[buffer]


def block_slots(read, extra):
    slots = [[read(field, a) for a in range(4)] for field in range(3)] + [extra]
    return slots + [[read(3 + (a + d) % 4, a) for a in range(4)] for d in range(4)]


def single_slots(read):
    return [[None if q == 3 and a == 3 else read(q, a) for a in range(4)] for q in range(1, 4)]


def own_first_kernel(lam_in, winds_in, inv_in, x_in, own, to_west, to_east, lam, winds, inv, x, sem):
    four = pl.ds(0, 4)
    copy_all(
        [
            (inv_in.at[pl.ds(0, 1)], inv),
            (winds_in.at[:, four], winds),
            (lam_in.at[four], lam),
            (x_in, x),
        ],
        sem,
    )

    def read(field, a):
        return field_ref(lam, winds, inv, field, 0, a)[...]

    slots = block_slots(read, [x[0, f] for f in range(4)])
    slots += single_slots(lambda q, a: x[q, a])
    pack_columns(slots, own, 0, to_west, to_east, 0, ROWS)


def own_rest_kernel(lam, winds, inv, own, to_west, to_east):
    def step(n, carry):
        def read(field, a):
            return field_ref(lam, winds, inv, field, n, a)[...]

        pack_columns(block_slots(read, None), own, 8 * (n - 1), to_west, to_east, 2 * (n - 1), ROWS)
        return carry

    lax.fori_loop(1, BLOCKS, step, 0)


def settle_rows(first_in, second_in, south, north, beyond_fold):
    _, lat, _, is_top = places()
    even = lat % 2 == 0

    @pl.when(even)
    def _():
        south[...] = second_in[...]
        north[...] = first_in[...]

    @pl.when(jnp.logical_not(even))
    def _():
        south[...] = first_in[...]

    @pl.when(jnp.logical_not(even) & jnp.logical_not(is_top))
    def _():
        north[...] = second_in[...]

    pl.when(is_top)(beyond_fold)


def pick(values, at):
    tiles = [
        jnp.take_along_axis(values[8 * t : 8 * t + 8], at, axis=1, mode="promise_in_bounds")
        for t in range(values.shape[0] // 8)
    ]
    return jnp.concatenate(tiles, axis=0)


def halo_first_kernel(
    fold, first_in, second_in, fold_a, fold_b, mid_west, mid_east,
    south, north, h, hx, own, to_west, to_east,
):
    def beyond_fold():
        turn, lane = fold[0] % COLS, lanes()
        source = jnp.where(turn >= lane, turn - lane, turn - lane + COLS)
        keep = lax.broadcasted_iota(jnp.int32, (ROW_BUFFER, COLS), 1) <= turn
        north[...] = jnp.where(keep, pick(fold_a[...], source), pick(fold_b[...], source))

    settle_rows(first_in, second_in, south, north, beyond_fold)
    for field, _, a, at, count in first_pieces():
        h[field, a, 8 - count : 8, :] = south[at : at + count, :]
        h[field, a, 8 : 8 + count, :] = north[at : at + count, :]
    for quad, member, at, count in SINGLES:
        hx[quad, member, 8 - count : 8, :] = south[at : at + count, :]
        hx[quad, member, 8 : 8 + count, :] = north[at : at + count, :]
    slots = block_slots(lambda field, a: h[field, a], [hx[0, f] for f in range(4)])
    slots += single_slots(lambda q, a: hx[q, a])
    pack_columns(slots, own, 0, to_west, to_east, 0, 16)
    to_west[:, 16:EXT, :] = mid_west[...]
    to_east[:, 16:EXT, :] = mid_east[...]


REST = BLOCKS - 1
COL_BUFFER = REST * (EXT + ROWS)


def halo_rest_kernel(south, north, mid_west, mid_east, h, own, to_west, to_east, west, east):
    for field, n, a, at, count in rest_pieces():
        h[n - 1, field, a, 8 - count : 8, :] = south[at : at + count, :]
        h[n - 1, field, a, 8 : 8 + count, :] = north[at : at + count, :]

    def step(n, carry):
        slots = [[h[n, field, a] for a in range(4)] for field in range(3)]
        pack_columns(slots, own, 3 * n, west, east, n, 16)
        return carry

    lax.fori_loop(0, REST, step, 0)
    for out, halo, mid in ((to_west, west, mid_west), (to_east, east, mid_east)):
        for n in range(REST):
            out[EXT * n : EXT * n + 16, :] = halo[n]
            out[EXT * n + 16 : EXT * (n + 1), :] = mid[2 * n]
            at = EXT * REST + ROWS * n
            out[at : at + ROWS, :] = mid[2 * n + 1]


def ext_lanes():
    return lax.broadcasted_iota(jnp.int32, (EXT, COLS), 1)


def barrier_masks():
    comp, _, _, is_top = places()
    row = lax.broadcasted_iota(jnp.int32, (EXT, COLS), 0)
    apart = is_top & (comp == 0)
    keep_c = jnp.where(apart & (row == 40), 0.0, 1.0).astype(F32)
    keep_d = jnp.where(apart & (row == 39), 0.0, 1.0).astype(F32)
    return stack([keep_c] * 5), stack([keep_d] * 5)


def assemble_strip(slot, west, east, mid, halo=None):
    group = lax.broadcasted_iota(jnp.int32, west.shape, 1) % 32
    edge = jnp.where(group < 8, roll_lanes(west, -8 * slot), roll_lanes(east, 24 - 8 * slot))
    inner = (group >= 8) & (group < 24)
    if halo is None:
        return jnp.where(inner, mid, edge)
    return jnp.concatenate(
        [
            jnp.where(inner[0:8], halo[0:8], edge[0:8]),
            jnp.where(inner[0:32], mid, edge[16:48]),
            jnp.where(inner[0:8], halo[8:16], edge[8:16]),
        ],
        axis=0,
    )


class First:
    def __init__(self, lam, winds, inv, h, own, own_halo, from_west, from_east, x_in, hx):
        self.lam, self.winds, self.inv, self.h = lam, winds, inv, h
        self.own, self.own_halo, self.from_west, self.from_east = own, own_halo, from_west, from_east
        self.x_in, self.hx = x_in, hx

    def main(self, field, n, a):
        halo = self.h[field, a]
        mid = field_ref(self.lam, self.winds, self.inv, field, 0, a)[...]
        return jnp.concatenate([halo[0:8], mid, halo[8:16]], axis=0)

    def single(self, quad, a):
        halo = self.hx[quad, a]
        return jnp.concatenate([halo[0:8], self.x_in[quad, a], halo[8:16]], axis=0)

    def strip(self, n, which, slot):
        at = 4 * which + slot
        return assemble_strip(slot, self.from_west[which], self.from_east[which], self.own[at], self.own_halo[at])

    def single_strip(self, quad):
        return self.strip(0, 0, 3) if quad == 0 else self.strip(0, 2, quad - 1)


class Rest:
    def __init__(self, lam, winds, inv, h, own, own_halo, from_west, from_east):
        self.lam, self.winds, self.inv, self.h = lam, winds, inv, h
        self.own, self.own_halo, self.from_west, self.from_east = own, own_halo, from_west, from_east

    def main(self, field, n, a):
        mid = field_ref(self.lam, self.winds, self.inv, field, n, a)[...]
        if field >= 3:
            return mid
        halo = self.h[n - 1, field, a]
        return jnp.concatenate([halo[0:8], mid, halo[8:16]], axis=0)

    def strip(self, n, which, slot):
        mid = self.own[8 * (n - 1) + 4 * which + slot]
        if which == 1:
            rows = pl.ds(pl.multiple_of(EXT * REST + ROWS * (n - 1), 8), ROWS)
            return assemble_strip(slot, self.from_west[rows, :], self.from_east[rows, :], mid)
        rows = pl.ds(pl.multiple_of(EXT * (n - 1), 8), EXT)
        halo = self.own_halo[3 * (n - 1) + slot]
        return assemble_strip(slot, self.from_west[rows, :], self.from_east[rows, :], mid, halo)


def stack(values):
    return jnp.concatenate(values, axis=0)


def unstack(value):
    return [value[EXT * k : EXT * (k + 1)] for k in range(value.shape[0] // EXT)]


def replicate(strip, a):
    lane = ext_lanes()
    out = roll_lanes(strip, -32 * a)
    base = jnp.where(lane < 32, out, 0.0)
    for g in range(1, 4):
        base = jnp.where((lane >= 32 * g) & (lane < 32 * g + 32), roll_lanes(out, 32 * g), base)
    return base


def advect(tracer, coefs, land):
    to_south, to_north, to_west = coefs
    for _ in range(3):
        a = to_west[...] * tracer
        b = (2 * DIFFUSE) * tracer - a
        east, west = roll_lanes(a, -1), roll_lanes(b, 1)
        new = (1.0 - 4 * DIFFUSE) * tracer
        new = new + roll_rows(to_south[...] * tracer, -1) + roll_rows(to_north[...] * tracer, 1)
        tracer = (new + (east + west)) * land[...]
    return tracer


def coefficients(fields, n, masks):
    merid = stack([fields.main(1, n, a) for a in range(4)] + [fields.strip(n, 0, 1)])
    zonal = stack([fields.main(2, n, a) for a in range(4)] + [fields.strip(n, 0, 2)])
    to_south = (DIFFUSE + 0.5 * merid) * masks[0]
    to_north = (DIFFUSE - 0.5 * merid) * masks[1]
    return to_south, to_north, DIFFUSE + 0.5 * zonal


def solve(inverse, strip_inverse, old):
    moved = [old[4]] + [roll_lanes(old[4], -32 * d) for d in range(1, 4)]
    new = []
    for a in range(4):
        total = inverse(a, 0) * old[0]
        for b in range(1, 4):
            total = total + inverse(a, b) * old[b]
        new.append(total)
    total = strip_inverse(0) * moved[0]
    for d in range(1, 4):
        total = total + strip_inverse(d) * moved[d]
    return new + [total]


def solve_first(fields, tracer):
    return solve(lambda a, b: fields.main(3 + b, 0, a), lambda d: fields.strip(0, 1, d), unstack(tracer))


def main_from_strip(main, strip, a, width):
    lane = lax.broadcasted_iota(jnp.int32, main.shape, 1)
    main = jnp.where(lane < width, roll_lanes(strip, -(32 * a + 8)), main)
    return jnp.where(lane >= COLS - width, roll_lanes(strip, 104 - 32 * a), main)


def merge(state):
    strip = state[4]
    lane = lax.broadcasted_iota(jnp.int32, strip.shape, 1)
    new_strip = strip
    mains = [main_from_strip(state[a], strip, a, 3) for a in range(4)]
    for a in range(4):
        west = (lane >= 32 * a + 11) & (lane < 32 * a + 16)
        east = (lane >= 32 * a + 16) & (lane < 32 * a + 21)
        new_strip = jnp.where(west, roll_lanes(state[a], 32 * a + 8), new_strip)
        new_strip = jnp.where(east, roll_lanes(state[a], 32 * a + 24), new_strip)
    return mains + [new_strip]


def load_block(fields, n):
    return [fields.main(0, n, a) for a in range(4)] + [fields.strip(n, 0, 0)]


def fluxes_out(fields, state, payload, strip_coefs):
    surface = state[0] * fields.single(3, 1)
    for f in range(4):
        payload[f] = fields.single(0, f) * surface
    wet_strip = roll_lanes(fields.single_strip(3), -32)
    payload[4] = strip_coefs * replicate(state[4] * wet_strip, 0)


def couple(fields, received, strip_coefs, strip_weights, land_strip):
    sources = [received[f] for f in range(4)] + [roll_lanes(received[4], -32 * f) for f in range(4)]
    coefs = [fields.single(0, f) for f in range(4)] + [strip_coefs[f] for f in range(4)]
    weights = [fields.single(1 + s // 4, s % 4) for s in range(9)]
    moved = {dc: [roll_lanes(source, -dc) for source in sources] for dc in (-1, 0, 1)}
    totals = []
    for table, parts in ((weights, range(4)), ([strip_weights[s] for s in range(9)], range(4, 8))):
        total = None
        for k in parts:
            part = None
            for dr in (-1, 0, 1):
                across = None
                for dc in (-1, 0, 1):
                    term = table[3 * (dr + 1) + dc + 1] * roll_rows(moved[dc][k], -dr)
                    across = term if across is None else across + term
                part = across if part is None else part + across
            total = coefs[k] * part if total is None else total + coefs[k] * part
        totals.append(total)
    return totals[0] * fields.single(3, 2), totals[1] * land_strip


INPUTS = 8


def first_kernel(*refs):
    fields = First(*refs[: INPUTS + 2])
    payload, state, land, to_south, to_north, to_west, strip_coefs, strip_weights = refs[INPUTS + 2 :]
    quads = [fields.single_strip(q) for q in range(4)]
    main_land = fields.single(3, 2)
    land[...] = stack([main_land] * 4 + [replicate(quads[3], 2)])
    coefs = (to_south, to_north, to_west)
    for ref, value in zip(coefs, coefficients(fields, 0, barrier_masks()), strict=True):
        ref[...] = value
    tracer = advect(stack(load_block(fields, 0)), coefs, land)
    merged = merge(solve_first(fields, tracer))
    for a in range(5):
        state[a] = merged[a]
    fluxes_out(fields, merged, payload, quads[0])
    for f in range(4):
        strip_coefs[f] = roll_lanes(quads[0], -32 * f)
    for k in range(9):
        strip_weights[k] = roll_lanes(quads[1 + k // 4], -32 * (k % 4))


def own_rows(tracer):
    return [value[8:40] for value in unstack(tracer)]


def rest_first_kernel(*refs):
    fields = Rest(*refs[:INPUTS])
    land, state, coefs, strip_inverse, first_out, second_out, mirror_out, edges, store, mask_c, mask_d = refs[INPUTS:]
    mask_c[...], mask_d[...] = barrier_masks()

    def block(n, carry):
        mine = tuple(coefs.at[n - 1, k] for k in range(3))
        for ref, value in zip(mine, coefficients(fields, n, (mask_c[...], mask_d[...])), strict=True):
            ref[...] = value
        tracer = advect(stack(load_block(fields, n)), mine, land)
        for d in range(4):
            strip_inverse[n - 1, d] = fields.strip(n, 1, d)
        merged = merge(
            solve(lambda a, b: fields.main(3 + b, n, a), lambda d: strip_inverse[n - 1, d], own_rows(tracer))
        )
        for a in range(5):
            state[n - 1, a] = merged[a]
            edges[0, n - 1, a] = merged[a][24:32]
            edges[1, n - 1, a] = merged[a][0:8]
            edges[2, n - 1, a] = reverse(merged[a][24:32])
        return carry

    lax.fori_loop(1, BLOCKS, block, 0)
    for n in range(REST):
        for a in range(5):
            at = 24 * a + 3 * n
            store[0, at : at + 3, :] = edges[0, n, a, 5:8, :]
            store[1, at : at + 3, :] = edges[1, n, a, 0:3, :]
            store[2, at : at + 3, :] = edges[2, n, a, 0:3, :]
    for k in range(3):
        for a in range(5):
            store[k, 24 * a + 21 : 24 * a + 24, :] = jnp.zeros((3, COLS), F32)
    hand_over(store, first_out, second_out, mirror_out)


def rest_second_kernel(*refs):
    fold, inv, strip_inverse, land, state, coefs, first_in, second_in, fold_a, fold_b, before = refs[:11]
    out, result, south, north, halo, sem = refs[11:]
    del before

    def beyond_fold():
        turn, lane = fold[0] % COLS, lanes()
        source = jnp.where(turn >= lane, turn - lane, turn - lane + COLS)
        keep = lax.broadcasted_iota(jnp.int32, (24, COLS), 1) <= turn
        group, in_group = lane // 32, lane % 32
        column = jnp.where(in_group < 16, in_group - 8, in_group + 104)
        at_a = turn - column
        at_b = at_a + COLS
        main_a, main_b = jnp.clip(at_a, 0, COLS - 1), jnp.clip(at_b, 0, COLS - 1)
        strip_a = 32 * group + jnp.clip(at_a - 104, 0, 31)
        strip_b = 32 * group + jnp.clip(at_b + 8, 0, 31)
        wide_a = stack([at_a] * 3)
        wide_b = stack([at_b] * 3)
        wide_group = stack([group] * 3)
        strip = jnp.where(wide_a >= COLS, pick(fold_a[96:120, :], strip_a), pick(fold_b[96:120, :], strip_b))
        for a in range(4):
            values_a, values_b = fold_a[24 * a : 24 * a + 24, :], fold_b[24 * a : 24 * a + 24, :]
            north[24 * a : 24 * a + 24, :] = jnp.where(keep, pick(values_a, source), pick(values_b, source))
            inside = (wide_group == a) & (wide_a < COLS) & (wide_b >= 0)
            strip = jnp.where(inside, jnp.where(wide_a >= 0, pick(values_a, main_a), pick(values_b, main_b)), strip)
        north[96:120, :] = strip

    settle_rows(first_in, second_in, south, north, beyond_fold)
    for n in range(REST):
        for a in range(5):
            at = 24 * a + 3 * n
            halo[n, a, 5:8, :] = south[at : at + 3, :]
            halo[n, a, 8:11, :] = north[at : at + 3, :]

    def block(n, carry):
        mine = tuple(coefs.at[n - 1, k] for k in range(3))
        parts = []
        for a in range(5):
            edge = halo[n - 1, a]
            parts += [edge[0:8], state[n - 1, a], edge[8:16]]
        tracer = advect(stack(parts), mine, land)
        solved = solve(lambda a, b: inv[n, a, b], lambda d: strip_inverse[n - 1, d], own_rows(tracer))
        for a in range(4):
            result[4 * (n - 1) + a] = main_from_strip(solved[a], solved[4], a, 3)
        return carry

    lax.fori_loop(1, BLOCKS, block, 0)
    copy_all([(result, out.at[pl.ds(4, 4 * REST)])], sem)


def second_kernel(*refs):
    fields = First(None, None, *refs[:INPUTS])
    land, to_south, to_north, to_west, strip_coefs, strip_weights, received, state_in = refs[INPUTS : INPUTS + 8]
    payload, state = refs[INPUTS + 8 :]
    added, added_strip = couple(fields, received, strip_coefs, strip_weights, land[4 * EXT :])
    lane = ext_lanes()
    strip = state_in[4] + jnp.where(lane < 32, added_strip, 0.0)
    top = main_from_strip(state_in[0] + added, strip, 0, 1)
    tracer = stack([top] + [state_in[a] for a in range(1, 4)] + [strip])
    solved = solve_first(fields, advect(tracer, (to_south, to_north, to_west), land))
    merged = [main_from_strip(solved[a], solved[4], a, 3) for a in range(4)] + [solved[4]]
    for a in range(5):
        state[a] = merged[a]
    fluxes_out(fields, merged, payload, fields.single_strip(0))


def last_kernel(x_in, hx, land, strip_coefs, strip_weights, received, state, out, result, sem):
    fields = First(*[None] * 8, x_in, hx)
    added, added_strip = couple(fields, received, strip_coefs, strip_weights, land[4 * EXT :])
    strip = state[4] + added_strip
    result[0] = main_from_strip(state[0] + added, strip, 0, 1)[8:40]
    for a in range(1, 4):
        result[a] = state[a][8:40]
    copy_all([(result, out.at[pl.ds(0, 4)])], sem)


MICROSECONDS = {
    "start_rows_kernel": 3.2,
    "own_first_kernel": 2.0,
    "own_rest_kernel": 2.5,
    "halo_first_kernel": 1.7,
    "halo_rest_kernel": 1.3,
    "first_kernel": 1.0,
    "rest_first_kernel": 4.3,
    "second_kernel": 1.0,
    "last_kernel": 0.5,
    "rest_second_kernel": 4.6,
}


def call(kernel, outs, args, specs, scratch=(), params=PARAMS, **more):
    cost = int(MICROSECONDS[kernel.__name__] * 3.5e6)
    return pl.pallas_call(
        kernel,
        out_shape=[jax.ShapeDtypeStruct(s, jnp.int32 if spec is SMEM else F32) for s, spec in outs],
        in_specs=specs,
        out_specs=[spec for _, spec in outs],
        scratch_shapes=list(scratch),
        compiler_params=params,
        cost_estimate=pl.CostEstimate(flops=0, bytes_accessed=cost, transcendentals=0),
        **more,
    )(*args)


def index(c, a, o):
    return (c * LAT + a) * LON + o % LON


def lon_pairs(do):
    return [(index(c, a, o), index(c, a, o + do)) for c in range(2) for a in range(LAT) for o in range(LON)]


def swap_pairs(start):
    pairs = []
    for c in range(2):
        for a in range(start, LAT - 1, 2):
            for o in range(LON):
                pairs += [(index(c, a, o), index(c, a + 1, o)), (index(c, a + 1, o), index(c, a, o))]
    return pairs


def fold_pairs(total, comps):
    return [(index(c, LAT - 1, o), index(c, LAT - 1, total - o)) for c in comps for o in range(LON)]


def body(
    adjoint_state,
    winds,
    block_inverse,
    flux_coef,
    sea_mask,
    intersection_cell,
    intersection_weight,
    fold_map,
):
    lam = adjoint_state[0]
    wind = winds[:, 0]
    inv = block_inverse[0]
    rows = (ROW_BUFFER, COLS)
    x, first, second, mirror, turn = call(
        start_rows_kernel,
        [((4, 4, ROWS, COLS), VMEM)] + [(rows, VMEM)] * 3 + [((1,), SMEM)],
        (fold_map, lam, wind, inv, flux_coef[0], sea_mask, intersection_cell, intersection_weight),
        [SMEM] + [HBM] * 7,
        [
            pltpu.VMEM((3, *rows), F32),
            pltpu.VMEM((32, 16, COLS), F32),
            pltpu.VMEM((2, 32, 16, COLS), F32),
            pltpu.VMEM((1, 4, 4, 16, COLS), F32),
            pltpu.VMEM((4, ROWS, COLS), F32),
            pltpu.VMEM((ROWS, COLS), jnp.int32),
            pltpu.VMEM((2, 4, ROWS, COLS), jnp.int32),
            pltpu.VMEM((4, ROWS, COLS), F32),
            pltpu.SemaphoreType.DMA((10,)),
        ],
        FULL,
    )
    def swap(first, second):
        return lax.ppermute(first, AXES, swap_pairs(0)), lax.ppermute(second, AXES, swap_pairs(1))

    def around(to_west, to_east):
        return lax.ppermute(to_east, AXES, lon_pairs(1)), lax.ppermute(to_west, AXES, lon_pairs(-1))

    def across(value):
        return lax.ppermute(value, AXES, [(i, (i + LAT * LON) % (2 * LAT * LON)) for i in range(2 * LAT * LON)])

    def vmem(*shape):
        return ((*shape, COLS), VMEM)

    state_in = (lam, wind, inv)
    swapped = swap(first, second)

    def across_fold(total, mirror, lam, wind, inv, x):
        folded = [lax.ppermute(mirror, AXES, fold_pairs(total - k, (0, 1))) for k in range(2)]
        own = call(
            own_first_kernel,
            [vmem(12, ROWS), vmem(3, ROWS), vmem(3, ROWS)],
            (lam, wind, inv, x),
            [HBM] * 4,
            [
                pltpu.VMEM((4, ROWS, COLS), F32),
                pltpu.VMEM((2, 4, ROWS, COLS), F32),
                pltpu.VMEM((1, 4, 4, ROWS, COLS), F32),
                pltpu.VMEM((4, 4, ROWS, COLS), F32),
                pltpu.SemaphoreType.DMA((4,)),
            ],
        )
        rest_own = call(
            own_rest_kernel,
            [vmem(8 * REST, ROWS), vmem(2 * REST, ROWS), vmem(2 * REST, ROWS)],
            (lam, wind, inv),
            [VMEM] * 3,
        )
        return *folded, *own, *rest_own

    *folded, own, mid_west, mid_east, rest_own, rest_mid_west, rest_mid_east = lax.switch(
        turn[0], [functools.partial(across_fold, total) for total in range(LON)], mirror, lam, wind, inv, x
    )
    moved = (*swapped, *folded)
    south, north, h, hx, own_halo, to_west, to_east = call(
        halo_first_kernel,
        [vmem(ROW_BUFFER)] * 2 + [vmem(7, 4, 16), vmem(4, 4, 16), vmem(12, 16), vmem(3, EXT), vmem(3, EXT)],
        (fold_map, *moved, mid_west, mid_east),
        [SMEM] + [VMEM] * 6,
    )
    rest_h, rest_own_halo, rest_to_west, rest_to_east = call(
        halo_rest_kernel,
        [vmem(REST, 3, 4, 16), vmem(3 * REST, 16), vmem(COL_BUFFER), vmem(COL_BUFFER)],
        (south, north, rest_mid_west, rest_mid_east),
        [VMEM] * 4,
        [pltpu.VMEM((REST, 16, COLS), F32)] * 2,
    )
    h, rest_to_west, rest_to_east = lax.optimization_barrier((h, rest_to_west, rest_to_east))
    args = (inv, h, own, own_halo, *around(to_west, to_east), x, hx)
    five = vmem(5, EXT)
    tall = vmem(5 * EXT)
    payload, state, land, *tables = call(
        first_kernel,
        [five, five] + [tall] * 4 + [vmem(4, EXT), vmem(9, EXT)],
        (lam, wind, *args),
        [VMEM] * (INPUTS + 2),
    )
    received = across(payload)
    rest_args = (*state_in, rest_h, rest_own, rest_own_halo, *around(rest_to_west, rest_to_east))
    whole = ((32, ROWS, COLS), HBM)
    done = pltpu.SemaphoreType.DMA((1,))
    rest_state, rest_coefs, strip_inverse, *rest_rows = call(
        rest_first_kernel,
        [vmem(REST, 5, ROWS), vmem(REST, 3, 5 * EXT), vmem(REST, 4, ROWS)] + [vmem(120)] * 3,
        (*rest_args, land),
        [VMEM] * (INPUTS + 1),
        [pltpu.VMEM((3, REST, 5, 8, COLS), F32), pltpu.VMEM((3, 120, COLS), F32)]
        + [pltpu.VMEM((5 * EXT, COLS), F32)] * 2,
    )
    rest_swapped = swap(*rest_rows[:2])
    received, rest_mirror = lax.optimization_barrier((received, rest_rows[2]))
    payload, state = call(
        second_kernel, [five, five], (*args, land, *tables, received, state), [VMEM] * (INPUTS + 8)
    )

    def finish(total, mirror, payload, last_args, rest_args, swapped):
        folded = [lax.ppermute(mirror, AXES, fold_pairs(total - k, (1,))) for k in range(2)]
        x, hx, land, strip_coefs, strip_weights, state = last_args
        (out,) = call(
            last_kernel,
            [whole],
            (x, hx, land, strip_coefs, strip_weights, across(payload), state),
            [VMEM] * 7,
            [pltpu.VMEM((4, ROWS, COLS), F32), done],
        )
        return call(
            rest_second_kernel,
            [whole],
            (*rest_args, *swapped, *folded, out),
            [SMEM] + [VMEM] * 9 + [HBM],
            [
                pltpu.VMEM((4 * REST, ROWS, COLS), F32),
                pltpu.VMEM((120, COLS), F32),
                pltpu.VMEM((120, COLS), F32),
                pltpu.VMEM((REST, 5, 16, COLS), F32),
                done,
            ],
            input_output_aliases={10: 0},
        )[0]

    out = lax.switch(
        turn[0],
        [functools.partial(finish, total) for total in range(LON)],
        rest_mirror,
        payload,
        (x, hx, land, *tables[3:], state),
        (fold_map, inv, strip_inverse, land, rest_state, rest_coefs),
        rest_swapped,
    )
    return out[None]


def solution(mesh):
    return jax.shard_map(
        body,
        mesh=mesh,
        in_specs=(
            P("comp", None, "lat", "lon"),
            P(None, "comp", None, "lat", "lon"),
            P("comp", None, None, None, "lat", "lon"),
            P("comp", None, "lat", "lon"),
            P("lat", "lon"),
            P(None, None, "lat", "lon"),
            P(None, "lat", "lon"),
            P(),
        ),
        out_specs=P("comp", None, "lat", "lon"),
        check_vma=False,
    )
```

```python
import functools

import jax
import jax.numpy as jnp
from jax import lax
from jax.experimental import pallas as pl
from jax.experimental.pallas import tpu as pltpu
from jax.sharding import PartitionSpec as P

DIFFUSE = 0.15
ROWS = 32
EXT = 48
COLS = 128
HALF = COLS // 2
BLOCKS = 8
F32 = jnp.float32
AXES = ("comp", "lat", "lon")
LAT, LON = 8, 8
VMEM = pl.BlockSpec(memory_space=pltpu.VMEM)
ANY = pl.BlockSpec(memory_space=pl.ANY)
HBM = pl.BlockSpec(memory_space=pltpu.HBM)
SMEM = pl.BlockSpec(memory_space=pltpu.SMEM)
PARAMS = pltpu.CompilerParams(vmem_limit_bytes=16 * 1024 * 1024)
FULL = pltpu.CompilerParams(vmem_limit_bytes=63 * 1024 * 1024)


def places():
    comp, lat, lon = (lax.axis_index(name) for name in AXES)
    return comp, lat, lon, lat == LAT - 1


def first_pieces():
    pieces = []
    for a in range(4):
        pieces.append((0, 0, a, 8 * a, 8))
        pieces.append((1, 0, a, 32 + 8 * a, 8))
        pieces.append((2, 0, a, 64 + 7 * a, 7))
    for b in range(4):
        pieces.append((3 + b, 0, 0, 92 + 5 * b, 5))
        for a in range(1, 4):
            pieces.append((3 + b, 0, a, 120 + 4 * (4 * (a - 1) + b), 4))
    return pieces


def rest_pieces():
    pieces = []
    for n in range(1, BLOCKS):
        at = 240 + 32 * (n - 1)
        for a in range(4):
            pieces.append((0, n, a, at + 3 * a, 3))
            pieces.append((1, n, a, at + 12 + 3 * a, 3))
            pieces.append((2, n, a, at + 24 + 2 * a, 2))
    return pieces


ROW_BUFFER = 240 + 32 * (BLOCKS - 1)
SINGLES = (
    [(0, f, 168 + 5 * f, 5) for f in range(4)]
    + [(1 + s // 4, s % 4, 188 + 4 * s, 4) for s in range(9)]
    + [(3, 1, 112, 8), (3, 2, 224, 8)]
)


def mirrored_single(quad, member):
    if quad in (1, 2) or (quad == 3 and member == 0):
        s = 8 - (4 * (quad - 1) + member)
        return 1 + s // 4, s % 4
    return quad, member


def copy_all(pairs, sem):
    copies = [pltpu.make_async_copy(a, b, sem.at[k]) for k, (a, b) in enumerate(pairs)]
    for copy in copies:
        copy.start()
    for copy in copies:
        copy.wait()


def reverse(tile):
    flip = 7 - lax.broadcasted_iota(jnp.int32, (8, COLS), 0)
    return jnp.take_along_axis(tile, flip, axis=0, mode="promise_in_bounds")


def put_piece(store, ref, at, count):
    end = ref.shape[0]
    store[0, at : at + count, :] = ref[end - count : end, :]
    store[1, at : at + count, :] = ref[0:count, :]


def put_mirrored(store, ref, at, count, sign):
    end = ref.shape[0]
    turned = reverse(ref[end - 8 : end, :])
    if sign < 0:
        turned = -turned
    store[2, at : at + count, :] = turned[0:count, :]


def field_ref(lam, winds, inv, field, n, a):
    if field == 0:
        return lam.at[4 * n + a]
    if field <= 2:
        return winds.at[2 - field, 4 * n + a]
    return inv.at[n, a, field - 3]


def sign_of(field):
    return -1 if field in (1, 2) else 1


def hand_over(store, first_out, second_out, mirror_out):
    _, lat, _, _ = places()
    odd = lat % 2
    first_out[...] = store[odd]
    second_out[...] = store[1 - odd]
    mirror_out[...] = store[2]


def start_rows_kernel(
    fold, lam_in, winds_in, inv_in, fc_in, mask_in, cell_in, weight_in,
    x_out, first_out, second_out, mirror_out, low_out, high_out, turn_out, half_turn_out,
    store, lam, winds, inv, fc, mask, cell, weight, sem,
):
    comp, lat_pos, lon_pos, _ = places()
    turn_out[0] = fold[0] // COLS
    half_turn_out[0] = fold[0] // HALF
    pairs = [(fc_in, fc), (mask_in, mask), (cell_in, cell), (weight_in, weight)]
    for half, rows in enumerate((pl.ds(0, 8), pl.ds(ROWS - 8, 8))):
        at = pl.ds(8 * half, 8)
        pairs.append((lam_in.at[:, rows], lam.at[:, at]))
        pairs.append((winds_in.at[:, :, rows], winds.at[:, :, at]))
        pairs.append((inv_in.at[pl.ds(0, 1), :, :, rows], inv.at[:, :, :, at]))
    copy_all(pairs, sem)
    wet = mask[...].astype(F32)
    x_out[3, 1] = wet
    x_out[3, 2] = jnp.where(comp == 1, wet, jnp.ones_like(wet))
    x_out[3, 3] = jnp.zeros_like(wet)
    for f in range(4):
        x_out[0, f] = fc[f]
    rows = lat_pos * ROWS + lax.broadcasted_iota(jnp.int32, (ROWS, COLS), 0)
    cols = lon_pos * COLS + lax.broadcasted_iota(jnp.int32, (ROWS, COLS), 1)
    row_shift = [cell[0, k] - rows for k in range(4)]
    col_shift = []
    for k in range(4):
        d = cell[1, k] - cols
        d = jnp.where(d > 1, d - LON * COLS, d)
        col_shift.append(jnp.where(d < -1, d + LON * COLS, d))
    code = [3 * row_shift[k] + col_shift[k] + 4 for k in range(4)]
    weights = [weight[k] for k in range(4)]
    for s in range(9):
        total = jnp.where(code[0] == s, weights[0], 0.0)
        for k in range(1, 4):
            total = total + jnp.where(code[k] == s, weights[k], 0.0)
        x_out[1 + s // 4, s % 4] = total
    pieces = [(field_ref(lam, winds, inv, f, n, a), at, count, sign_of(f)) for f, n, a, at, count in first_pieces()]
    pieces += [(field_ref(lam, winds, inv, f, n, a), at, count, sign_of(f)) for f, n, a, at, count in rest_pieces()]
    for ref, at, count, _ in pieces:
        put_piece(store, ref, at, count)
    for quad, member, at, count in SINGLES:
        put_piece(store, x_out.at[quad, member], at, count)

    @pl.when(places()[3])
    def _():
        for ref, at, count, sign in pieces:
            put_mirrored(store, ref, at, count, sign)
        for quad, member, at, count in SINGLES:
            put_mirrored(store, x_out.at[mirrored_single(quad, member)], at, count, 1)
        a, b = store[2, 0 : ROW_BUFFER // 2, :], store[2, ROW_BUFFER // 2 : ROW_BUFFER, :]
        low = lax.broadcasted_iota(jnp.int32, a.shape, 1) < HALF
        low_out[...] = jnp.where(low, a, roll_lanes(b, HALF))
        high_out[...] = jnp.where(low, roll_lanes(a, HALF), b)

    hand_over(store, first_out, second_out, mirror_out)


def lanes():
    return lax.broadcasted_iota(jnp.int32, (8, COLS), 1)


def roll_lanes(x, by):
    by = by % COLS
    return x if by == 0 else pltpu.roll(x, by, axis=1)


def roll_rows(x, by):
    by = by % x.shape[0]
    return x if by == 0 else pltpu.roll(x, by, axis=0)


def pack_columns(slots, strip_at, to_west, to_east, buffer_at, row_count):
    rows = row_count
    used = [k for k, members in enumerate(slots) if members is not None]
    zero = jnp.zeros((rows, COLS), F32)
    lane = lax.broadcasted_iota(jnp.int32, (len(used) * rows, COLS), 1)
    pair = jnp.zeros((len(used) * rows, COLS), F32)
    for a in range(4):
        values = [zero if slots[k][a] is None else slots[k][a] for k in used]
        moved = roll_lanes(jnp.concatenate(values, axis=0), 32 * a + 8)
        pair = jnp.where((lane >= 32 * a) & (lane < 32 * a + 16), moved, pair)
    strips = jnp.where(lane % 32 < 16, pair, roll_lanes(pair, 16))
    group = lax.broadcasted_iota(jnp.int32, (rows, COLS), 1) % 32
    buffers = -(-len(slots) // 4)
    west, east = [zero] * buffers, [zero] * buffers
    for i, k in enumerate(used):
        ref, at = strip_at[k]
        ref[at] = strips[i * rows : (i + 1) * rows]
        mine = pair[i * rows : (i + 1) * rows]
        buffer, slot = k // 4, k % 4
        here = (group >= 8 * slot) & (group < 8 * slot + 8)
        west[buffer] = jnp.where(here, roll_lanes(mine, 8 * slot - 8), west[buffer])
        east[buffer] = jnp.where(here, roll_lanes(mine, 8 * slot), east[buffer])
    for buffer in range(buffers):
        at = pl.ds(pl.multiple_of(rows * (buffer_at + buffer), 8), rows)
        to_west[at, :] = west[buffer]
        to_east[at, :] = east[buffer]


def block_slots(read, extra):
    slots = [[read(field, a) for a in range(4)] for field in range(3)] + [extra]
    return slots + [[read(3 + (a + d) % 4, a) for a in range(4)] for d in range(4)]


def single_slots(read):
    return [[None if q == 3 and a == 3 else read(q, a) for a in range(4)] for q in range(1, 4)]


def own_first_kernel(lam_in, winds_in, inv_in, x_in, own, to_west, to_east, lam, winds, inv, x, sem):
    four = pl.ds(0, 4)
    copy_all(
        [
            (inv_in.at[pl.ds(0, 1)], inv),
            (winds_in.at[:, four], winds),
            (lam_in.at[four], lam),
            (x_in, x),
        ],
        sem,
    )

    def read(field, a):
        return field_ref(lam, winds, inv, field, 0, a)[...]

    slots = block_slots(read, [x[0, f] for f in range(4)])
    slots += single_slots(lambda q, a: x[q, a])
    pack_columns(slots, [(own, k) for k in range(12)], to_west, to_east, 0, ROWS)


def own_rest_kernel(lam_in, winds_in, inv_in, own, to_west, to_east, lam, winds, inv, sem):
    def fetch(n):
        levels = pl.ds(4 * n, 4)
        pairs = ((winds_in.at[:, levels], winds.at[:, levels]), (lam_in.at[levels], lam.at[levels]), (inv_in.at[n], inv.at[n]))
        return [pltpu.make_async_copy(a, b, sem.at[n - 1, k]) for k, (a, b) in enumerate(pairs)]

    for n in range(1, BLOCKS):
        for copy in fetch(n):
            copy.start()

    def step(n, carry):
        for copy in fetch(n):
            copy.wait()

        def read(field, a):
            return field_ref(lam, winds, inv, field, n, a)[...]

        strip_at = [(own, 8 * (n - 1) + k) for k in range(8)]
        pack_columns(block_slots(read, None), strip_at, to_west, to_east, 2 * (n - 1), ROWS)
        return carry

    lax.fori_loop(1, BLOCKS, step, 0)


def settle_rows(first_in, second_in, south, north, beyond_fold):
    _, lat, _, is_top = places()
    even = lat % 2 == 0

    @pl.when(even)
    def _():
        south[...] = second_in[...]
        north[...] = first_in[...]

    @pl.when(jnp.logical_not(even))
    def _():
        south[...] = first_in[...]

    @pl.when(jnp.logical_not(even) & jnp.logical_not(is_top))
    def _():
        north[...] = second_in[...]

    pl.when(is_top)(beyond_fold)


def pick(values, at):
    tiles = [
        jnp.take_along_axis(values[8 * t : 8 * t + 8], at, axis=1, mode="promise_in_bounds")
        for t in range(values.shape[0] // 8)
    ]
    return jnp.concatenate(tiles, axis=0)


REST = BLOCKS - 1
COL_OWN = 16 * (3 + REST)
COL_BUFFER = COL_OWN + ROWS * (3 + 2 * REST)


def halo_kernel(
    fold, first_in, second_in, fold_whole, fold_half, mid_west, mid_east, rest_west, rest_east, *refs,
):
    brought_in, (h, hx, own, rest_h, rest_own, to_west, to_east), refs = refs[:BROUGHT], refs[BROUGHT : BROUGHT + 7], refs[BROUGHT + 7 :]
    brought, (south, north, sem) = refs[:BROUGHT], refs[BROUGHT:]
    mids = (ROWS * 3, ROWS * 2 * REST)
    pairs = [(rest_west, to_west.at[pl.ds(COL_OWN + mids[0], mids[1])])]
    pairs += [(rest_east, to_east.at[pl.ds(COL_OWN + mids[0], mids[1])])]
    pairs += [(mid_west, to_west.at[pl.ds(COL_OWN, mids[0])]), (mid_east, to_east.at[pl.ds(COL_OWN, mids[0])])]
    pairs += list(zip(brought_in, brought, strict=True))
    copies = [pltpu.make_async_copy(a, b, sem.at[k]) for k, (a, b) in enumerate(pairs)]
    for copy in copies:
        copy.start()

    def beyond_fold():
        turn, lane = fold[0] % COLS, lanes()
        source = jnp.where(turn >= lane, turn - lane, turn - lane + COLS)
        in_half = source % HALF
        few = jnp.concatenate([pick(fold_half[...], in_half), pick(fold_half[...], in_half + HALF)], axis=0)
        many = pick(fold_whole[...], source)
        column = lax.broadcasted_iota(jnp.int32, (ROW_BUFFER, COLS), 1)
        whole_is_first = turn >= HALF
        first = (column <= turn).astype(jnp.int32)
        north[...] = jnp.where(first == whole_is_first.astype(jnp.int32), many, few)

    settle_rows(first_in, second_in, south, north, beyond_fold)
    for field, _, a, at, count in first_pieces():
        h[field, a, 8 - count : 8, :] = south[at : at + count, :]
        h[field, a, 8 : 8 + count, :] = north[at : at + count, :]
    for quad, member, at, count in SINGLES:
        hx[quad, member, 8 - count : 8, :] = south[at : at + count, :]
        hx[quad, member, 8 : 8 + count, :] = north[at : at + count, :]
    for field, n, a, at, count in rest_pieces():
        rest_h[n - 1, field, a, 8 - count : 8, :] = south[at : at + count, :]
        rest_h[n - 1, field, a, 8 : 8 + count, :] = north[at : at + count, :]
    slots = block_slots(lambda field, a: h[field, a], [hx[0, f] for f in range(4)])
    slots += single_slots(lambda q, a: hx[q, a]) + [None]
    strip_at = [(own, k) for k in range(11)] + [None]
    for n in range(REST):
        slots += [[rest_h[n, field, a] for a in range(4)] for field in range(3)] + [None]
        strip_at += [(rest_own, 3 * n + k) for k in range(3)] + [None]
    pack_columns(slots, strip_at, to_west, to_east, 0, 16)
    for copy in copies:
        copy.wait()


BROUGHT = 5


def ext_lanes():
    return lax.broadcasted_iota(jnp.int32, (EXT, COLS), 1)


def barrier_masks():
    comp, _, _, is_top = places()
    row = lax.broadcasted_iota(jnp.int32, (EXT, COLS), 0)
    apart = is_top & (comp == 0)
    keep_c = jnp.where(apart & (row == 40), 0.0, 1.0).astype(F32)
    keep_d = jnp.where(apart & (row == 39), 0.0, 1.0).astype(F32)
    return stack([keep_c] * 5), stack([keep_d] * 5)


def edges_of(slot, west, east):
    group = lax.broadcasted_iota(jnp.int32, west.shape, 1) % 32
    edge = jnp.where(group < 8, roll_lanes(west, -8 * slot), roll_lanes(east, 24 - 8 * slot))
    return edge, (group >= 8) & (group < 24)


def assemble_strip(slot, sides, buffer, mid, halo_buffer=None, halo=None):
    rows = pl.ds(pl.multiple_of(COL_OWN + ROWS * buffer, 8), ROWS)
    edge, inner = edges_of(slot, sides[0][rows, :], sides[1][rows, :])
    middle = jnp.where(inner, mid, edge)
    if halo is None:
        return middle
    rows = pl.ds(pl.multiple_of(16 * halo_buffer, 8), 16)
    edge, inner = edges_of(slot, sides[0][rows, :], sides[1][rows, :])
    outer = jnp.where(inner, halo, edge)
    return jnp.concatenate([outer[0:8], middle, outer[8:16]], axis=0)


class First:
    def __init__(self, lam, winds, inv, h, own, own_halo, from_west, from_east, x_in, hx):
        self.lam, self.winds, self.inv, self.h = lam, winds, inv, h
        self.own, self.own_halo, self.sides = own, own_halo, (from_west, from_east)
        self.x_in, self.hx = x_in, hx

    def main(self, field, n, a):
        halo = self.h[field, a]
        mid = field_ref(self.lam, self.winds, self.inv, field, 0, a)[...]
        return jnp.concatenate([halo[0:8], mid, halo[8:16]], axis=0)

    def single(self, quad, a):
        halo = self.hx[quad, a]
        return jnp.concatenate([halo[0:8], self.x_in[quad, a], halo[8:16]], axis=0)

    def strip(self, n, which, slot):
        at = 4 * which + slot
        return assemble_strip(slot, self.sides, which, self.own[at], which, self.own_halo[at])

    def single_strip(self, quad):
        return self.strip(0, 0, 3) if quad == 0 else self.strip(0, 2, quad - 1)


class Rest:
    def __init__(self, lam, winds, inv, h, own, own_halo, from_west, from_east):
        self.lam, self.winds, self.inv, self.h = lam, winds, inv, h
        self.own, self.own_halo, self.sides = own, own_halo, (from_west, from_east)

    def main(self, field, n, a):
        mid = field_ref(self.lam, self.winds, self.inv, field, n, a)[...]
        if field >= 3:
            return mid
        halo = self.h[n - 1, field, a]
        return jnp.concatenate([halo[0:8], mid, halo[8:16]], axis=0)

    def strip(self, n, which, slot):
        mid = self.own[8 * (n - 1) + 4 * which + slot]
        buffer = 3 + 2 * (n - 1) + which
        if which == 1:
            return assemble_strip(slot, self.sides, buffer, mid)
        return assemble_strip(slot, self.sides, buffer, mid, 2 + n, self.own_halo[3 * (n - 1) + slot])


def stack(values):
    return jnp.concatenate(values, axis=0)


def unstack(value):
    return [value[EXT * k : EXT * (k + 1)] for k in range(value.shape[0] // EXT)]


def replicate(strip, a):
    lane = ext_lanes()
    out = roll_lanes(strip, -32 * a)
    base = jnp.where(lane < 32, out, 0.0)
    for g in range(1, 4):
        base = jnp.where((lane >= 32 * g) & (lane < 32 * g + 32), roll_lanes(out, 32 * g), base)
    return base


def advect(tracer, coefs, land):
    to_south, to_north, to_west = coefs
    for _ in range(3):
        a = to_west[...] * tracer
        b = (2 * DIFFUSE) * tracer - a
        east, west = roll_lanes(a, -1), roll_lanes(b, 1)
        new = (1.0 - 4 * DIFFUSE) * tracer
        new = new + roll_rows(to_south[...] * tracer, -1) + roll_rows(to_north[...] * tracer, 1)
        tracer = (new + (east + west)) * land[...]
    return tracer


def coefficients(fields, n, masks):
    merid = stack([fields.main(1, n, a) for a in range(4)] + [fields.strip(n, 0, 1)])
    zonal = stack([fields.main(2, n, a) for a in range(4)] + [fields.strip(n, 0, 2)])
    to_south = (DIFFUSE + 0.5 * merid) * masks[0]
    to_north = (DIFFUSE - 0.5 * merid) * masks[1]
    return to_south, to_north, DIFFUSE + 0.5 * zonal


def solve(inverse, strip_inverse, old):
    moved = [old[4]] + [roll_lanes(old[4], -32 * d) for d in range(1, 4)]
    new = []
    for a in range(4):
        total = inverse(a, 0) * old[0]
        for b in range(1, 4):
            total = total + inverse(a, b) * old[b]
        new.append(total)
    total = strip_inverse(0) * moved[0]
    for d in range(1, 4):
        total = total + strip_inverse(d) * moved[d]
    return new + [total]


def solve_first(inverse, strip_inverse, tracer):
    return solve(lambda a, b: inverse[4 * a + b], lambda d: strip_inverse[d], unstack(tracer))


def main_from_strip(main, strip, a, width):
    lane = lax.broadcasted_iota(jnp.int32, main.shape, 1)
    main = jnp.where(lane < width, roll_lanes(strip, -(32 * a + 8)), main)
    return jnp.where(lane >= COLS - width, roll_lanes(strip, 104 - 32 * a), main)


def merge(state):
    strip = state[4]
    lane = lax.broadcasted_iota(jnp.int32, strip.shape, 1)
    new_strip = strip
    mains = [main_from_strip(state[a], strip, a, 3) for a in range(4)]
    for a in range(4):
        west = (lane >= 32 * a + 11) & (lane < 32 * a + 16)
        east = (lane >= 32 * a + 16) & (lane < 32 * a + 21)
        new_strip = jnp.where(west, roll_lanes(state[a], 32 * a + 8), new_strip)
        new_strip = jnp.where(east, roll_lanes(state[a], 32 * a + 24), new_strip)
    return mains + [new_strip]


def load_block(fields, n):
    return [fields.main(0, n, a) for a in range(4)] + [fields.strip(n, 0, 0)]


def fluxes_out(fields, state, payload, strips):
    surface = state[0] * fields.single(3, 1)
    for f in range(4):
        payload[f] = fields.single(0, f) * surface
    payload[4] = strips[0] * replicate(state[4] * strips[1], 0)


def couple(fields, received, strip_coefs, strip_weights, land_strip):
    sources = [received[f] for f in range(4)] + [roll_lanes(received[4], -32 * f) for f in range(4)]
    coefs = [fields.single(0, f) for f in range(4)] + [strip_coefs[f] for f in range(4)]
    weights = [fields.single(1 + s // 4, s % 4) for s in range(9)]
    moved = {dc: [roll_lanes(source, -dc) for source in sources] for dc in (-1, 0, 1)}
    totals = []
    for table, parts in ((weights, range(4)), ([strip_weights[s] for s in range(9)], range(4, 8))):
        total = None
        for k in parts:
            part = None
            for dr in (-1, 0, 1):
                across = None
                for dc in (-1, 0, 1):
                    term = table[3 * (dr + 1) + dc + 1] * roll_rows(moved[dc][k], -dr)
                    across = term if across is None else across + term
                part = across if part is None else part + across
            total = coefs[k] * part if total is None else total + coefs[k] * part
        totals.append(total)
    return totals[0] * fields.single(3, 2), totals[1] * land_strip


INPUTS = 8


def first_kernel(*refs):
    fields = First(*refs[: INPUTS + 2])
    payload, state, land, to_south, to_north, to_west, strip_coefs, strip_weights = refs[INPUTS + 2 : INPUTS + 10]
    inverse, strip_inverse, flux_strips = refs[INPUTS + 10 :]
    quads = [fields.single_strip(q) for q in range(4)]
    main_land = fields.single(3, 2)
    land[...] = stack([main_land] * 4 + [replicate(quads[3], 2)])
    coefs = (to_south, to_north, to_west)
    for ref, value in zip(coefs, coefficients(fields, 0, barrier_masks()), strict=True):
        ref[...] = value
    tracer = advect(stack(load_block(fields, 0)), coefs, land)
    for a in range(4):
        for b in range(4):
            inverse[4 * a + b] = fields.main(3 + b, 0, a)
        strip_inverse[a] = fields.strip(0, 1, a)
    flux_strips[0] = quads[0]
    flux_strips[1] = roll_lanes(quads[3], -32)
    merged = merge(solve_first(inverse, strip_inverse, tracer))
    for a in range(5):
        state[a] = merged[a]
    fluxes_out(fields, merged, payload, flux_strips)
    for f in range(4):
        strip_coefs[f] = roll_lanes(quads[0], -32 * f)
    for k in range(9):
        strip_weights[k] = roll_lanes(quads[1 + k // 4], -32 * (k % 4))


def own_rows(tracer):
    return [value[8:40] for value in unstack(tracer)]


def rest_first_kernel(*refs):
    fields = Rest(*refs[:INPUTS])
    land, state, coefs, strip_inverse, first_out, second_out, mirror_out, edges, store, mask_c, mask_d = refs[INPUTS:]
    mask_c[...], mask_d[...] = barrier_masks()

    def block(n, carry):
        mine = tuple(coefs.at[n - 1, k] for k in range(3))
        for ref, value in zip(mine, coefficients(fields, n, (mask_c[...], mask_d[...])), strict=True):
            ref[...] = value
        tracer = advect(stack(load_block(fields, n)), mine, land)
        for d in range(4):
            strip_inverse[n - 1, d] = fields.strip(n, 1, d)
        merged = merge(
            solve(lambda a, b: fields.main(3 + b, n, a), lambda d: strip_inverse[n - 1, d], own_rows(tracer))
        )
        for a in range(5):
            state[n - 1, a] = merged[a]
            edges[0, n - 1, a] = merged[a][24:32]
            edges[1, n - 1, a] = merged[a][0:8]
            edges[2, n - 1, a] = reverse(merged[a][24:32])
        return carry

    lax.fori_loop(1, BLOCKS, block, 0)
    for n in range(REST):
        for a in range(5):
            at = 24 * a + 3 * n
            store[0, at : at + 3, :] = edges[0, n, a, 5:8, :]
            store[1, at : at + 3, :] = edges[1, n, a, 0:3, :]
            store[2, at : at + 3, :] = edges[2, n, a, 0:3, :]
    for k in range(3):
        for a in range(5):
            store[k, 24 * a + 21 : 24 * a + 24, :] = jnp.zeros((3, COLS), F32)
    hand_over(store, first_out, second_out, mirror_out)


def rest_second_kernel(*refs):
    fold, inv, strip_inverse, land, state, coefs, first_in, second_in, fold_a, fold_b = refs[:10]
    out, result, south, north, halo, sem = refs[10:]

    def beyond_fold():
        turn, lane = fold[0] % COLS, lanes()
        source = jnp.where(turn >= lane, turn - lane, turn - lane + COLS)
        keep = lax.broadcasted_iota(jnp.int32, (24, COLS), 1) <= turn
        group, in_group = lane // 32, lane % 32
        column = jnp.where(in_group < 16, in_group - 8, in_group + 104)
        at_a = turn - column
        at_b = at_a + COLS
        main_a, main_b = jnp.clip(at_a, 0, COLS - 1), jnp.clip(at_b, 0, COLS - 1)
        strip_a = 32 * group + jnp.clip(at_a - 104, 0, 31)
        strip_b = 32 * group + jnp.clip(at_b + 8, 0, 31)
        wide_a = stack([at_a] * 3)
        wide_b = stack([at_b] * 3)
        wide_group = stack([group] * 3)
        strip = jnp.where(wide_a >= COLS, pick(fold_a[96:120, :], strip_a), pick(fold_b[96:120, :], strip_b))
        for a in range(4):
            values_a, values_b = fold_a[24 * a : 24 * a + 24, :], fold_b[24 * a : 24 * a + 24, :]
            north[24 * a : 24 * a + 24, :] = jnp.where(keep, pick(values_a, source), pick(values_b, source))
            inside = (wide_group == a) & (wide_a < COLS) & (wide_b >= 0)
            strip = jnp.where(inside, jnp.where(wide_a >= 0, pick(values_a, main_a), pick(values_b, main_b)), strip)
        north[96:120, :] = strip

    settle_rows(first_in, second_in, south, north, beyond_fold)
    for n in range(REST):
        for a in range(5):
            at = 24 * a + 3 * n
            halo[n, a, 5:8, :] = south[at : at + 3, :]
            halo[n, a, 8:11, :] = north[at : at + 3, :]

    def block(n, carry):
        mine = tuple(coefs.at[n - 1, k] for k in range(3))
        parts = []
        for a in range(5):
            edge = halo[n - 1, a]
            parts += [edge[0:8], state[n - 1, a], edge[8:16]]
        tracer = advect(stack(parts), mine, land)
        solved = solve(lambda a, b: inv[n, a, b], lambda d: strip_inverse[n - 1, d], own_rows(tracer))
        for a in range(4):
            result[4 * (n - 1) + a] = main_from_strip(solved[a], solved[4], a, 3)
        return carry

    lax.fori_loop(1, BLOCKS, block, 0)
    copy_all([(result, out.at[pl.ds(4, 4 * REST)])], sem)


def second_kernel(
    x_in, hx, land, to_south, to_north, to_west, strip_coefs, strip_weights, inverse, strip_inverse, flux_strips,
    received, state_in, payload, state,
):
    fields = First(*[None] * 8, x_in, hx)
    added, added_strip = couple(fields, received, strip_coefs, strip_weights, land[4 * EXT :])
    lane = ext_lanes()
    strip = state_in[4] + jnp.where(lane < 32, added_strip, 0.0)
    top = main_from_strip(state_in[0] + added, strip, 0, 1)
    tracer = stack([top] + [state_in[a] for a in range(1, 4)] + [strip])
    solved = solve_first(inverse, strip_inverse, advect(tracer, (to_south, to_north, to_west), land))
    merged = [main_from_strip(solved[a], solved[4], a, 3) for a in range(4)] + [solved[4]]
    for a in range(5):
        state[a] = merged[a]
    fluxes_out(fields, merged, payload, flux_strips)


def last_kernel(x_in, hx, land, strip_coefs, strip_weights, received, state, rest, out, result, sem):
    del rest
    fields = First(*[None] * 8, x_in, hx)
    added, added_strip = couple(fields, received, strip_coefs, strip_weights, land[4 * EXT :])
    strip = state[4] + added_strip
    result[0] = main_from_strip(state[0] + added, strip, 0, 1)[8:40]
    for a in range(1, 4):
        result[a] = state[a][8:40]
    copy_all([(result, out.at[pl.ds(0, 4)])], sem)


MICROSECONDS = {
    "start_rows_kernel": 3.2,
    "own_first_kernel": 2.0,
    "own_rest_kernel": 2.5,
    "halo_kernel": 2.8,
    "first_kernel": 1.0,
    "rest_first_kernel": 4.3,
    "second_kernel": 1.0,
    "last_kernel": 0.5,
    "rest_second_kernel": 4.6,
}


def call(kernel, outs, args, specs, scratch=(), params=PARAMS, **more):
    cost = int(MICROSECONDS[kernel.__name__] * 3.5e6)
    return pl.pallas_call(
        kernel,
        out_shape=[jax.ShapeDtypeStruct(s, jnp.int32 if spec is SMEM else F32) for s, spec in outs],
        in_specs=specs,
        out_specs=[spec for _, spec in outs],
        scratch_shapes=list(scratch),
        compiler_params=params,
        cost_estimate=pl.CostEstimate(flops=0, bytes_accessed=cost, transcendentals=0),
        **more,
    )(*args)


def index(c, a, o):
    return (c * LAT + a) * LON + o % LON


def lon_pairs(do):
    return [(index(c, a, o), index(c, a, o + do)) for c in range(2) for a in range(LAT) for o in range(LON)]


def swap_pairs(start):
    pairs = []
    for c in range(2):
        for a in range(start, LAT - 1, 2):
            for o in range(LON):
                pairs += [(index(c, a, o), index(c, a + 1, o)), (index(c, a + 1, o), index(c, a, o))]
    return pairs


def fold_pairs(total, comps):
    return [(index(c, LAT - 1, o), index(c, LAT - 1, total - o)) for c in comps for o in range(LON)]


def body(
    adjoint_state,
    winds,
    block_inverse,
    flux_coef,
    sea_mask,
    intersection_cell,
    intersection_weight,
    fold_map,
):
    lam = adjoint_state[0]
    wind = winds[:, 0]
    inv = block_inverse[0]
    rows = (ROW_BUFFER, COLS)
    x, first, second, mirror, low, high, turn, half_turn = call(
        start_rows_kernel,
        [((4, 4, ROWS, COLS), VMEM)] + [(rows, VMEM)] * 3 + [((ROW_BUFFER // 2, COLS), VMEM)] * 2 + [((1,), SMEM)] * 2,
        (fold_map, lam, wind, inv, flux_coef[0], sea_mask, intersection_cell, intersection_weight),
        [SMEM] + [HBM] * 7,
        [
            pltpu.VMEM((3, *rows), F32),
            pltpu.VMEM((32, 16, COLS), F32),
            pltpu.VMEM((2, 32, 16, COLS), F32),
            pltpu.VMEM((1, 4, 4, 16, COLS), F32),
            pltpu.VMEM((4, ROWS, COLS), F32),
            pltpu.VMEM((ROWS, COLS), jnp.int32),
            pltpu.VMEM((2, 4, ROWS, COLS), jnp.int32),
            pltpu.VMEM((4, ROWS, COLS), F32),
            pltpu.SemaphoreType.DMA((10,)),
        ],
        FULL,
    )
    def swap(first, second):
        return lax.ppermute(first, AXES, swap_pairs(0)), lax.ppermute(second, AXES, swap_pairs(1))

    def around(to_west, to_east):
        return lax.ppermute(to_east, AXES, lon_pairs(1)), lax.ppermute(to_west, AXES, lon_pairs(-1))

    def across(value):
        return lax.ppermute(value, AXES, [(i, (i + LAT * LON) % (2 * LAT * LON)) for i in range(2 * LAT * LON)])

    def vmem(*shape):
        return ((*shape, COLS), VMEM)

    state_in = (lam, wind, inv)
    swapped = swap(first, second)

    def across_fold(step, mirror, low, high, lam, wind, inv, x):
        total, in_late_half = step // 2, step % 2
        whole = lax.ppermute(mirror, AXES, fold_pairs(total - 1 + in_late_half, (0, 1)))
        half = lax.ppermute(high if in_late_half else low, AXES, fold_pairs(total - in_late_half, (0, 1)))
        folded = (whole, half)
        own = call(
            own_first_kernel,
            [vmem(12, ROWS), vmem(3 * ROWS), vmem(3 * ROWS)]
            + [vmem(4, ROWS), vmem(2, 4, ROWS), vmem(1, 4, 4, ROWS)],
            (lam, wind, inv, x),
            [HBM] * 4,
            [pltpu.VMEM((4, 4, ROWS, COLS), F32), pltpu.SemaphoreType.DMA((4,))],
        )
        rest_own = call(
            own_rest_kernel,
            [vmem(8 * REST, ROWS), vmem(2 * REST * ROWS), vmem(2 * REST * ROWS)],
            (lam, wind, inv),
            [HBM] * 3,
            [
                pltpu.VMEM((32, ROWS, COLS), F32),
                pltpu.VMEM((2, 32, ROWS, COLS), F32),
                pltpu.VMEM((BLOCKS, 4, 4, ROWS, COLS), F32),
                pltpu.SemaphoreType.DMA((REST, 3)),
            ],
        )
        return *folded, *own, *rest_own

    *folded, own, mid_west, mid_east, lam0, wind0, inv0, rest_own, rest_mid_west, rest_mid_east = lax.switch(
        half_turn[0], [functools.partial(across_fold, step) for step in range(2 * LON)], mirror, low, high, lam, wind, inv, x
    )
    moved = (*swapped, *folded)
    brought = (own, lam0, wind0, inv0, rest_own)
    h, hx, own_halo, rest_h, rest_own_halo, to_west, to_east, own, lam0, wind0, inv0, rest_own = call(
        halo_kernel,
        [vmem(7, 4, 16), vmem(4, 4, 16), vmem(12, 16), vmem(REST, 3, 4, 16), vmem(3 * REST, 16)]
        + [vmem(COL_BUFFER)] * 2
        + [(value.shape, VMEM) for value in brought],
        (fold_map, *moved, mid_west, mid_east, rest_mid_west, rest_mid_east, *brought),
        [SMEM] + [VMEM] * 4 + [HBM] * (4 + BROUGHT),
        [pltpu.VMEM((ROW_BUFFER, COLS), F32)] * 2 + [pltpu.SemaphoreType.DMA((4 + BROUGHT,))],
    )
    from_sides = around(to_west, to_east)
    five = vmem(5, EXT)
    tall = vmem(5 * EXT)
    payload, state, land, *tables = call(
        first_kernel,
        [five, five] + [tall] * 4 + [vmem(k, EXT) for k in (4, 9, 16, 4, 2)],
        (lam0, wind0, inv0, h, own, own_halo, *from_sides, x, hx),
        [VMEM] * (INPUTS + 2),
    )
    received = across(payload)
    rest_args = (*state_in, rest_h, rest_own, rest_own_halo, *from_sides)
    whole = ((32, ROWS, COLS), HBM)
    done = pltpu.SemaphoreType.DMA((1,))
    rest_state, rest_coefs, strip_inverse, *rest_rows = call(
        rest_first_kernel,
        [vmem(REST, 5, ROWS), vmem(REST, 3, 5 * EXT), vmem(REST, 4, ROWS)] + [vmem(120)] * 3,
        (*rest_args, land),
        [VMEM] * (INPUTS + 1),
        [pltpu.VMEM((3, REST, 5, 8, COLS), F32), pltpu.VMEM((3, 120, COLS), F32)]
        + [pltpu.VMEM((5 * EXT, COLS), F32)] * 2,
    )
    def finish(total, rest_rows, received, chain, rest_args):
        folded = [lax.ppermute(rest_rows[2], AXES, fold_pairs(total - k, (1,))) for k in range(2)]
        swapped = swap(*rest_rows[:2])
        received, swapped = lax.optimization_barrier((received, swapped))
        x, hx, land, *tables, state = chain
        payload, state = call(second_kernel, [five, five], (x, hx, land, *tables, received, state), [VMEM] * 13)
        payload, folded = lax.optimization_barrier((payload, folded))
        received = across(payload)
        (rest,) = call(
            rest_second_kernel,
            [whole],
            (*rest_args, *swapped, *folded),
            [SMEM] + [VMEM] * 9,
            [
                pltpu.VMEM((4 * REST, ROWS, COLS), F32),
                pltpu.VMEM((120, COLS), F32),
                pltpu.VMEM((120, COLS), F32),
                pltpu.VMEM((REST, 5, 16, COLS), F32),
                done,
            ],
        )
        return call(
            last_kernel,
            [whole],
            (x, hx, land, *tables[3:5], received, state, rest),
            [VMEM] * 7 + [HBM],
            [pltpu.VMEM((4, ROWS, COLS), F32), done],
            input_output_aliases={7: 0},
        )[0]

    out = lax.switch(
        turn[0],
        [functools.partial(finish, total) for total in range(LON)],
        rest_rows,
        received,
        (x, hx, land, *tables, state),
        (fold_map, inv, strip_inverse, land, rest_state, rest_coefs),
    )
    return out[None]


def solution(mesh):
    return jax.shard_map(
        body,
        mesh=mesh,
        in_specs=(
            P("comp", None, "lat", "lon"),
            P(None, "comp", None, "lat", "lon"),
            P("comp", None, None, None, "lat", "lon"),
            P("comp", None, "lat", "lon"),
            P("lat", "lon"),
            P(None, None, "lat", "lon"),
            P(None, "lat", "lon"),
            P(),
        ),
        out_specs=P("comp", None, "lat", "lon"),
        check_vma=False,
    )
```

```python
import functools

import jax
import jax.numpy as jnp
from jax import lax
from jax.experimental import pallas as pl
from jax.experimental.pallas import tpu as pltpu
from jax.sharding import PartitionSpec as P

DIFFUSE = 0.15
ROWS = 32
EXT = 48
COLS = 128
HALF = COLS // 2
BLOCKS = 8
F32 = jnp.float32
AXES = ("comp", "lat", "lon")
LAT, LON = 8, 8
VMEM = pl.BlockSpec(memory_space=pltpu.VMEM)
ANY = pl.BlockSpec(memory_space=pl.ANY)
HBM = pl.BlockSpec(memory_space=pltpu.HBM)
SMEM = pl.BlockSpec(memory_space=pltpu.SMEM)
PARAMS = pltpu.CompilerParams(vmem_limit_bytes=16 * 1024 * 1024)
FULL = pltpu.CompilerParams(vmem_limit_bytes=63 * 1024 * 1024)


def places():
    comp, lat, lon = (lax.axis_index(name) for name in AXES)
    return comp, lat, lon, lat == LAT - 1


def first_pieces():
    pieces = []
    for a in range(4):
        pieces.append((0, 0, a, 8 * a, 8))
        pieces.append((1, 0, a, 32 + 8 * a, 8))
        pieces.append((2, 0, a, 64 + 7 * a, 7))
    for b in range(4):
        pieces.append((3 + b, 0, 0, 92 + 5 * b, 5))
        for a in range(1, 4):
            pieces.append((3 + b, 0, a, 120 + 4 * (4 * (a - 1) + b), 4))
    return pieces


def rest_pieces():
    pieces = []
    for n in range(1, BLOCKS):
        at = 240 + 32 * (n - 1)
        for a in range(4):
            pieces.append((0, n, a, at + 3 * a, 3))
            pieces.append((1, n, a, at + 12 + 3 * a, 3))
            pieces.append((2, n, a, at + 24 + 2 * a, 2))
    return pieces


ROW_BUFFER = 240 + 32 * (BLOCKS - 1)
SINGLES = (
    [(0, f, 168 + 5 * f, 5) for f in range(4)]
    + [(1 + s // 4, s % 4, 188 + 4 * s, 4) for s in range(9)]
    + [(3, 1, 112, 8), (3, 2, 224, 8)]
)


def mirrored_single(quad, member):
    if quad in (1, 2) or (quad == 3 and member == 0):
        s = 8 - (4 * (quad - 1) + member)
        return 1 + s // 4, s % 4
    return quad, member


def copy_all(pairs, sem):
    copies = [pltpu.make_async_copy(a, b, sem.at[k]) for k, (a, b) in enumerate(pairs)]
    for copy in copies:
        copy.start()
    for copy in copies:
        copy.wait()


def reverse(tile):
    flip = 7 - lax.broadcasted_iota(jnp.int32, (8, COLS), 0)
    return jnp.take_along_axis(tile, flip, axis=0, mode="promise_in_bounds")


def put_piece(store, ref, at, count):
    end = ref.shape[0]
    store[0, at : at + count, :] = ref[end - count : end, :]
    store[1, at : at + count, :] = ref[0:count, :]


def put_mirrored(store, ref, at, count, sign):
    end = ref.shape[0]
    turned = reverse(ref[end - 8 : end, :])
    if sign < 0:
        turned = -turned
    store[2, at : at + count, :] = turned[0:count, :]


def field_ref(lam, winds, inv, field, n, a):
    if field == 0:
        return lam.at[4 * n + a]
    if field <= 2:
        return winds.at[2 - field, 4 * n + a]
    return inv.at[n, a, field - 3]


def sign_of(field):
    return -1 if field in (1, 2) else 1


def hand_over(store, first_out, second_out, mirror_out):
    _, lat, _, _ = places()
    odd = lat % 2
    first_out[...] = store[odd]
    second_out[...] = store[1 - odd]
    mirror_out[...] = store[2]


def start_rows_kernel(
    fold, lam_in, winds_in, inv_in, fc_in, mask_in, cell_in, weight_in,
    x_out, first_out, second_out, mirror_out, low_out, high_out, turn_out, half_turn_out,
    store, lam, winds, inv, fc, mask, cell, weight, sem,
):
    comp, lat_pos, lon_pos, _ = places()
    turn_out[0] = fold[0] // COLS
    half_turn_out[0] = fold[0] // HALF
    pairs = [(fc_in, fc), (mask_in, mask), (cell_in, cell), (weight_in, weight)]
    for half, rows in enumerate((pl.ds(0, 8), pl.ds(ROWS - 8, 8))):
        at = pl.ds(8 * half, 8)
        pairs.append((lam_in.at[:, rows], lam.at[:, at]))
        pairs.append((winds_in.at[:, :, rows], winds.at[:, :, at]))
        pairs.append((inv_in.at[pl.ds(0, 1), :, :, rows], inv.at[:, :, :, at]))
    copy_all(pairs, sem)
    wet = mask[...].astype(F32)
    x_out[3, 1] = wet
    x_out[3, 2] = jnp.where(comp == 1, wet, jnp.ones_like(wet))
    x_out[3, 3] = jnp.zeros_like(wet)
    for f in range(4):
        x_out[0, f] = fc[f]
    rows = lat_pos * ROWS + lax.broadcasted_iota(jnp.int32, (ROWS, COLS), 0)
    cols = lon_pos * COLS + lax.broadcasted_iota(jnp.int32, (ROWS, COLS), 1)
    row_shift = [cell[0, k] - rows for k in range(4)]
    col_shift = []
    for k in range(4):
        d = cell[1, k] - cols
        d = jnp.where(d > 1, d - LON * COLS, d)
        col_shift.append(jnp.where(d < -1, d + LON * COLS, d))
    code = [3 * row_shift[k] + col_shift[k] + 4 for k in range(4)]
    weights = [weight[k] for k in range(4)]
    for s in range(9):
        total = jnp.where(code[0] == s, weights[0], 0.0)
        for k in range(1, 4):
            total = total + jnp.where(code[k] == s, weights[k], 0.0)
        x_out[1 + s // 4, s % 4] = total
    pieces = [(field_ref(lam, winds, inv, f, n, a), at, count, sign_of(f)) for f, n, a, at, count in first_pieces()]
    pieces += [(field_ref(lam, winds, inv, f, n, a), at, count, sign_of(f)) for f, n, a, at, count in rest_pieces()]
    for ref, at, count, _ in pieces:
        put_piece(store, ref, at, count)
    for quad, member, at, count in SINGLES:
        put_piece(store, x_out.at[quad, member], at, count)

    @pl.when(places()[3])
    def _():
        for ref, at, count, sign in pieces:
            put_mirrored(store, ref, at, count, sign)
        for quad, member, at, count in SINGLES:
            put_mirrored(store, x_out.at[mirrored_single(quad, member)], at, count, 1)
        a, b = store[2, 0 : ROW_BUFFER // 2, :], store[2, ROW_BUFFER // 2 : ROW_BUFFER, :]
        low = lax.broadcasted_iota(jnp.int32, a.shape, 1) < HALF
        low_out[...] = jnp.where(low, a, roll_lanes(b, HALF))
        high_out[...] = jnp.where(low, roll_lanes(a, HALF), b)

    hand_over(store, first_out, second_out, mirror_out)


def lanes():
    return lax.broadcasted_iota(jnp.int32, (8, COLS), 1)


def roll_lanes(x, by):
    by = by % COLS
    return x if by == 0 else pltpu.roll(x, by, axis=1)


def roll_rows(x, by):
    by = by % x.shape[0]
    return x if by == 0 else pltpu.roll(x, by, axis=0)


def pack_columns(slots, strip_at, to_west, to_east, buffer_at, row_count):
    rows = row_count
    used = [k for k, members in enumerate(slots) if members is not None]
    zero = jnp.zeros((rows, COLS), F32)
    lane = lax.broadcasted_iota(jnp.int32, (len(used) * rows, COLS), 1)
    pair = jnp.zeros((len(used) * rows, COLS), F32)
    for a in range(4):
        values = [zero if slots[k][a] is None else slots[k][a] for k in used]
        moved = roll_lanes(jnp.concatenate(values, axis=0), 32 * a + 8)
        pair = jnp.where((lane >= 32 * a) & (lane < 32 * a + 16), moved, pair)
    strips = jnp.where(lane % 32 < 16, pair, roll_lanes(pair, 16))
    group = lax.broadcasted_iota(jnp.int32, (rows, COLS), 1) % 32
    buffers = -(-len(slots) // 4)
    west, east = [zero] * buffers, [zero] * buffers
    for i, k in enumerate(used):
        ref, at = strip_at[k]
        ref[at] = strips[i * rows : (i + 1) * rows]
        mine = pair[i * rows : (i + 1) * rows]
        buffer, slot = k // 4, k % 4
        here = (group >= 8 * slot) & (group < 8 * slot + 8)
        west[buffer] = jnp.where(here, roll_lanes(mine, 8 * slot - 8), west[buffer])
        east[buffer] = jnp.where(here, roll_lanes(mine, 8 * slot), east[buffer])
    for buffer in range(buffers):
        at = pl.ds(pl.multiple_of(rows * (buffer_at + buffer), 8), rows)
        to_west[at, :] = west[buffer]
        to_east[at, :] = east[buffer]


def block_slots(read, extra):
    slots = [[read(field, a) for a in range(4)] for field in range(3)] + [extra]
    return slots + [[read(3 + (a + d) % 4, a) for a in range(4)] for d in range(4)]


def single_slots(read):
    return [[None if q == 3 and a == 3 else read(q, a) for a in range(4)] for q in range(1, 4)]


def own_kernel(
    lam_in, winds_in, inv_in, x_in,
    own, to_west, to_east, lam0, winds0, inv0, rest_own, rest_west, rest_east,
    lam, winds, inv, x, first_sem, sem,
):
    four = pl.ds(0, 4)
    first = [(inv_in.at[pl.ds(0, 1)], inv0), (winds_in.at[:, four], winds0), (lam_in.at[four], lam0), (x_in, x)]
    first = [pltpu.make_async_copy(a, b, first_sem.at[k]) for k, (a, b) in enumerate(first)]

    def fetch(n):
        levels = pl.ds(4 * n, 4)
        pairs = ((winds_in.at[:, levels], winds.at[:, levels]), (lam_in.at[levels], lam.at[levels]), (inv_in.at[n], inv.at[n]))
        return [pltpu.make_async_copy(a, b, sem.at[n - 1, k]) for k, (a, b) in enumerate(pairs)]

    for copy in first + [copy for n in range(1, BLOCKS) for copy in fetch(n)]:
        copy.start()
    for copy in first:
        copy.wait()
    slots = block_slots(lambda field, a: field_ref(lam0, winds0, inv0, field, 0, a)[...], [x[0, f] for f in range(4)])
    slots += single_slots(lambda q, a: x[q, a])
    pack_columns(slots, [(own, k) for k in range(12)], to_west, to_east, 0, ROWS)

    def step(n, carry):
        for copy in fetch(n):
            copy.wait()

        def read(field, a):
            return field_ref(lam, winds, inv, field, n, a)[...]

        strip_at = [(rest_own, 8 * (n - 1) + k) for k in range(8)]
        pack_columns(block_slots(read, None), strip_at, rest_west, rest_east, 2 * (n - 1), ROWS)
        return carry

    lax.fori_loop(1, BLOCKS, step, 0)


def settle_rows(first_in, second_in, south, north, beyond_fold):
    _, lat, _, is_top = places()
    even = lat % 2 == 0

    @pl.when(even)
    def _():
        south[...] = second_in[...]
        north[...] = first_in[...]

    @pl.when(jnp.logical_not(even))
    def _():
        south[...] = first_in[...]

    @pl.when(jnp.logical_not(even) & jnp.logical_not(is_top))
    def _():
        north[...] = second_in[...]

    pl.when(is_top)(beyond_fold)


def pick(values, at):
    tiles = [
        jnp.take_along_axis(values[8 * t : 8 * t + 8], at, axis=1, mode="promise_in_bounds")
        for t in range(values.shape[0] // 8)
    ]
    return jnp.concatenate(tiles, axis=0)


REST = BLOCKS - 1
COL_OWN = 16 * (3 + REST)
COL_BUFFER = COL_OWN + ROWS * (3 + 2 * REST)


def halo_kernel(
    fold, first_in, second_in, fold_whole, fold_half, mid_west, mid_east, rest_west, rest_east, *refs,
):
    brought_in, (h, hx, own, rest_h, rest_own, to_west, to_east), refs = refs[:BROUGHT], refs[BROUGHT : BROUGHT + 7], refs[BROUGHT + 7 :]
    brought, (south, north, sem) = refs[:BROUGHT], refs[BROUGHT:]
    mids = (ROWS * 3, ROWS * 2 * REST)
    pairs = [(rest_west, to_west.at[pl.ds(COL_OWN + mids[0], mids[1])])]
    pairs += [(rest_east, to_east.at[pl.ds(COL_OWN + mids[0], mids[1])])]
    pairs += [(mid_west, to_west.at[pl.ds(COL_OWN, mids[0])]), (mid_east, to_east.at[pl.ds(COL_OWN, mids[0])])]
    pairs += list(zip(brought_in, brought, strict=True))
    copies = [pltpu.make_async_copy(a, b, sem.at[k]) for k, (a, b) in enumerate(pairs)]
    for copy in copies:
        copy.start()

    def beyond_fold():
        turn, lane = fold[0] % COLS, lanes()
        source = jnp.where(turn >= lane, turn - lane, turn - lane + COLS)
        in_half = source % HALF
        few = jnp.concatenate([pick(fold_half[...], in_half), pick(fold_half[...], in_half + HALF)], axis=0)
        many = pick(fold_whole[...], source)
        column = lax.broadcasted_iota(jnp.int32, (ROW_BUFFER, COLS), 1)
        whole_is_first = turn >= HALF
        first = (column <= turn).astype(jnp.int32)
        north[...] = jnp.where(first == whole_is_first.astype(jnp.int32), many, few)

    settle_rows(first_in, second_in, south, north, beyond_fold)
    for field, _, a, at, count in first_pieces():
        h[field, a, 8 - count : 8, :] = south[at : at + count, :]
        h[field, a, 8 : 8 + count, :] = north[at : at + count, :]
    for quad, member, at, count in SINGLES:
        hx[quad, member, 8 - count : 8, :] = south[at : at + count, :]
        hx[quad, member, 8 : 8 + count, :] = north[at : at + count, :]
    for field, n, a, at, count in rest_pieces():
        rest_h[n - 1, field, a, 8 - count : 8, :] = south[at : at + count, :]
        rest_h[n - 1, field, a, 8 : 8 + count, :] = north[at : at + count, :]
    slots = block_slots(lambda field, a: h[field, a], [hx[0, f] for f in range(4)])
    slots += single_slots(lambda q, a: hx[q, a]) + [None]
    strip_at = [(own, k) for k in range(11)] + [None]
    for n in range(REST):
        slots += [[rest_h[n, field, a] for a in range(4)] for field in range(3)] + [None]
        strip_at += [(rest_own, 3 * n + k) for k in range(3)] + [None]
    pack_columns(slots, strip_at, to_west, to_east, 0, 16)
    for copy in copies:
        copy.wait()


BROUGHT = 5


def ext_lanes():
    return lax.broadcasted_iota(jnp.int32, (EXT, COLS), 1)


def barrier_masks():
    comp, _, _, is_top = places()
    row = lax.broadcasted_iota(jnp.int32, (EXT, COLS), 0)
    apart = is_top & (comp == 0)
    keep_c = jnp.where(apart & (row == 40), 0.0, 1.0).astype(F32)
    keep_d = jnp.where(apart & (row == 39), 0.0, 1.0).astype(F32)
    return stack([keep_c] * 5), stack([keep_d] * 5)


def edges_of(slot, west, east):
    group = lax.broadcasted_iota(jnp.int32, west.shape, 1) % 32
    edge = jnp.where(group < 8, roll_lanes(west, -8 * slot), roll_lanes(east, 24 - 8 * slot))
    return edge, (group >= 8) & (group < 24)


def assemble_strip(slot, sides, buffer, mid, halo_buffer=None, halo=None):
    rows = pl.ds(pl.multiple_of(COL_OWN + ROWS * buffer, 8), ROWS)
    edge, inner = edges_of(slot, sides[0][rows, :], sides[1][rows, :])
    middle = jnp.where(inner, mid, edge)
    if halo is None:
        return middle
    rows = pl.ds(pl.multiple_of(16 * halo_buffer, 8), 16)
    edge, inner = edges_of(slot, sides[0][rows, :], sides[1][rows, :])
    outer = jnp.where(inner, halo, edge)
    return jnp.concatenate([outer[0:8], middle, outer[8:16]], axis=0)


class First:
    def __init__(self, lam, winds, inv, h, own, own_halo, from_west, from_east, x_in, hx):
        self.lam, self.winds, self.inv, self.h = lam, winds, inv, h
        self.own, self.own_halo, self.sides = own, own_halo, (from_west, from_east)
        self.x_in, self.hx = x_in, hx

    def main(self, field, n, a):
        halo = self.h[field, a]
        mid = field_ref(self.lam, self.winds, self.inv, field, 0, a)[...]
        return jnp.concatenate([halo[0:8], mid, halo[8:16]], axis=0)

    def single(self, quad, a):
        halo = self.hx[quad, a]
        return jnp.concatenate([halo[0:8], self.x_in[quad, a], halo[8:16]], axis=0)

    def strip(self, n, which, slot):
        at = 4 * which + slot
        return assemble_strip(slot, self.sides, which, self.own[at], which, self.own_halo[at])

    def single_strip(self, quad):
        return self.strip(0, 0, 3) if quad == 0 else self.strip(0, 2, quad - 1)


class Rest:
    def __init__(self, lam, winds, inv, h, own, own_halo, from_west, from_east):
        self.lam, self.winds, self.inv, self.h = lam, winds, inv, h
        self.own, self.own_halo, self.sides = own, own_halo, (from_west, from_east)

    def main(self, field, n, a):
        mid = field_ref(self.lam, self.winds, self.inv, field, n, a)[...]
        if field >= 3:
            return mid
        halo = self.h[n - 1, field, a]
        return jnp.concatenate([halo[0:8], mid, halo[8:16]], axis=0)

    def strip(self, n, which, slot):
        mid = self.own[8 * (n - 1) + 4 * which + slot]
        buffer = 3 + 2 * (n - 1) + which
        if which == 1:
            return assemble_strip(slot, self.sides, buffer, mid)
        return assemble_strip(slot, self.sides, buffer, mid, 2 + n, self.own_halo[3 * (n - 1) + slot])


def stack(values):
    return jnp.concatenate(values, axis=0)


def unstack(value):
    return [value[EXT * k : EXT * (k + 1)] for k in range(value.shape[0] // EXT)]


def replicate(strip, a):
    lane = ext_lanes()
    out = roll_lanes(strip, -32 * a)
    base = jnp.where(lane < 32, out, 0.0)
    for g in range(1, 4):
        base = jnp.where((lane >= 32 * g) & (lane < 32 * g + 32), roll_lanes(out, 32 * g), base)
    return base


def advect(tracer, coefs, land):
    to_south, to_north, to_west = coefs
    for _ in range(3):
        a = to_west[...] * tracer
        b = (2 * DIFFUSE) * tracer - a
        east, west = roll_lanes(a, -1), roll_lanes(b, 1)
        new = (1.0 - 4 * DIFFUSE) * tracer
        new = new + roll_rows(to_south[...] * tracer, -1) + roll_rows(to_north[...] * tracer, 1)
        tracer = (new + (east + west)) * land[...]
    return tracer


def coefficients(fields, n, masks):
    merid = stack([fields.main(1, n, a) for a in range(4)] + [fields.strip(n, 0, 1)])
    zonal = stack([fields.main(2, n, a) for a in range(4)] + [fields.strip(n, 0, 2)])
    to_south = (DIFFUSE + 0.5 * merid) * masks[0]
    to_north = (DIFFUSE - 0.5 * merid) * masks[1]
    return to_south, to_north, DIFFUSE + 0.5 * zonal


def solve(inverse, strip_inverse, old):
    moved = [old[4]] + [roll_lanes(old[4], -32 * d) for d in range(1, 4)]
    new = []
    for a in range(4):
        total = inverse(a, 0) * old[0]
        for b in range(1, 4):
            total = total + inverse(a, b) * old[b]
        new.append(total)
    total = strip_inverse(0) * moved[0]
    for d in range(1, 4):
        total = total + strip_inverse(d) * moved[d]
    return new + [total]


def solve_first(inverse, strip_inverse, tracer):
    return solve(lambda a, b: inverse[4 * a + b], lambda d: strip_inverse[d], unstack(tracer))


def main_from_strip(main, strip, a, width):
    lane = lax.broadcasted_iota(jnp.int32, main.shape, 1)
    main = jnp.where(lane < width, roll_lanes(strip, -(32 * a + 8)), main)
    return jnp.where(lane >= COLS - width, roll_lanes(strip, 104 - 32 * a), main)


def merge(state):
    strip = state[4]
    lane = lax.broadcasted_iota(jnp.int32, strip.shape, 1)
    new_strip = strip
    mains = [main_from_strip(state[a], strip, a, 3) for a in range(4)]
    for a in range(4):
        west = (lane >= 32 * a + 11) & (lane < 32 * a + 16)
        east = (lane >= 32 * a + 16) & (lane < 32 * a + 21)
        new_strip = jnp.where(west, roll_lanes(state[a], 32 * a + 8), new_strip)
        new_strip = jnp.where(east, roll_lanes(state[a], 32 * a + 24), new_strip)
    return mains + [new_strip]


def load_block(fields, n):
    return [fields.main(0, n, a) for a in range(4)] + [fields.strip(n, 0, 0)]


def fluxes_out(fields, state, payload, strips):
    surface = state[0] * fields.single(3, 1)
    for f in range(4):
        payload[f] = fields.single(0, f) * surface
    payload[4] = strips[0] * replicate(state[4] * strips[1], 0)


def couple(fields, received, strip_coefs, strip_weights, land_strip):
    sources = [received[f] for f in range(4)] + [roll_lanes(received[4], -32 * f) for f in range(4)]
    coefs = [fields.single(0, f) for f in range(4)] + [strip_coefs[f] for f in range(4)]
    weights = [fields.single(1 + s // 4, s % 4) for s in range(9)]
    moved = {dc: [roll_lanes(source, -dc) for source in sources] for dc in (-1, 0, 1)}
    totals = []
    for table, parts in ((weights, range(4)), ([strip_weights[s] for s in range(9)], range(4, 8))):
        total = None
        for k in parts:
            part = None
            for dr in (-1, 0, 1):
                across = None
                for dc in (-1, 0, 1):
                    term = table[3 * (dr + 1) + dc + 1] * roll_rows(moved[dc][k], -dr)
                    across = term if across is None else across + term
                part = across if part is None else part + across
            total = coefs[k] * part if total is None else total + coefs[k] * part
        totals.append(total)
    return totals[0] * fields.single(3, 2), totals[1] * land_strip


INPUTS = 8


def first_kernel(*refs):
    fields = First(*refs[: INPUTS + 2])
    payload, state, land, to_south, to_north, to_west, strip_coefs, strip_weights = refs[INPUTS + 2 : INPUTS + 10]
    inverse, strip_inverse, flux_strips = refs[INPUTS + 10 :]
    quads = [fields.single_strip(q) for q in range(4)]
    main_land = fields.single(3, 2)
    land[...] = stack([main_land] * 4 + [replicate(quads[3], 2)])
    coefs = (to_south, to_north, to_west)
    for ref, value in zip(coefs, coefficients(fields, 0, barrier_masks()), strict=True):
        ref[...] = value
    tracer = advect(stack(load_block(fields, 0)), coefs, land)
    for a in range(4):
        for b in range(4):
            inverse[4 * a + b] = fields.main(3 + b, 0, a)
        strip_inverse[a] = fields.strip(0, 1, a)
    flux_strips[0] = quads[0]
    flux_strips[1] = roll_lanes(quads[3], -32)
    merged = merge(solve_first(inverse, strip_inverse, tracer))
    for a in range(5):
        state[a] = merged[a]
    fluxes_out(fields, merged, payload, flux_strips)
    for f in range(4):
        strip_coefs[f] = roll_lanes(quads[0], -32 * f)
    for k in range(9):
        strip_weights[k] = roll_lanes(quads[1 + k // 4], -32 * (k % 4))


def own_rows(tracer):
    return [value[8:40] for value in unstack(tracer)]


def rest_first_kernel(*refs):
    fields = Rest(*refs[:INPUTS])
    land, state, coefs, strip_inverse, first_out, second_out, mirror_out, edges, store, mask_c, mask_d = refs[INPUTS:]
    mask_c[...], mask_d[...] = barrier_masks()

    def block(n, carry):
        mine = tuple(coefs.at[n - 1, k] for k in range(3))
        for ref, value in zip(mine, coefficients(fields, n, (mask_c[...], mask_d[...])), strict=True):
            ref[...] = value
        tracer = advect(stack(load_block(fields, n)), mine, land)
        for d in range(4):
            strip_inverse[n - 1, d] = fields.strip(n, 1, d)
        merged = merge(
            solve(lambda a, b: fields.main(3 + b, n, a), lambda d: strip_inverse[n - 1, d], own_rows(tracer))
        )
        for a in range(5):
            state[n - 1, a] = merged[a]
            edges[0, n - 1, a] = merged[a][24:32]
            edges[1, n - 1, a] = merged[a][0:8]
            edges[2, n - 1, a] = reverse(merged[a][24:32])
        return carry

    lax.fori_loop(1, BLOCKS, block, 0, unroll=True)
    for n in range(REST):
        for a in range(5):
            at = 24 * a + 3 * n
            store[0, at : at + 3, :] = edges[0, n, a, 5:8, :]
            store[1, at : at + 3, :] = edges[1, n, a, 0:3, :]
            store[2, at : at + 3, :] = edges[2, n, a, 0:3, :]
    for k in range(3):
        for a in range(5):
            store[k, 24 * a + 21 : 24 * a + 24, :] = jnp.zeros((3, COLS), F32)
    hand_over(store, first_out, second_out, mirror_out)


def rest_second_kernel(*refs):
    fold, inv, strip_inverse, land, state, coefs, first_in, second_in, fold_a, fold_b = refs[:10]
    out, result, south, north, halo, sem = refs[10:]

    def beyond_fold():
        turn, lane = fold[0] % COLS, lanes()
        source = jnp.where(turn >= lane, turn - lane, turn - lane + COLS)
        keep = lax.broadcasted_iota(jnp.int32, (24, COLS), 1) <= turn
        group, in_group = lane // 32, lane % 32
        column = jnp.where(in_group < 16, in_group - 8, in_group + 104)
        at_a = turn - column
        at_b = at_a + COLS
        main_a, main_b = jnp.clip(at_a, 0, COLS - 1), jnp.clip(at_b, 0, COLS - 1)
        strip_a = 32 * group + jnp.clip(at_a - 104, 0, 31)
        strip_b = 32 * group + jnp.clip(at_b + 8, 0, 31)
        wide_a = stack([at_a] * 3)
        wide_b = stack([at_b] * 3)
        wide_group = stack([group] * 3)
        strip = jnp.where(wide_a >= COLS, pick(fold_a[96:120, :], strip_a), pick(fold_b[96:120, :], strip_b))
        for a in range(4):
            values_a, values_b = fold_a[24 * a : 24 * a + 24, :], fold_b[24 * a : 24 * a + 24, :]
            north[24 * a : 24 * a + 24, :] = jnp.where(keep, pick(values_a, source), pick(values_b, source))
            inside = (wide_group == a) & (wide_a < COLS) & (wide_b >= 0)
            strip = jnp.where(inside, jnp.where(wide_a >= 0, pick(values_a, main_a), pick(values_b, main_b)), strip)
        north[96:120, :] = strip

    settle_rows(first_in, second_in, south, north, beyond_fold)
    for n in range(REST):
        for a in range(5):
            at = 24 * a + 3 * n
            halo[n, a, 5:8, :] = south[at : at + 3, :]
            halo[n, a, 8:11, :] = north[at : at + 3, :]

    def block(n, carry):
        mine = tuple(coefs.at[n - 1, k] for k in range(3))
        parts = []
        for a in range(5):
            edge = halo[n - 1, a]
            parts += [edge[0:8], state[n - 1, a], edge[8:16]]
        tracer = advect(stack(parts), mine, land)
        solved = solve(lambda a, b: inv[n, a, b], lambda d: strip_inverse[n - 1, d], own_rows(tracer))
        for a in range(4):
            result[4 * (n - 1) + a] = main_from_strip(solved[a], solved[4], a, 3)
        return carry

    lax.fori_loop(1, BLOCKS, block, 0)
    copy_all([(result, out.at[pl.ds(4, 4 * REST)])], sem)


def second_kernel(
    x_in, hx, land, to_south, to_north, to_west, strip_coefs, strip_weights, inverse, strip_inverse, flux_strips,
    received, state_in, payload, state,
):
    fields = First(*[None] * 8, x_in, hx)
    added, added_strip = couple(fields, received, strip_coefs, strip_weights, land[4 * EXT :])
    lane = ext_lanes()
    strip = state_in[4] + jnp.where(lane < 32, added_strip, 0.0)
    top = main_from_strip(state_in[0] + added, strip, 0, 1)
    tracer = stack([top] + [state_in[a] for a in range(1, 4)] + [strip])
    solved = solve_first(inverse, strip_inverse, advect(tracer, (to_south, to_north, to_west), land))
    merged = [main_from_strip(solved[a], solved[4], a, 3) for a in range(4)] + [solved[4]]
    for a in range(5):
        state[a] = merged[a]
    fluxes_out(fields, merged, payload, flux_strips)


def last_kernel(x_in, hx, land, strip_coefs, strip_weights, received, state, rest, out, result, sem):
    del rest
    fields = First(*[None] * 8, x_in, hx)
    added, added_strip = couple(fields, received, strip_coefs, strip_weights, land[4 * EXT :])
    strip = state[4] + added_strip
    result[0] = main_from_strip(state[0] + added, strip, 0, 1)[8:40]
    for a in range(1, 4):
        result[a] = state[a][8:40]
    copy_all([(result, out.at[pl.ds(0, 4)])], sem)


MICROSECONDS = {
    "start_rows_kernel": 3.2,
    "own_kernel": 4.0,
    "halo_kernel": 2.8,
    "first_kernel": 1.0,
    "rest_first_kernel": 4.3,
    "second_kernel": 1.0,
    "last_kernel": 0.5,
    "rest_second_kernel": 4.6,
}


def call(kernel, outs, args, specs, scratch=(), params=PARAMS, **more):
    cost = int(MICROSECONDS[kernel.__name__] * 3.5e6)
    return pl.pallas_call(
        kernel,
        out_shape=[jax.ShapeDtypeStruct(s, jnp.int32 if spec is SMEM else F32) for s, spec in outs],
        in_specs=specs,
        out_specs=[spec for _, spec in outs],
        scratch_shapes=list(scratch),
        compiler_params=params,
        cost_estimate=pl.CostEstimate(flops=0, bytes_accessed=cost, transcendentals=0),
        **more,
    )(*args)


def index(c, a, o):
    return (c * LAT + a) * LON + o % LON


def lon_pairs(do):
    return [(index(c, a, o), index(c, a, o + do)) for c in range(2) for a in range(LAT) for o in range(LON)]


def swap_pairs(start):
    pairs = []
    for c in range(2):
        for a in range(start, LAT - 1, 2):
            for o in range(LON):
                pairs += [(index(c, a, o), index(c, a + 1, o)), (index(c, a + 1, o), index(c, a, o))]
    return pairs


def fold_pairs(total, comps):
    return [(index(c, LAT - 1, o), index(c, LAT - 1, total - o)) for c in comps for o in range(LON)]


def body(
    adjoint_state,
    winds,
    block_inverse,
    flux_coef,
    sea_mask,
    intersection_cell,
    intersection_weight,
    fold_map,
):
    lam = adjoint_state[0]
    wind = winds[:, 0]
    inv = block_inverse[0]
    rows = (ROW_BUFFER, COLS)
    x, first, second, mirror, low, high, turn, half_turn = call(
        start_rows_kernel,
        [((4, 4, ROWS, COLS), VMEM)] + [(rows, VMEM)] * 3 + [((ROW_BUFFER // 2, COLS), VMEM)] * 2 + [((1,), SMEM)] * 2,
        (fold_map, lam, wind, inv, flux_coef[0], sea_mask, intersection_cell, intersection_weight),
        [SMEM] + [HBM] * 7,
        [
            pltpu.VMEM((3, *rows), F32),
            pltpu.VMEM((32, 16, COLS), F32),
            pltpu.VMEM((2, 32, 16, COLS), F32),
            pltpu.VMEM((1, 4, 4, 16, COLS), F32),
            pltpu.VMEM((4, ROWS, COLS), F32),
            pltpu.VMEM((ROWS, COLS), jnp.int32),
            pltpu.VMEM((2, 4, ROWS, COLS), jnp.int32),
            pltpu.VMEM((4, ROWS, COLS), F32),
            pltpu.SemaphoreType.DMA((10,)),
        ],
        FULL,
    )
    def swap(first, second):
        return lax.ppermute(first, AXES, swap_pairs(0)), lax.ppermute(second, AXES, swap_pairs(1))

    def around(to_west, to_east):
        return lax.ppermute(to_east, AXES, lon_pairs(1)), lax.ppermute(to_west, AXES, lon_pairs(-1))

    def across(value):
        return lax.ppermute(value, AXES, [(i, (i + LAT * LON) % (2 * LAT * LON)) for i in range(2 * LAT * LON)])

    def vmem(*shape):
        return ((*shape, COLS), VMEM)

    state_in = (lam, wind, inv)
    swapped = swap(first, second)

    def across_fold(step, mirror, low, high, lam, wind, inv, x):
        total, in_late_half = step // 2, step % 2
        whole = lax.ppermute(mirror, AXES, fold_pairs(total - 1 + in_late_half, (0, 1)))
        half = lax.ppermute(high if in_late_half else low, AXES, fold_pairs(total - in_late_half, (0, 1)))
        folded = (whole, half)
        own = call(
            own_kernel,
            [vmem(12, ROWS), vmem(3 * ROWS), vmem(3 * ROWS)]
            + [vmem(4, ROWS), vmem(2, 4, ROWS), vmem(1, 4, 4, ROWS)]
            + [vmem(8 * REST, ROWS), vmem(2 * REST * ROWS), vmem(2 * REST * ROWS)],
            (lam, wind, inv, x),
            [HBM] * 4,
            [
                pltpu.VMEM((32, ROWS, COLS), F32),
                pltpu.VMEM((2, 32, ROWS, COLS), F32),
                pltpu.VMEM((BLOCKS, 4, 4, ROWS, COLS), F32),
                pltpu.VMEM((4, 4, ROWS, COLS), F32),
                pltpu.SemaphoreType.DMA((4,)),
                pltpu.SemaphoreType.DMA((REST, 3)),
            ],
        )
        return *folded, *own

    *folded, own, mid_west, mid_east, lam0, wind0, inv0, rest_own, rest_mid_west, rest_mid_east = lax.switch(
        half_turn[0], [functools.partial(across_fold, step) for step in range(2 * LON)], mirror, low, high, lam, wind, inv, x
    )
    moved = (*swapped, *folded)
    brought = (own, lam0, wind0, inv0, rest_own)
    h, hx, own_halo, rest_h, rest_own_halo, to_west, to_east, own, lam0, wind0, inv0, rest_own = call(
        halo_kernel,
        [vmem(7, 4, 16), vmem(4, 4, 16), vmem(12, 16), vmem(REST, 3, 4, 16), vmem(3 * REST, 16)]
        + [vmem(COL_BUFFER)] * 2
        + [(value.shape, VMEM) for value in brought],
        (fold_map, *moved, mid_west, mid_east, rest_mid_west, rest_mid_east, *brought),
        [SMEM] + [VMEM] * 4 + [HBM] * (4 + BROUGHT),
        [pltpu.VMEM((ROW_BUFFER, COLS), F32)] * 2 + [pltpu.SemaphoreType.DMA((4 + BROUGHT,))],
    )
    from_sides = around(to_west, to_east)
    five = vmem(5, EXT)
    tall = vmem(5 * EXT)
    payload, state, land, *tables = call(
        first_kernel,
        [five, five] + [tall] * 4 + [vmem(k, EXT) for k in (4, 9, 16, 4, 2)],
        (lam0, wind0, inv0, h, own, own_halo, *from_sides, x, hx),
        [VMEM] * (INPUTS + 2),
    )
    received = across(payload)
    rest_args = (*state_in, rest_h, rest_own, rest_own_halo, *from_sides)
    whole = ((32, ROWS, COLS), HBM)
    done = pltpu.SemaphoreType.DMA((1,))
    rest_state, rest_coefs, strip_inverse, *rest_rows = call(
        rest_first_kernel,
        [vmem(REST, 5, ROWS), vmem(REST, 3, 5 * EXT), vmem(REST, 4, ROWS)] + [vmem(120)] * 3,
        (*rest_args, land),
        [VMEM] * (INPUTS + 1),
        [pltpu.VMEM((3, REST, 5, 8, COLS), F32), pltpu.VMEM((3, 120, COLS), F32)]
        + [pltpu.VMEM((5 * EXT, COLS), F32)] * 2,
    )
    def finish(total, rest_rows, received, chain, rest_args):
        folded = [lax.ppermute(rest_rows[2], AXES, fold_pairs(total - k, (1,))) for k in range(2)]
        swapped = swap(*rest_rows[:2])
        x, hx, land, *tables, state = chain
        payload, state = call(second_kernel, [five, five], (x, hx, land, *tables, received, state), [VMEM] * 13)
        payload, swapped, folded = lax.optimization_barrier((payload, swapped, folded))
        received = across(payload)
        (rest,) = call(
            rest_second_kernel,
            [whole],
            (*rest_args, *swapped, *folded),
            [SMEM] + [VMEM] * 9,
            [
                pltpu.VMEM((4 * REST, ROWS, COLS), F32),
                pltpu.VMEM((120, COLS), F32),
                pltpu.VMEM((120, COLS), F32),
                pltpu.VMEM((REST, 5, 16, COLS), F32),
                done,
            ],
        )
        return call(
            last_kernel,
            [whole],
            (x, hx, land, *tables[3:5], received, state, rest),
            [VMEM] * 7 + [HBM],
            [pltpu.VMEM((4, ROWS, COLS), F32), done],
            input_output_aliases={7: 0},
        )[0]

    out = lax.switch(
        turn[0],
        [functools.partial(finish, total) for total in range(LON)],
        rest_rows,
        received,
        (x, hx, land, *tables, state),
        (fold_map, inv, strip_inverse, land, rest_state, rest_coefs),
    )
    return out[None]


def solution(mesh):
    return jax.shard_map(
        body,
        mesh=mesh,
        in_specs=(
            P("comp", None, "lat", "lon"),
            P(None, "comp", None, "lat", "lon"),
            P("comp", None, None, None, "lat", "lon"),
            P("comp", None, "lat", "lon"),
            P("lat", "lon"),
            P(None, None, "lat", "lon"),
            P(None, "lat", "lon"),
            P(),
        ),
        out_specs=P("comp", None, "lat", "lon"),
        check_vma=False,
    )
```

```python
import functools

import jax
import jax.numpy as jnp
from jax import lax
from jax.experimental import pallas as pl
from jax.experimental.pallas import tpu as pltpu
from jax.sharding import PartitionSpec as P

DIFFUSE = 0.15
ROWS = 32
EXT = 48
COLS = 128
HALF = COLS // 2
BLOCKS = 8
F32 = jnp.float32
AXES = ("comp", "lat", "lon")
LAT, LON = 8, 8
VMEM = pl.BlockSpec(memory_space=pltpu.VMEM)
ANY = pl.BlockSpec(memory_space=pl.ANY)
HBM = pl.BlockSpec(memory_space=pltpu.HBM)
SMEM = pl.BlockSpec(memory_space=pltpu.SMEM)
PARAMS = pltpu.CompilerParams(vmem_limit_bytes=16 * 1024 * 1024)
FULL = pltpu.CompilerParams(vmem_limit_bytes=63 * 1024 * 1024)


def places():
    comp, lat, lon = (lax.axis_index(name) for name in AXES)
    return comp, lat, lon, lat == LAT - 1


def first_pieces():
    pieces = []
    for a in range(4):
        pieces.append((0, 0, a, 8 * a, 8))
        pieces.append((1, 0, a, 32 + 8 * a, 8))
        pieces.append((2, 0, a, 64 + 7 * a, 7))
    for b in range(4):
        pieces.append((3 + b, 0, 0, 92 + 5 * b, 5))
        for a in range(1, 4):
            pieces.append((3 + b, 0, a, 120 + 4 * (4 * (a - 1) + b), 4))
    return pieces


def rest_pieces():
    pieces = []
    for n in range(1, BLOCKS):
        at = 240 + 32 * (n - 1)
        for a in range(4):
            pieces.append((0, n, a, at + 3 * a, 3))
            pieces.append((1, n, a, at + 12 + 3 * a, 3))
            pieces.append((2, n, a, at + 24 + 2 * a, 2))
    return pieces


ROW_BUFFER = 240 + 32 * (BLOCKS - 1)
SINGLES = (
    [(0, f, 168 + 5 * f, 5) for f in range(4)]
    + [(1 + s // 4, s % 4, 188 + 4 * s, 4) for s in range(9)]
    + [(3, 1, 112, 8), (3, 2, 224, 8)]
)


def mirrored_single(quad, member):
    if quad in (1, 2) or (quad == 3 and member == 0):
        s = 8 - (4 * (quad - 1) + member)
        return 1 + s // 4, s % 4
    return quad, member


def copy_all(pairs, sem):
    copies = [pltpu.make_async_copy(a, b, sem.at[k]) for k, (a, b) in enumerate(pairs)]
    for copy in copies:
        copy.start()
    for copy in copies:
        copy.wait()


def reverse(tile):
    flip = 7 - lax.broadcasted_iota(jnp.int32, (8, COLS), 0)
    return jnp.take_along_axis(tile, flip, axis=0, mode="promise_in_bounds")


def put_piece(store, ref, at, count):
    end = ref.shape[0]
    store[0, at : at + count, :] = ref[end - count : end, :]
    store[1, at : at + count, :] = ref[0:count, :]


def put_mirrored(store, ref, at, count, sign):
    end = ref.shape[0]
    turned = reverse(ref[end - 8 : end, :])
    if sign < 0:
        turned = -turned
    store[2, at : at + count, :] = turned[0:count, :]


def field_ref(lam, winds, inv, field, n, a):
    if field == 0:
        return lam.at[4 * n + a]
    if field <= 2:
        return winds.at[2 - field, 4 * n + a]
    return inv.at[n, a, field - 3]


def sign_of(field):
    return -1 if field in (1, 2) else 1


def hand_over(store, first_out, second_out, mirror_out):
    _, lat, _, _ = places()
    odd = lat % 2
    first_out[...] = store[odd]
    second_out[...] = store[1 - odd]
    mirror_out[...] = store[2]


def start_rows_kernel(
    fold, lam_in, winds_in, inv_in, fc_in, mask_in, cell_in, weight_in,
    x_out, first_out, second_out, mirror_out, low_out, high_out, turn_out, half_turn_out,
    store, lam, winds, inv, fc, mask, cell, weight, sem,
):
    comp, lat_pos, lon_pos, _ = places()
    turn_out[0] = fold[0] // COLS
    half_turn_out[0] = fold[0] // HALF
    pairs = [(fc_in, fc), (mask_in, mask), (cell_in, cell), (weight_in, weight)]
    for half, rows in enumerate((pl.ds(0, 8), pl.ds(ROWS - 8, 8))):
        at = pl.ds(8 * half, 8)
        pairs.append((lam_in.at[:, rows], lam.at[:, at]))
        pairs.append((winds_in.at[:, :, rows], winds.at[:, :, at]))
        pairs.append((inv_in.at[pl.ds(0, 1), :, :, rows], inv.at[:, :, :, at]))
    copy_all(pairs, sem)
    wet = mask[...].astype(F32)
    x_out[3, 1] = wet
    x_out[3, 2] = jnp.where(comp == 1, wet, jnp.ones_like(wet))
    x_out[3, 3] = jnp.zeros_like(wet)
    for f in range(4):
        x_out[0, f] = fc[f]
    rows = lat_pos * ROWS + lax.broadcasted_iota(jnp.int32, (ROWS, COLS), 0)
    cols = lon_pos * COLS + lax.broadcasted_iota(jnp.int32, (ROWS, COLS), 1)
    row_shift = [cell[0, k] - rows for k in range(4)]
    col_shift = []
    for k in range(4):
        d = cell[1, k] - cols
        d = jnp.where(d > 1, d - LON * COLS, d)
        col_shift.append(jnp.where(d < -1, d + LON * COLS, d))
    code = [3 * row_shift[k] + col_shift[k] + 4 for k in range(4)]
    weights = [weight[k] for k in range(4)]
    for s in range(9):
        total = jnp.where(code[0] == s, weights[0], 0.0)
        for k in range(1, 4):
            total = total + jnp.where(code[k] == s, weights[k], 0.0)
        x_out[1 + s // 4, s % 4] = total
    pieces = [(field_ref(lam, winds, inv, f, n, a), at, count, sign_of(f)) for f, n, a, at, count in first_pieces()]
    pieces += [(field_ref(lam, winds, inv, f, n, a), at, count, sign_of(f)) for f, n, a, at, count in rest_pieces()]
    for ref, at, count, _ in pieces:
        put_piece(store, ref, at, count)
    for quad, member, at, count in SINGLES:
        put_piece(store, x_out.at[quad, member], at, count)

    @pl.when(places()[3])
    def _():
        for ref, at, count, sign in pieces:
            put_mirrored(store, ref, at, count, sign)
        for quad, member, at, count in SINGLES:
            put_mirrored(store, x_out.at[mirrored_single(quad, member)], at, count, 1)
        a, b = store[2, 0 : ROW_BUFFER // 2, :], store[2, ROW_BUFFER // 2 : ROW_BUFFER, :]
        low = lax.broadcasted_iota(jnp.int32, a.shape, 1) < HALF
        low_out[...] = jnp.where(low, a, roll_lanes(b, HALF))
        high_out[...] = jnp.where(low, roll_lanes(a, HALF), b)

    hand_over(store, first_out, second_out, mirror_out)


def lanes():
    return lax.broadcasted_iota(jnp.int32, (8, COLS), 1)


def roll_lanes(x, by):
    by = by % COLS
    return x if by == 0 else pltpu.roll(x, by, axis=1)


def roll_rows(x, by):
    by = by % x.shape[0]
    return x if by == 0 else pltpu.roll(x, by, axis=0)


def pack_columns(slots, strip_at, to_west, to_east, buffer_at, row_count):
    rows = row_count
    used = [k for k, members in enumerate(slots) if members is not None]
    zero = jnp.zeros((rows, COLS), F32)
    lane = lax.broadcasted_iota(jnp.int32, (len(used) * rows, COLS), 1)
    pair = jnp.zeros((len(used) * rows, COLS), F32)
    for a in range(4):
        values = [zero if slots[k][a] is None else slots[k][a] for k in used]
        moved = roll_lanes(jnp.concatenate(values, axis=0), 32 * a + 8)
        pair = jnp.where((lane >= 32 * a) & (lane < 32 * a + 16), moved, pair)
    strips = jnp.where(lane % 32 < 16, pair, roll_lanes(pair, 16))
    group = lax.broadcasted_iota(jnp.int32, (rows, COLS), 1) % 32
    buffers = -(-len(slots) // 4)
    west, east = [zero] * buffers, [zero] * buffers
    for i, k in enumerate(used):
        ref, at = strip_at[k]
        ref[at] = strips[i * rows : (i + 1) * rows]
        mine = pair[i * rows : (i + 1) * rows]
        buffer, slot = k // 4, k % 4
        here = (group >= 8 * slot) & (group < 8 * slot + 8)
        west[buffer] = jnp.where(here, roll_lanes(mine, 8 * slot - 8), west[buffer])
        east[buffer] = jnp.where(here, roll_lanes(mine, 8 * slot), east[buffer])
    for buffer in range(buffers):
        at = pl.ds(pl.multiple_of(rows * (buffer_at + buffer), 8), rows)
        to_west[at, :] = west[buffer]
        to_east[at, :] = east[buffer]


def block_slots(read, extra):
    slots = [[read(field, a) for a in range(4)] for field in range(3)] + [extra]
    return slots + [[read(3 + (a + d) % 4, a) for a in range(4)] for d in range(4)]


def single_slots(read):
    return [[None if q == 3 and a == 3 else read(q, a) for a in range(4)] for q in range(1, 4)]


def own_kernel(
    lam_in, winds_in, inv_in, x_in,
    own, to_west, to_east, lam0, winds0, inv0, rest_own, rest_west, rest_east,
    lam, winds, inv, x, first_sem, sem,
):
    four = pl.ds(0, 4)
    first = [(inv_in.at[pl.ds(0, 1)], inv0), (winds_in.at[:, four], winds0), (lam_in.at[four], lam0), (x_in, x)]
    first = [pltpu.make_async_copy(a, b, first_sem.at[k]) for k, (a, b) in enumerate(first)]

    def fetch(n):
        levels = pl.ds(4 * n, 4)
        pairs = ((winds_in.at[:, levels], winds.at[:, levels]), (lam_in.at[levels], lam.at[levels]), (inv_in.at[n], inv.at[n]))
        return [pltpu.make_async_copy(a, b, sem.at[n - 1, k]) for k, (a, b) in enumerate(pairs)]

    for copy in first + [copy for n in range(1, BLOCKS) for copy in fetch(n)]:
        copy.start()
    for copy in first:
        copy.wait()
    slots = block_slots(lambda field, a: field_ref(lam0, winds0, inv0, field, 0, a)[...], [x[0, f] for f in range(4)])
    slots += single_slots(lambda q, a: x[q, a])
    pack_columns(slots, [(own, k) for k in range(12)], to_west, to_east, 0, ROWS)

    def step(n, carry):
        for copy in fetch(n):
            copy.wait()

        def read(field, a):
            return field_ref(lam, winds, inv, field, n, a)[...]

        strip_at = [(rest_own, 8 * (n - 1) + k) for k in range(8)]
        pack_columns(block_slots(read, None), strip_at, rest_west, rest_east, 2 * (n - 1), ROWS)
        return carry

    lax.fori_loop(1, BLOCKS, step, 0)


def settle_rows(first_in, second_in, south, north, beyond_fold):
    _, lat, _, is_top = places()
    even = lat % 2 == 0

    @pl.when(even)
    def _():
        south[...] = second_in[...]
        north[...] = first_in[...]

    @pl.when(jnp.logical_not(even))
    def _():
        south[...] = first_in[...]

    @pl.when(jnp.logical_not(even) & jnp.logical_not(is_top))
    def _():
        north[...] = second_in[...]

    pl.when(is_top)(beyond_fold)


def pick(values, at):
    tiles = [
        jnp.take_along_axis(values[8 * t : 8 * t + 8], at, axis=1, mode="promise_in_bounds")
        for t in range(values.shape[0] // 8)
    ]
    return jnp.concatenate(tiles, axis=0)


REST = BLOCKS - 1
COL_OWN = 16 * (3 + REST)
COL_BUFFER = COL_OWN + ROWS * (3 + 2 * REST)


def halo_kernel(
    fold, first_in, second_in, fold_whole, fold_half, mid_west, mid_east, rest_west, rest_east, *refs,
):
    brought_in, (h, hx, own, rest_h, rest_own, to_west, to_east), refs = refs[:BROUGHT], refs[BROUGHT : BROUGHT + 7], refs[BROUGHT + 7 :]
    brought, (south, north) = refs[:BROUGHT], refs[BROUGHT:]
    for out, mid, rest_mid in ((to_west, mid_west, rest_west), (to_east, mid_east, rest_east)):
        out[COL_OWN : COL_OWN + 3 * ROWS, :] = mid[...]
        out[COL_OWN + 3 * ROWS : COL_BUFFER, :] = rest_mid[...]
    for source, target in zip(brought_in, brought, strict=True):
        target[...] = source[...]

    def beyond_fold():
        turn, lane = fold[0] % COLS, lanes()
        source = jnp.where(turn >= lane, turn - lane, turn - lane + COLS)
        in_half = source % HALF
        few = jnp.concatenate([pick(fold_half[...], in_half), pick(fold_half[...], in_half + HALF)], axis=0)
        many = pick(fold_whole[...], source)
        column = lax.broadcasted_iota(jnp.int32, (ROW_BUFFER, COLS), 1)
        whole_is_first = turn >= HALF
        first = (column <= turn).astype(jnp.int32)
        north[...] = jnp.where(first == whole_is_first.astype(jnp.int32), many, few)

    settle_rows(first_in, second_in, south, north, beyond_fold)
    for field, _, a, at, count in first_pieces():
        h[field, a, 8 - count : 8, :] = south[at : at + count, :]
        h[field, a, 8 : 8 + count, :] = north[at : at + count, :]
    for quad, member, at, count in SINGLES:
        hx[quad, member, 8 - count : 8, :] = south[at : at + count, :]
        hx[quad, member, 8 : 8 + count, :] = north[at : at + count, :]
    for field, n, a, at, count in rest_pieces():
        rest_h[n - 1, field, a, 8 - count : 8, :] = south[at : at + count, :]
        rest_h[n - 1, field, a, 8 : 8 + count, :] = north[at : at + count, :]
    slots = block_slots(lambda field, a: h[field, a], [hx[0, f] for f in range(4)])
    slots += single_slots(lambda q, a: hx[q, a]) + [None]
    strip_at = [(own, k) for k in range(11)] + [None]
    for n in range(REST):
        slots += [[rest_h[n, field, a] for a in range(4)] for field in range(3)] + [None]
        strip_at += [(rest_own, 3 * n + k) for k in range(3)] + [None]
    pack_columns(slots, strip_at, to_west, to_east, 0, 16)


BROUGHT = 5


def ext_lanes():
    return lax.broadcasted_iota(jnp.int32, (EXT, COLS), 1)


def barrier_masks():
    comp, _, _, is_top = places()
    row = lax.broadcasted_iota(jnp.int32, (EXT, COLS), 0)
    apart = is_top & (comp == 0)
    keep_c = jnp.where(apart & (row == 40), 0.0, 1.0).astype(F32)
    keep_d = jnp.where(apart & (row == 39), 0.0, 1.0).astype(F32)
    return stack([keep_c] * 5), stack([keep_d] * 5)


def edges_of(slot, west, east):
    group = lax.broadcasted_iota(jnp.int32, west.shape, 1) % 32
    edge = jnp.where(group < 8, roll_lanes(west, -8 * slot), roll_lanes(east, 24 - 8 * slot))
    return edge, (group >= 8) & (group < 24)


def assemble_strip(slot, sides, buffer, mid, halo_buffer=None, halo=None):
    rows = pl.ds(pl.multiple_of(COL_OWN + ROWS * buffer, 8), ROWS)
    edge, inner = edges_of(slot, sides[0][rows, :], sides[1][rows, :])
    middle = jnp.where(inner, mid, edge)
    if halo is None:
        return middle
    rows = pl.ds(pl.multiple_of(16 * halo_buffer, 8), 16)
    edge, inner = edges_of(slot, sides[0][rows, :], sides[1][rows, :])
    outer = jnp.where(inner, halo, edge)
    return jnp.concatenate([outer[0:8], middle, outer[8:16]], axis=0)


class First:
    def __init__(self, lam, winds, inv, h, own, own_halo, from_west, from_east, x_in, hx):
        self.lam, self.winds, self.inv, self.h = lam, winds, inv, h
        self.own, self.own_halo, self.sides = own, own_halo, (from_west, from_east)
        self.x_in, self.hx = x_in, hx

    def main(self, field, n, a):
        halo = self.h[field, a]
        mid = field_ref(self.lam, self.winds, self.inv, field, 0, a)[...]
        return jnp.concatenate([halo[0:8], mid, halo[8:16]], axis=0)

    def single(self, quad, a):
        halo = self.hx[quad, a]
        return jnp.concatenate([halo[0:8], self.x_in[quad, a], halo[8:16]], axis=0)

    def strip(self, n, which, slot):
        at = 4 * which + slot
        return assemble_strip(slot, self.sides, which, self.own[at], which, self.own_halo[at])

    def single_strip(self, quad):
        return self.strip(0, 0, 3) if quad == 0 else self.strip(0, 2, quad - 1)


class Rest:
    def __init__(self, lam, winds, inv, h, own, own_halo, from_west, from_east):
        self.lam, self.winds, self.inv, self.h = lam, winds, inv, h
        self.own, self.own_halo, self.sides = own, own_halo, (from_west, from_east)

    def main(self, field, n, a):
        mid = field_ref(self.lam, self.winds, self.inv, field, n, a)[...]
        if field >= 3:
            return mid
        halo = self.h[n - 1, field, a]
        return jnp.concatenate([halo[0:8], mid, halo[8:16]], axis=0)

    def strip(self, n, which, slot):
        mid = self.own[8 * (n - 1) + 4 * which + slot]
        buffer = 3 + 2 * (n - 1) + which
        if which == 1:
            return assemble_strip(slot, self.sides, buffer, mid)
        return assemble_strip(slot, self.sides, buffer, mid, 2 + n, self.own_halo[3 * (n - 1) + slot])


def stack(values):
    return jnp.concatenate(values, axis=0)


def unstack(value):
    return [value[EXT * k : EXT * (k + 1)] for k in range(value.shape[0] // EXT)]


def replicate(strip, a):
    lane = ext_lanes()
    out = roll_lanes(strip, -32 * a)
    base = jnp.where(lane < 32, out, 0.0)
    for g in range(1, 4):
        base = jnp.where((lane >= 32 * g) & (lane < 32 * g + 32), roll_lanes(out, 32 * g), base)
    return base


def advect(tracer, coefs, land):
    to_south, to_north, to_west = coefs
    for _ in range(3):
        a = to_west[...] * tracer
        b = (2 * DIFFUSE) * tracer - a
        east, west = roll_lanes(a, -1), roll_lanes(b, 1)
        new = (1.0 - 4 * DIFFUSE) * tracer
        new = new + roll_rows(to_south[...] * tracer, -1) + roll_rows(to_north[...] * tracer, 1)
        tracer = (new + (east + west)) * land[...]
    return tracer


def coefficients(fields, n, masks):
    merid = stack([fields.main(1, n, a) for a in range(4)] + [fields.strip(n, 0, 1)])
    zonal = stack([fields.main(2, n, a) for a in range(4)] + [fields.strip(n, 0, 2)])
    to_south = (DIFFUSE + 0.5 * merid) * masks[0]
    to_north = (DIFFUSE - 0.5 * merid) * masks[1]
    return to_south, to_north, DIFFUSE + 0.5 * zonal


def solve(inverse, strip_inverse, old):
    moved = [old[4]] + [roll_lanes(old[4], -32 * d) for d in range(1, 4)]
    new = []
    for a in range(4):
        total = inverse(a, 0) * old[0]
        for b in range(1, 4):
            total = total + inverse(a, b) * old[b]
        new.append(total)
    total = strip_inverse(0) * moved[0]
    for d in range(1, 4):
        total = total + strip_inverse(d) * moved[d]
    return new + [total]


def solve_first(inverse, strip_inverse, tracer):
    return solve(lambda a, b: inverse[4 * a + b], lambda d: strip_inverse[d], unstack(tracer))


def main_from_strip(main, strip, a, width):
    lane = lax.broadcasted_iota(jnp.int32, main.shape, 1)
    main = jnp.where(lane < width, roll_lanes(strip, -(32 * a + 8)), main)
    return jnp.where(lane >= COLS - width, roll_lanes(strip, 104 - 32 * a), main)


def merge(state):
    strip = state[4]
    lane = lax.broadcasted_iota(jnp.int32, strip.shape, 1)
    new_strip = strip
    mains = [main_from_strip(state[a], strip, a, 3) for a in range(4)]
    for a in range(4):
        west = (lane >= 32 * a + 11) & (lane < 32 * a + 16)
        east = (lane >= 32 * a + 16) & (lane < 32 * a + 21)
        new_strip = jnp.where(west, roll_lanes(state[a], 32 * a + 8), new_strip)
        new_strip = jnp.where(east, roll_lanes(state[a], 32 * a + 24), new_strip)
    return mains + [new_strip]


def load_block(fields, n):
    return [fields.main(0, n, a) for a in range(4)] + [fields.strip(n, 0, 0)]


def fluxes_out(fields, state, payload, strips):
    surface = state[0] * fields.single(3, 1)
    for f in range(4):
        payload[f] = fields.single(0, f) * surface
    payload[4] = strips[0] * replicate(state[4] * strips[1], 0)


def couple(fields, received, strip_coefs, strip_weights, land_strip):
    sources = [received[f] for f in range(4)] + [roll_lanes(received[4], -32 * f) for f in range(4)]
    coefs = [fields.single(0, f) for f in range(4)] + [strip_coefs[f] for f in range(4)]
    weights = [fields.single(1 + s // 4, s % 4) for s in range(9)]
    moved = {dc: [roll_lanes(source, -dc) for source in sources] for dc in (-1, 0, 1)}
    totals = []
    for table, parts in ((weights, range(4)), ([strip_weights[s] for s in range(9)], range(4, 8))):
        total = None
        for k in parts:
            part = None
            for dr in (-1, 0, 1):
                across = None
                for dc in (-1, 0, 1):
                    term = table[3 * (dr + 1) + dc + 1] * roll_rows(moved[dc][k], -dr)
                    across = term if across is None else across + term
                part = across if part is None else part + across
            total = coefs[k] * part if total is None else total + coefs[k] * part
        totals.append(total)
    return totals[0] * fields.single(3, 2), totals[1] * land_strip


INPUTS = 8


def first_kernel(*refs):
    fields = First(*refs[: INPUTS + 2])
    payload, state, land, to_south, to_north, to_west, strip_coefs, strip_weights = refs[INPUTS + 2 : INPUTS + 10]
    inverse, strip_inverse, flux_strips = refs[INPUTS + 10 :]
    quads = [fields.single_strip(q) for q in range(4)]
    main_land = fields.single(3, 2)
    land[...] = stack([main_land] * 4 + [replicate(quads[3], 2)])
    coefs = (to_south, to_north, to_west)
    for ref, value in zip(coefs, coefficients(fields, 0, barrier_masks()), strict=True):
        ref[...] = value
    tracer = advect(stack(load_block(fields, 0)), coefs, land)
    for a in range(4):
        for b in range(4):
            inverse[4 * a + b] = fields.main(3 + b, 0, a)
        strip_inverse[a] = fields.strip(0, 1, a)
    flux_strips[0] = quads[0]
    flux_strips[1] = roll_lanes(quads[3], -32)
    merged = merge(solve_first(inverse, strip_inverse, tracer))
    for a in range(5):
        state[a] = merged[a]
    fluxes_out(fields, merged, payload, flux_strips)
    for f in range(4):
        strip_coefs[f] = roll_lanes(quads[0], -32 * f)
    for k in range(9):
        strip_weights[k] = roll_lanes(quads[1 + k // 4], -32 * (k % 4))


def own_rows(tracer):
    return [value[8:40] for value in unstack(tracer)]


def rest_first_kernel(*refs):
    fields = Rest(*refs[:INPUTS])
    land, state, coefs, strip_inverse, first_out, second_out, mirror_out, edges, store, mask_c, mask_d = refs[INPUTS:]
    mask_c[...], mask_d[...] = barrier_masks()

    def block(n, carry):
        mine = tuple(coefs.at[n - 1, k] for k in range(3))
        for ref, value in zip(mine, coefficients(fields, n, (mask_c[...], mask_d[...])), strict=True):
            ref[...] = value
        tracer = advect(stack(load_block(fields, n)), mine, land)
        for d in range(4):
            strip_inverse[n - 1, d] = fields.strip(n, 1, d)
        merged = merge(
            solve(lambda a, b: fields.main(3 + b, n, a), lambda d: strip_inverse[n - 1, d], own_rows(tracer))
        )
        for a in range(5):
            state[n - 1, a] = merged[a]
            edges[0, n - 1, a] = merged[a][24:32]
            edges[1, n - 1, a] = merged[a][0:8]
            edges[2, n - 1, a] = reverse(merged[a][24:32])
        return carry

    lax.fori_loop(1, BLOCKS, block, 0, unroll=True)
    for n in range(REST):
        for a in range(5):
            at = 24 * a + 3 * n
            store[0, at : at + 3, :] = edges[0, n, a, 5:8, :]
            store[1, at : at + 3, :] = edges[1, n, a, 0:3, :]
            store[2, at : at + 3, :] = edges[2, n, a, 0:3, :]
    for k in range(3):
        for a in range(5):
            store[k, 24 * a + 21 : 24 * a + 24, :] = jnp.zeros((3, COLS), F32)
    hand_over(store, first_out, second_out, mirror_out)


def rest_second_kernel(*refs):
    fold, inv, strip_inverse, land, state, coefs, first_in, second_in, fold_a, fold_b = refs[:10]
    out, result, south, north, halo, sem = refs[10:]

    def beyond_fold():
        turn, lane = fold[0] % COLS, lanes()
        source = jnp.where(turn >= lane, turn - lane, turn - lane + COLS)
        keep = lax.broadcasted_iota(jnp.int32, (24, COLS), 1) <= turn
        group, in_group = lane // 32, lane % 32
        column = jnp.where(in_group < 16, in_group - 8, in_group + 104)
        at_a = turn - column
        at_b = at_a + COLS
        main_a, main_b = jnp.clip(at_a, 0, COLS - 1), jnp.clip(at_b, 0, COLS - 1)
        strip_a = 32 * group + jnp.clip(at_a - 104, 0, 31)
        strip_b = 32 * group + jnp.clip(at_b + 8, 0, 31)
        wide_a = stack([at_a] * 3)
        wide_b = stack([at_b] * 3)
        wide_group = stack([group] * 3)
        strip = jnp.where(wide_a >= COLS, pick(fold_a[96:120, :], strip_a), pick(fold_b[96:120, :], strip_b))
        for a in range(4):
            values_a, values_b = fold_a[24 * a : 24 * a + 24, :], fold_b[24 * a : 24 * a + 24, :]
            north[24 * a : 24 * a + 24, :] = jnp.where(keep, pick(values_a, source), pick(values_b, source))
            inside = (wide_group == a) & (wide_a < COLS) & (wide_b >= 0)
            strip = jnp.where(inside, jnp.where(wide_a >= 0, pick(values_a, main_a), pick(values_b, main_b)), strip)
        north[96:120, :] = strip

    settle_rows(first_in, second_in, south, north, beyond_fold)
    for n in range(REST):
        for a in range(5):
            at = 24 * a + 3 * n
            halo[n, a, 5:8, :] = south[at : at + 3, :]
            halo[n, a, 8:11, :] = north[at : at + 3, :]

    def leave(n):
        return pltpu.make_async_copy(result.at[pl.ds(4 * (n - 1), 4)], out.at[pl.ds(4 * n, 4)], sem.at[n - 1])

    def block(n, carry):
        mine = tuple(coefs.at[n - 1, k] for k in range(3))
        parts = []
        for a in range(5):
            edge = halo[n - 1, a]
            parts += [edge[0:8], state[n - 1, a], edge[8:16]]
        tracer = advect(stack(parts), mine, land)
        solved = solve(lambda a, b: inv[n, a, b], lambda d: strip_inverse[n - 1, d], own_rows(tracer))
        for a in range(4):
            result[4 * (n - 1) + a] = main_from_strip(solved[a], solved[4], a, 3)
        leave(n).start()
        return carry

    lax.fori_loop(1, BLOCKS, block, 0)
    for n in range(1, BLOCKS):
        leave(n).wait()


def second_kernel(
    x_in, hx, land, to_south, to_north, to_west, strip_coefs, strip_weights, inverse, strip_inverse, flux_strips,
    received, state_in, payload, state,
):
    fields = First(*[None] * 8, x_in, hx)
    added, added_strip = couple(fields, received, strip_coefs, strip_weights, land[4 * EXT :])
    lane = ext_lanes()
    strip = state_in[4] + jnp.where(lane < 32, added_strip, 0.0)
    top = main_from_strip(state_in[0] + added, strip, 0, 1)
    tracer = stack([top] + [state_in[a] for a in range(1, 4)] + [strip])
    solved = solve_first(inverse, strip_inverse, advect(tracer, (to_south, to_north, to_west), land))
    merged = [main_from_strip(solved[a], solved[4], a, 3) for a in range(4)] + [solved[4]]
    for a in range(5):
        state[a] = merged[a]
    fluxes_out(fields, merged, payload, flux_strips)


def last_kernel(x_in, hx, land, strip_coefs, strip_weights, received, state, rest, out, result, sem):
    del rest
    fields = First(*[None] * 8, x_in, hx)
    added, added_strip = couple(fields, received, strip_coefs, strip_weights, land[4 * EXT :])
    strip = state[4] + added_strip
    result[0] = main_from_strip(state[0] + added, strip, 0, 1)[8:40]
    for a in range(1, 4):
        result[a] = state[a][8:40]
    copy_all([(result, out.at[pl.ds(0, 4)])], sem)


MICROSECONDS = {
    "start_rows_kernel": 3.2,
    "own_kernel": 4.0,
    "halo_kernel": 2.8,
    "first_kernel": 1.0,
    "rest_first_kernel": 4.3,
    "second_kernel": 1.0,
    "last_kernel": 0.5,
    "rest_second_kernel": 4.6,
}


def call(kernel, outs, args, specs, scratch=(), params=PARAMS, **more):
    cost = int(MICROSECONDS[kernel.__name__] * 3.5e6)
    return pl.pallas_call(
        kernel,
        out_shape=[jax.ShapeDtypeStruct(s, jnp.int32 if spec is SMEM else F32) for s, spec in outs],
        in_specs=specs,
        out_specs=[spec for _, spec in outs],
        scratch_shapes=list(scratch),
        compiler_params=params,
        cost_estimate=pl.CostEstimate(flops=0, bytes_accessed=cost, transcendentals=0),
        **more,
    )(*args)


def index(c, a, o):
    return (c * LAT + a) * LON + o % LON


def lon_pairs(do):
    return [(index(c, a, o), index(c, a, o + do)) for c in range(2) for a in range(LAT) for o in range(LON)]


def swap_pairs(start):
    pairs = []
    for c in range(2):
        for a in range(start, LAT - 1, 2):
            for o in range(LON):
                pairs += [(index(c, a, o), index(c, a + 1, o)), (index(c, a + 1, o), index(c, a, o))]
    return pairs


def fold_pairs(total, comps):
    return [(index(c, LAT - 1, o), index(c, LAT - 1, total - o)) for c in comps for o in range(LON)]


def body(
    adjoint_state,
    winds,
    block_inverse,
    flux_coef,
    sea_mask,
    intersection_cell,
    intersection_weight,
    fold_map,
):
    lam = adjoint_state[0]
    wind = winds[:, 0]
    inv = block_inverse[0]
    rows = (ROW_BUFFER, COLS)
    x, first, second, mirror, low, high, turn, half_turn = call(
        start_rows_kernel,
        [((4, 4, ROWS, COLS), VMEM)] + [(rows, VMEM)] * 3 + [((ROW_BUFFER // 2, COLS), VMEM)] * 2 + [((1,), SMEM)] * 2,
        (fold_map, lam, wind, inv, flux_coef[0], sea_mask, intersection_cell, intersection_weight),
        [SMEM] + [HBM] * 7,
        [
            pltpu.VMEM((3, *rows), F32),
            pltpu.VMEM((32, 16, COLS), F32),
            pltpu.VMEM((2, 32, 16, COLS), F32),
            pltpu.VMEM((1, 4, 4, 16, COLS), F32),
            pltpu.VMEM((4, ROWS, COLS), F32),
            pltpu.VMEM((ROWS, COLS), jnp.int32),
            pltpu.VMEM((2, 4, ROWS, COLS), jnp.int32),
            pltpu.VMEM((4, ROWS, COLS), F32),
            pltpu.SemaphoreType.DMA((10,)),
        ],
        FULL,
    )
    def swap(first, second):
        return lax.ppermute(first, AXES, swap_pairs(0)), lax.ppermute(second, AXES, swap_pairs(1))

    def around(to_west, to_east):
        return lax.ppermute(to_east, AXES, lon_pairs(1)), lax.ppermute(to_west, AXES, lon_pairs(-1))

    def across(value):
        return lax.ppermute(value, AXES, [(i, (i + LAT * LON) % (2 * LAT * LON)) for i in range(2 * LAT * LON)])

    def vmem(*shape):
        return ((*shape, COLS), VMEM)

    state_in = (lam, wind, inv)
    swapped = swap(first, second)

    def across_fold(step, mirror, low, high, lam, wind, inv, x):
        total, in_late_half = step // 2, step % 2
        whole = lax.ppermute(mirror, AXES, fold_pairs(total - 1 + in_late_half, (0, 1)))
        half = lax.ppermute(high if in_late_half else low, AXES, fold_pairs(total - in_late_half, (0, 1)))
        folded = (whole, half)
        own = call(
            own_kernel,
            [vmem(12, ROWS), vmem(3 * ROWS), vmem(3 * ROWS)]
            + [vmem(4, ROWS), vmem(2, 4, ROWS), vmem(1, 4, 4, ROWS)]
            + [vmem(8 * REST, ROWS), vmem(2 * REST * ROWS), vmem(2 * REST * ROWS)],
            (lam, wind, inv, x),
            [HBM] * 4,
            [
                pltpu.VMEM((32, ROWS, COLS), F32),
                pltpu.VMEM((2, 32, ROWS, COLS), F32),
                pltpu.VMEM((BLOCKS, 4, 4, ROWS, COLS), F32),
                pltpu.VMEM((4, 4, ROWS, COLS), F32),
                pltpu.SemaphoreType.DMA((4,)),
                pltpu.SemaphoreType.DMA((REST, 3)),
            ],
        )
        return *folded, *own

    *folded, own, mid_west, mid_east, lam0, wind0, inv0, rest_own, rest_mid_west, rest_mid_east = lax.switch(
        half_turn[0], [functools.partial(across_fold, step) for step in range(2 * LON)], mirror, low, high, lam, wind, inv, x
    )
    moved = (*swapped, *folded)
    brought = (own, lam0, wind0, inv0, rest_own)
    h, hx, own_halo, rest_h, rest_own_halo, to_west, to_east, own, lam0, wind0, inv0, rest_own = call(
        halo_kernel,
        [vmem(7, 4, 16), vmem(4, 4, 16), vmem(12, 16), vmem(REST, 3, 4, 16), vmem(3 * REST, 16)]
        + [vmem(COL_BUFFER)] * 2
        + [(value.shape, VMEM) for value in brought],
        (fold_map, *moved, mid_west, mid_east, rest_mid_west, rest_mid_east, *brought),
        [SMEM] + [VMEM] * (8 + BROUGHT),
        [pltpu.VMEM((ROW_BUFFER, COLS), F32)] * 2,
    )
    from_sides = around(to_west, to_east)
    five = vmem(5, EXT)
    tall = vmem(5 * EXT)
    payload, state, land, *tables = call(
        first_kernel,
        [five, five] + [tall] * 4 + [vmem(k, EXT) for k in (4, 9, 16, 4, 2)],
        (lam0, wind0, inv0, h, own, own_halo, *from_sides, x, hx),
        [VMEM] * (INPUTS + 2),
    )
    received = across(payload)
    rest_args = (*state_in, rest_h, rest_own, rest_own_halo, *from_sides)
    whole = ((32, ROWS, COLS), HBM)
    done = pltpu.SemaphoreType.DMA((1,))
    rest_state, rest_coefs, strip_inverse, *rest_rows = call(
        rest_first_kernel,
        [vmem(REST, 5, ROWS), vmem(REST, 3, 5 * EXT), vmem(REST, 4, ROWS)] + [vmem(120)] * 3,
        (*rest_args, land),
        [VMEM] * (INPUTS + 1),
        [pltpu.VMEM((3, REST, 5, 8, COLS), F32), pltpu.VMEM((3, 120, COLS), F32)]
        + [pltpu.VMEM((5 * EXT, COLS), F32)] * 2,
    )
    def finish(total, rest_rows, received, chain, rest_args):
        folded = [lax.ppermute(rest_rows[2], AXES, fold_pairs(total - k, (1,))) for k in range(2)]
        swapped = swap(*rest_rows[:2])
        x, hx, land, *tables, state = chain
        payload, state = call(second_kernel, [five, five], (x, hx, land, *tables, received, state), [VMEM] * 13)
        payload, swapped, folded = lax.optimization_barrier((payload, swapped, folded))
        received = across(payload)
        (rest,) = call(
            rest_second_kernel,
            [whole],
            (*rest_args, *swapped, *folded),
            [SMEM] + [VMEM] * 9,
            [
                pltpu.VMEM((4 * REST, ROWS, COLS), F32),
                pltpu.VMEM((120, COLS), F32),
                pltpu.VMEM((120, COLS), F32),
                pltpu.VMEM((REST, 5, 16, COLS), F32),
                pltpu.SemaphoreType.DMA((REST,)),
            ],
        )
        return call(
            last_kernel,
            [whole],
            (x, hx, land, *tables[3:5], received, state, rest),
            [VMEM] * 7 + [HBM],
            [pltpu.VMEM((4, ROWS, COLS), F32), done],
            input_output_aliases={7: 0},
        )[0]

    out = lax.switch(
        turn[0],
        [functools.partial(finish, total) for total in range(LON)],
        rest_rows,
        received,
        (x, hx, land, *tables, state),
        (fold_map, inv, strip_inverse, land, rest_state, rest_coefs),
    )
    return out[None]


def solution(mesh):
    return jax.shard_map(
        body,
        mesh=mesh,
        in_specs=(
            P("comp", None, "lat", "lon"),
            P(None, "comp", None, "lat", "lon"),
            P("comp", None, None, None, "lat", "lon"),
            P("comp", None, "lat", "lon"),
            P("lat", "lon"),
            P(None, None, "lat", "lon"),
            P(None, "lat", "lon"),
            P(),
        ),
        out_specs=P("comp", None, "lat", "lon"),
        check_vma=False,
    )
```

```python
import functools

import jax
import jax.numpy as jnp
from jax import lax
from jax.experimental import pallas as pl
from jax.experimental.pallas import tpu as pltpu
from jax.sharding import PartitionSpec as P

DIFFUSE = 0.15
ROWS = 32
EXT = 48
COLS = 128
HALF = COLS // 2
BLOCKS = 8
F32 = jnp.float32
AXES = ("comp", "lat", "lon")
LAT, LON = 8, 8
VMEM = pl.BlockSpec(memory_space=pltpu.VMEM)
ANY = pl.BlockSpec(memory_space=pl.ANY)
HBM = pl.BlockSpec(memory_space=pltpu.HBM)
SMEM = pl.BlockSpec(memory_space=pltpu.SMEM)
PARAMS = pltpu.CompilerParams(vmem_limit_bytes=16 * 1024 * 1024)
FULL = pltpu.CompilerParams(vmem_limit_bytes=63 * 1024 * 1024)


def places():
    comp, lat, lon = (lax.axis_index(name) for name in AXES)
    return comp, lat, lon, lat == LAT - 1


def first_pieces():
    pieces = []
    for a in range(4):
        pieces.append((0, 0, a, 8 * a, 8))
        pieces.append((1, 0, a, 32 + 8 * a, 8))
        pieces.append((2, 0, a, 64 + 7 * a, 7))
    for b in range(4):
        pieces.append((3 + b, 0, 0, 92 + 5 * b, 5))
        for a in range(1, 4):
            pieces.append((3 + b, 0, a, 120 + 4 * (4 * (a - 1) + b), 4))
    return pieces


def rest_pieces():
    pieces = []
    for n in range(1, BLOCKS):
        at = 240 + 32 * (n - 1)
        for a in range(4):
            pieces.append((0, n, a, at + 3 * a, 3))
            pieces.append((1, n, a, at + 12 + 3 * a, 3))
            pieces.append((2, n, a, at + 24 + 2 * a, 2))
    return pieces


ROW_BUFFER = 240 + 32 * (BLOCKS - 1)
SINGLES = (
    [(0, f, 168 + 5 * f, 5) for f in range(4)]
    + [(1 + s // 4, s % 4, 188 + 4 * s, 4) for s in range(9)]
    + [(3, 1, 112, 8), (3, 2, 224, 8)]
)


def mirrored_single(quad, member):
    if quad in (1, 2) or (quad == 3 and member == 0):
        s = 8 - (4 * (quad - 1) + member)
        return 1 + s // 4, s % 4
    return quad, member


def copy_all(pairs, sem):
    copies = [pltpu.make_async_copy(a, b, sem.at[k]) for k, (a, b) in enumerate(pairs)]
    for copy in copies:
        copy.start()
    for copy in copies:
        copy.wait()


def reverse(tile):
    flip = 7 - lax.broadcasted_iota(jnp.int32, (8, COLS), 0)
    return jnp.take_along_axis(tile, flip, axis=0, mode="promise_in_bounds")


def put_piece(store, ref, at, count):
    end = ref.shape[0]
    store[0, at : at + count, :] = ref[end - count : end, :]
    store[1, at : at + count, :] = ref[0:count, :]


def put_mirrored(store, ref, at, count, sign):
    end = ref.shape[0]
    turned = reverse(ref[end - 8 : end, :])
    if sign < 0:
        turned = -turned
    store[2, at : at + count, :] = turned[0:count, :]


def field_ref(lam, winds, inv, field, n, a):
    if field == 0:
        return lam.at[4 * n + a]
    if field <= 2:
        return winds.at[2 - field, 4 * n + a]
    return inv.at[n, a, field - 3]


def sign_of(field):
    return -1 if field in (1, 2) else 1


def hand_over(store, first_out, second_out, mirror_out):
    _, lat, _, _ = places()
    odd = lat % 2
    first_out[...] = store[odd]
    second_out[...] = store[1 - odd]
    mirror_out[...] = store[2]


def start_rows_kernel(
    fold, lam_in, winds_in, inv_in, fc_in, mask_in, cell_in, weight_in,
    x_out, first_out, second_out, mirror_out, low_out, high_out, turn_out, half_turn_out,
    store, lam, winds, inv, fc, mask, cell, weight, sem,
):
    comp, lat_pos, lon_pos, _ = places()
    turn_out[0] = fold[0] // COLS
    half_turn_out[0] = fold[0] // HALF
    pairs = [(fc_in, fc), (mask_in, mask), (cell_in, cell), (weight_in, weight)]
    for half, rows in enumerate((pl.ds(0, 8), pl.ds(ROWS - 8, 8))):
        at = pl.ds(8 * half, 8)
        pairs.append((lam_in.at[:, rows], lam.at[:, at]))
        pairs.append((winds_in.at[:, :, rows], winds.at[:, :, at]))
        pairs.append((inv_in.at[pl.ds(0, 1), :, :, rows], inv.at[:, :, :, at]))
    copy_all(pairs, sem)
    wet = mask[...].astype(F32)
    x_out[3, 1] = wet
    x_out[3, 2] = jnp.where(comp == 1, wet, jnp.ones_like(wet))
    x_out[3, 3] = jnp.zeros_like(wet)
    for f in range(4):
        x_out[0, f] = fc[f]
    rows = lat_pos * ROWS + lax.broadcasted_iota(jnp.int32, (ROWS, COLS), 0)
    cols = lon_pos * COLS + lax.broadcasted_iota(jnp.int32, (ROWS, COLS), 1)
    row_shift = [cell[0, k] - rows for k in range(4)]
    col_shift = []
    for k in range(4):
        d = cell[1, k] - cols
        d = jnp.where(d > 1, d - LON * COLS, d)
        col_shift.append(jnp.where(d < -1, d + LON * COLS, d))
    code = [3 * row_shift[k] + col_shift[k] + 4 for k in range(4)]
    weights = [weight[k] for k in range(4)]
    for s in range(9):
        total = jnp.where(code[0] == s, weights[0], 0.0)
        for k in range(1, 4):
            total = total + jnp.where(code[k] == s, weights[k], 0.0)
        x_out[1 + s // 4, s % 4] = total
    pieces = [(field_ref(lam, winds, inv, f, n, a), at, count, sign_of(f)) for f, n, a, at, count in first_pieces()]
    pieces += [(field_ref(lam, winds, inv, f, n, a), at, count, sign_of(f)) for f, n, a, at, count in rest_pieces()]
    for ref, at, count, _ in pieces:
        put_piece(store, ref, at, count)
    for quad, member, at, count in SINGLES:
        put_piece(store, x_out.at[quad, member], at, count)

    @pl.when(places()[3])
    def _():
        for ref, at, count, sign in pieces:
            put_mirrored(store, ref, at, count, sign)
        for quad, member, at, count in SINGLES:
            put_mirrored(store, x_out.at[mirrored_single(quad, member)], at, count, 1)
        a, b = store[2, 0 : ROW_BUFFER // 2, :], store[2, ROW_BUFFER // 2 : ROW_BUFFER, :]
        low = lax.broadcasted_iota(jnp.int32, a.shape, 1) < HALF
        low_out[...] = jnp.where(low, a, roll_lanes(b, HALF))
        high_out[...] = jnp.where(low, roll_lanes(a, HALF), b)

    hand_over(store, first_out, second_out, mirror_out)


def lanes():
    return lax.broadcasted_iota(jnp.int32, (8, COLS), 1)


def roll_lanes(x, by):
    by = by % COLS
    return x if by == 0 else pltpu.roll(x, by, axis=1)


def roll_rows(x, by):
    by = by % x.shape[0]
    return x if by == 0 else pltpu.roll(x, by, axis=0)


def pack_columns(slots, strip_at, to_west, to_east, buffer_at, row_count):
    rows = row_count
    used = [k for k, members in enumerate(slots) if members is not None]
    zero = jnp.zeros((rows, COLS), F32)
    lane = lax.broadcasted_iota(jnp.int32, (len(used) * rows, COLS), 1)
    pair = jnp.zeros((len(used) * rows, COLS), F32)
    for a in range(4):
        values = [zero if slots[k][a] is None else slots[k][a] for k in used]
        moved = roll_lanes(jnp.concatenate(values, axis=0), 32 * a + 8)
        pair = jnp.where((lane >= 32 * a) & (lane < 32 * a + 16), moved, pair)
    strips = jnp.where(lane % 32 < 16, pair, roll_lanes(pair, 16))
    group = lax.broadcasted_iota(jnp.int32, (rows, COLS), 1) % 32
    buffers = -(-len(slots) // 4)
    west, east = [zero] * buffers, [zero] * buffers
    for i, k in enumerate(used):
        ref, at = strip_at[k]
        ref[at] = strips[i * rows : (i + 1) * rows]
        mine = pair[i * rows : (i + 1) * rows]
        buffer, slot = k // 4, k % 4
        here = (group >= 8 * slot) & (group < 8 * slot + 8)
        west[buffer] = jnp.where(here, roll_lanes(mine, 8 * slot - 8), west[buffer])
        east[buffer] = jnp.where(here, roll_lanes(mine, 8 * slot), east[buffer])
    for buffer in range(buffers):
        at = pl.ds(pl.multiple_of(rows * (buffer_at + buffer), 8), rows)
        to_west[at, :] = west[buffer]
        to_east[at, :] = east[buffer]


def block_slots(read, extra):
    slots = [[read(field, a) for a in range(4)] for field in range(3)] + [extra]
    return slots + [[read(3 + (a + d) % 4, a) for a in range(4)] for d in range(4)]


def single_slots(read):
    return [[None if q == 3 and a == 3 else read(q, a) for a in range(4)] for q in range(1, 4)]


def own_kernel(
    lam_in, winds_in, inv_in, x_in,
    own, to_west, to_east, lam0, winds0, inv0, rest_own, rest_west, rest_east,
    lam, winds, inv, x, first_sem, sem,
):
    four = pl.ds(0, 4)
    first = [(inv_in.at[pl.ds(0, 1)], inv0), (winds_in.at[:, four], winds0), (lam_in.at[four], lam0), (x_in, x)]
    first = [pltpu.make_async_copy(a, b, first_sem.at[k]) for k, (a, b) in enumerate(first)]

    def fetch(n):
        levels = pl.ds(4 * n, 4)
        pairs = ((winds_in.at[:, levels], winds.at[:, levels]), (lam_in.at[levels], lam.at[levels]), (inv_in.at[n], inv.at[n]))
        return [pltpu.make_async_copy(a, b, sem.at[n - 1, k]) for k, (a, b) in enumerate(pairs)]

    for copy in first + [copy for n in range(1, BLOCKS) for copy in fetch(n)]:
        copy.start()
    for copy in first:
        copy.wait()
    slots = block_slots(lambda field, a: field_ref(lam0, winds0, inv0, field, 0, a)[...], [x[0, f] for f in range(4)])
    slots += single_slots(lambda q, a: x[q, a])
    pack_columns(slots, [(own, k) for k in range(12)], to_west, to_east, 0, ROWS)

    def step(n, carry):
        for copy in fetch(n):
            copy.wait()

        def read(field, a):
            return field_ref(lam, winds, inv, field, n, a)[...]

        strip_at = [(rest_own, 8 * (n - 1) + k) for k in range(8)]
        pack_columns(block_slots(read, None), strip_at, rest_west, rest_east, 2 * (n - 1), ROWS)
        return carry

    lax.fori_loop(1, BLOCKS, step, 0)


def settle_rows(first_in, second_in, south, north, beyond_fold):
    _, lat, _, is_top = places()
    even = lat % 2 == 0

    @pl.when(even)
    def _():
        south[...] = second_in[...]
        north[...] = first_in[...]

    @pl.when(jnp.logical_not(even))
    def _():
        south[...] = first_in[...]

    @pl.when(jnp.logical_not(even) & jnp.logical_not(is_top))
    def _():
        north[...] = second_in[...]

    pl.when(is_top)(beyond_fold)


def pick(values, at):
    tiles = [
        jnp.take_along_axis(values[8 * t : 8 * t + 8], at, axis=1, mode="promise_in_bounds")
        for t in range(values.shape[0] // 8)
    ]
    return jnp.concatenate(tiles, axis=0)


REST = BLOCKS - 1
COL_OWN = 16 * (3 + REST)
COL_BUFFER = COL_OWN + ROWS * (3 + 2 * REST)


def halo_kernel(
    fold, first_in, second_in, fold_whole, fold_half, mid_west, mid_east, rest_west, rest_east, *refs,
):
    brought_in, (h, hx, own, rest_h, rest_own, to_west, to_east), refs = refs[:BROUGHT], refs[BROUGHT : BROUGHT + 7], refs[BROUGHT + 7 :]
    brought, (south, north) = refs[:BROUGHT], refs[BROUGHT:]
    for out, mid, rest_mid in ((to_west, mid_west, rest_west), (to_east, mid_east, rest_east)):
        out[COL_OWN : COL_OWN + 3 * ROWS, :] = mid[...]
        out[COL_OWN + 3 * ROWS : COL_BUFFER, :] = rest_mid[...]
    for source, target in zip(brought_in, brought, strict=True):
        target[...] = source[...]

    def beyond_fold():
        turn, lane = fold[0] % COLS, lanes()
        source = jnp.where(turn >= lane, turn - lane, turn - lane + COLS)
        in_half = source % HALF
        few = jnp.concatenate([pick(fold_half[...], in_half), pick(fold_half[...], in_half + HALF)], axis=0)
        many = pick(fold_whole[...], source)
        column = lax.broadcasted_iota(jnp.int32, (ROW_BUFFER, COLS), 1)
        whole_is_first = turn >= HALF
        first = (column <= turn).astype(jnp.int32)
        north[...] = jnp.where(first == whole_is_first.astype(jnp.int32), many, few)

    settle_rows(first_in, second_in, south, north, beyond_fold)
    for field, _, a, at, count in first_pieces():
        h[field, a, 8 - count : 8, :] = south[at : at + count, :]
        h[field, a, 8 : 8 + count, :] = north[at : at + count, :]
    for quad, member, at, count in SINGLES:
        hx[quad, member, 8 - count : 8, :] = south[at : at + count, :]
        hx[quad, member, 8 : 8 + count, :] = north[at : at + count, :]
    for field, n, a, at, count in rest_pieces():
        rest_h[n - 1, field, a, 8 - count : 8, :] = south[at : at + count, :]
        rest_h[n - 1, field, a, 8 : 8 + count, :] = north[at : at + count, :]
    slots = block_slots(lambda field, a: h[field, a], [hx[0, f] for f in range(4)])
    slots += single_slots(lambda q, a: hx[q, a]) + [None]
    strip_at = [(own, k) for k in range(11)] + [None]
    for n in range(REST):
        slots += [[rest_h[n, field, a] for a in range(4)] for field in range(3)] + [None]
        strip_at += [(rest_own, 3 * n + k) for k in range(3)] + [None]
    pack_columns(slots, strip_at, to_west, to_east, 0, 16)


BROUGHT = 5


def ext_lanes():
    return lax.broadcasted_iota(jnp.int32, (EXT, COLS), 1)


def barrier_masks():
    comp, _, _, is_top = places()
    row = lax.broadcasted_iota(jnp.int32, (EXT, COLS), 0)
    apart = is_top & (comp == 0)
    keep_c = jnp.where(apart & (row == 40), 0.0, 1.0).astype(F32)
    keep_d = jnp.where(apart & (row == 39), 0.0, 1.0).astype(F32)
    return stack([keep_c] * 5), stack([keep_d] * 5)


def edges_of(slot, west, east):
    group = lax.broadcasted_iota(jnp.int32, west.shape, 1) % 32
    edge = jnp.where(group < 8, roll_lanes(west, -8 * slot), roll_lanes(east, 24 - 8 * slot))
    return edge, (group >= 8) & (group < 24)


def assemble_strip(slot, sides, buffer, mid, halo_buffer=None, halo=None):
    rows = pl.ds(pl.multiple_of(COL_OWN + ROWS * buffer, 8), ROWS)
    edge, inner = edges_of(slot, sides[0][rows, :], sides[1][rows, :])
    middle = jnp.where(inner, mid, edge)
    if halo is None:
        return middle
    rows = pl.ds(pl.multiple_of(16 * halo_buffer, 8), 16)
    edge, inner = edges_of(slot, sides[0][rows, :], sides[1][rows, :])
    outer = jnp.where(inner, halo, edge)
    return jnp.concatenate([outer[0:8], middle, outer[8:16]], axis=0)


class First:
    def __init__(self, lam, winds, inv, h, own, own_halo, from_west, from_east, x_in, hx):
        self.lam, self.winds, self.inv, self.h = lam, winds, inv, h
        self.own, self.own_halo, self.sides = own, own_halo, (from_west, from_east)
        self.x_in, self.hx = x_in, hx

    def main(self, field, n, a):
        halo = self.h[field, a]
        mid = field_ref(self.lam, self.winds, self.inv, field, 0, a)[...]
        return jnp.concatenate([halo[0:8], mid, halo[8:16]], axis=0)

    def single(self, quad, a):
        halo = self.hx[quad, a]
        return jnp.concatenate([halo[0:8], self.x_in[quad, a], halo[8:16]], axis=0)

    def strip(self, n, which, slot):
        at = 4 * which + slot
        return assemble_strip(slot, self.sides, which, self.own[at], which, self.own_halo[at])

    def single_strip(self, quad):
        return self.strip(0, 0, 3) if quad == 0 else self.strip(0, 2, quad - 1)


class Rest:
    def __init__(self, lam, winds, inv, h, own, own_halo, from_west, from_east):
        self.lam, self.winds, self.inv, self.h = lam, winds, inv, h
        self.own, self.own_halo, self.sides = own, own_halo, (from_west, from_east)

    def main(self, field, n, a):
        mid = field_ref(self.lam, self.winds, self.inv, field, n, a)[...]
        if field >= 3:
            return mid
        halo = self.h[n - 1, field, a]
        return jnp.concatenate([halo[0:8], mid, halo[8:16]], axis=0)

    def strip(self, n, which, slot):
        mid = self.own[8 * (n - 1) + 4 * which + slot]
        buffer = 3 + 2 * (n - 1) + which
        if which == 1:
            return assemble_strip(slot, self.sides, buffer, mid)
        return assemble_strip(slot, self.sides, buffer, mid, 2 + n, self.own_halo[3 * (n - 1) + slot])


def stack(values):
    return jnp.concatenate(values, axis=0)


def unstack(value):
    return [value[EXT * k : EXT * (k + 1)] for k in range(value.shape[0] // EXT)]


def replicate(strip, a):
    lane = ext_lanes()
    out = roll_lanes(strip, -32 * a)
    base = jnp.where(lane < 32, out, 0.0)
    for g in range(1, 4):
        base = jnp.where((lane >= 32 * g) & (lane < 32 * g + 32), roll_lanes(out, 32 * g), base)
    return base


def advect(tracer, coefs, land):
    to_south, to_north, to_west = coefs
    for _ in range(3):
        a = to_west[...] * tracer
        b = (2 * DIFFUSE) * tracer - a
        east, west = roll_lanes(a, -1), roll_lanes(b, 1)
        new = (1.0 - 4 * DIFFUSE) * tracer
        new = new + roll_rows(to_south[...] * tracer, -1) + roll_rows(to_north[...] * tracer, 1)
        tracer = (new + (east + west)) * land[...]
    return tracer


def coefficients(fields, n, masks):
    merid = stack([fields.main(1, n, a) for a in range(4)] + [fields.strip(n, 0, 1)])
    zonal = stack([fields.main(2, n, a) for a in range(4)] + [fields.strip(n, 0, 2)])
    to_south = (DIFFUSE + 0.5 * merid) * masks[0]
    to_north = (DIFFUSE - 0.5 * merid) * masks[1]
    return to_south, to_north, DIFFUSE + 0.5 * zonal


def solve(inverse, strip_inverse, old):
    moved = [old[4]] + [roll_lanes(old[4], -32 * d) for d in range(1, 4)]
    new = []
    for a in range(4):
        total = inverse(a, 0) * old[0]
        for b in range(1, 4):
            total = total + inverse(a, b) * old[b]
        new.append(total)
    total = strip_inverse(0) * moved[0]
    for d in range(1, 4):
        total = total + strip_inverse(d) * moved[d]
    return new + [total]


def solve_first(inverse, strip_inverse, tracer):
    return solve(lambda a, b: inverse[4 * a + b], lambda d: strip_inverse[d], unstack(tracer))


def main_from_strip(main, strip, a, width):
    lane = lax.broadcasted_iota(jnp.int32, main.shape, 1)
    main = jnp.where(lane < width, roll_lanes(strip, -(32 * a + 8)), main)
    return jnp.where(lane >= COLS - width, roll_lanes(strip, 104 - 32 * a), main)


def merge(state):
    strip = state[4]
    lane = lax.broadcasted_iota(jnp.int32, strip.shape, 1)
    new_strip = strip
    mains = [main_from_strip(state[a], strip, a, 3) for a in range(4)]
    for a in range(4):
        west = (lane >= 32 * a + 11) & (lane < 32 * a + 16)
        east = (lane >= 32 * a + 16) & (lane < 32 * a + 21)
        new_strip = jnp.where(west, roll_lanes(state[a], 32 * a + 8), new_strip)
        new_strip = jnp.where(east, roll_lanes(state[a], 32 * a + 24), new_strip)
    return mains + [new_strip]


def load_block(fields, n):
    return [fields.main(0, n, a) for a in range(4)] + [fields.strip(n, 0, 0)]


def fluxes_out(fields, state, payload, strips):
    surface = state[0] * fields.single(3, 1)
    for f in range(4):
        payload[f] = fields.single(0, f) * surface
    payload[4] = strips[0] * replicate(state[4] * strips[1], 0)


def couple(fields, received, strip_coefs, strip_weights, land_strip):
    sources = [received[f] for f in range(4)] + [roll_lanes(received[4], -32 * f) for f in range(4)]
    coefs = [fields.single(0, f) for f in range(4)] + [strip_coefs[f] for f in range(4)]
    weights = [fields.single(1 + s // 4, s % 4) for s in range(9)]
    moved = {dc: [roll_lanes(source, -dc) for source in sources] for dc in (-1, 0, 1)}
    totals = []
    for table, parts in ((weights, range(4)), ([strip_weights[s] for s in range(9)], range(4, 8))):
        total = None
        for k in parts:
            part = None
            for dr in (-1, 0, 1):
                across = None
                for dc in (-1, 0, 1):
                    term = table[3 * (dr + 1) + dc + 1] * roll_rows(moved[dc][k], -dr)
                    across = term if across is None else across + term
                part = across if part is None else part + across
            total = coefs[k] * part if total is None else total + coefs[k] * part
        totals.append(total)
    return totals[0] * fields.single(3, 2), totals[1] * land_strip


INPUTS = 8


def first_kernel(*refs):
    fields = First(*refs[: INPUTS + 2])
    payload, state, land, to_south, to_north, to_west, strip_coefs, strip_weights = refs[INPUTS + 2 : INPUTS + 10]
    inverse, strip_inverse, flux_strips = refs[INPUTS + 10 :]
    quads = [fields.single_strip(q) for q in range(4)]
    main_land = fields.single(3, 2)
    land[...] = stack([main_land] * 4 + [replicate(quads[3], 2)])
    coefs = (to_south, to_north, to_west)
    for ref, value in zip(coefs, coefficients(fields, 0, barrier_masks()), strict=True):
        ref[...] = value
    tracer = advect(stack(load_block(fields, 0)), coefs, land)
    for a in range(4):
        for b in range(4):
            inverse[4 * a + b] = fields.main(3 + b, 0, a)
        strip_inverse[a] = fields.strip(0, 1, a)
    flux_strips[0] = quads[0]
    flux_strips[1] = roll_lanes(quads[3], -32)
    merged = merge(solve_first(inverse, strip_inverse, tracer))
    for a in range(5):
        state[a] = merged[a]
    fluxes_out(fields, merged, payload, flux_strips)
    for f in range(4):
        strip_coefs[f] = roll_lanes(quads[0], -32 * f)
    for k in range(9):
        strip_weights[k] = roll_lanes(quads[1 + k // 4], -32 * (k % 4))


def own_rows(tracer):
    return [value[8:40] for value in unstack(tracer)]


def rest_first_kernel(*refs):
    fields = Rest(*refs[:INPUTS])
    land, state, coefs, strip_inverse, first_out, second_out, mirror_out, edges, store, mask_c, mask_d = refs[INPUTS:]
    mask_c[...], mask_d[...] = barrier_masks()

    def block(n, carry):
        mine = tuple(coefs.at[n - 1, k] for k in range(3))
        for ref, value in zip(mine, coefficients(fields, n, (mask_c[...], mask_d[...])), strict=True):
            ref[...] = value
        tracer = advect(stack(load_block(fields, n)), mine, land)
        for d in range(4):
            strip_inverse[n - 1, d] = fields.strip(n, 1, d)
        merged = merge(
            solve(lambda a, b: fields.main(3 + b, n, a), lambda d: strip_inverse[n - 1, d], own_rows(tracer))
        )
        for a in range(5):
            state[n - 1, a] = merged[a]
            edges[0, n - 1, a] = merged[a][24:32]
            edges[1, n - 1, a] = merged[a][0:8]
            edges[2, n - 1, a] = reverse(merged[a][24:32])
        return carry

    lax.fori_loop(1, BLOCKS, block, 0)
    for n in range(REST):
        for a in range(5):
            at = 24 * a + 3 * n
            store[0, at : at + 3, :] = edges[0, n, a, 5:8, :]
            store[1, at : at + 3, :] = edges[1, n, a, 0:3, :]
            store[2, at : at + 3, :] = edges[2, n, a, 0:3, :]
    for k in range(3):
        for a in range(5):
            store[k, 24 * a + 21 : 24 * a + 24, :] = jnp.zeros((3, COLS), F32)
    hand_over(store, first_out, second_out, mirror_out)


def rest_second_kernel(*refs):
    fold, inv, strip_inverse, land, state, coefs, first_in, second_in, fold_a, fold_b = refs[:10]
    out, result, south, north, halo, sem = refs[10:]

    def beyond_fold():
        turn, lane = fold[0] % COLS, lanes()
        source = jnp.where(turn >= lane, turn - lane, turn - lane + COLS)
        keep = lax.broadcasted_iota(jnp.int32, (24, COLS), 1) <= turn
        group, in_group = lane // 32, lane % 32
        column = jnp.where(in_group < 16, in_group - 8, in_group + 104)
        at_a = turn - column
        at_b = at_a + COLS
        main_a, main_b = jnp.clip(at_a, 0, COLS - 1), jnp.clip(at_b, 0, COLS - 1)
        strip_a = 32 * group + jnp.clip(at_a - 104, 0, 31)
        strip_b = 32 * group + jnp.clip(at_b + 8, 0, 31)
        wide_a = stack([at_a] * 3)
        wide_b = stack([at_b] * 3)
        wide_group = stack([group] * 3)
        strip = jnp.where(wide_a >= COLS, pick(fold_a[96:120, :], strip_a), pick(fold_b[96:120, :], strip_b))
        for a in range(4):
            values_a, values_b = fold_a[24 * a : 24 * a + 24, :], fold_b[24 * a : 24 * a + 24, :]
            north[24 * a : 24 * a + 24, :] = jnp.where(keep, pick(values_a, source), pick(values_b, source))
            inside = (wide_group == a) & (wide_a < COLS) & (wide_b >= 0)
            strip = jnp.where(inside, jnp.where(wide_a >= 0, pick(values_a, main_a), pick(values_b, main_b)), strip)
        north[96:120, :] = strip

    settle_rows(first_in, second_in, south, north, beyond_fold)
    for n in range(REST):
        for a in range(5):
            at = 24 * a + 3 * n
            halo[n, a, 5:8, :] = south[at : at + 3, :]
            halo[n, a, 8:11, :] = north[at : at + 3, :]

    def leave(n):
        return pltpu.make_async_copy(result.at[pl.ds(4 * (n - 1), 4)], out.at[pl.ds(4 * n, 4)], sem.at[n - 1])

    def block(n, carry):
        mine = tuple(coefs.at[n - 1, k] for k in range(3))
        parts = []
        for a in range(5):
            edge = halo[n - 1, a]
            parts += [edge[0:8], state[n - 1, a], edge[8:16]]
        tracer = advect(stack(parts), mine, land)
        solved = solve(lambda a, b: inv[n, a, b], lambda d: strip_inverse[n - 1, d], own_rows(tracer))
        for a in range(4):
            result[4 * (n - 1) + a] = main_from_strip(solved[a], solved[4], a, 3)
        leave(n).start()
        return carry

    lax.fori_loop(1, BLOCKS, block, 0)
    for n in range(1, BLOCKS):
        leave(n).wait()


def second_kernel(
    x_in, hx, land, to_south, to_north, to_west, strip_coefs, strip_weights, inverse, strip_inverse, flux_strips,
    received, state_in, payload, state,
):
    fields = First(*[None] * 8, x_in, hx)
    added, added_strip = couple(fields, received, strip_coefs, strip_weights, land[4 * EXT :])
    lane = ext_lanes()
    strip = state_in[4] + jnp.where(lane < 32, added_strip, 0.0)
    top = main_from_strip(state_in[0] + added, strip, 0, 1)
    tracer = stack([top] + [state_in[a] for a in range(1, 4)] + [strip])
    solved = solve_first(inverse, strip_inverse, advect(tracer, (to_south, to_north, to_west), land))
    merged = [main_from_strip(solved[a], solved[4], a, 3) for a in range(4)] + [solved[4]]
    for a in range(5):
        state[a] = merged[a]
    fluxes_out(fields, merged, payload, flux_strips)


def last_kernel(x_in, hx, land, strip_coefs, strip_weights, received, state, rest, out, result, sem):
    del rest
    fields = First(*[None] * 8, x_in, hx)
    added, added_strip = couple(fields, received, strip_coefs, strip_weights, land[4 * EXT :])
    strip = state[4] + added_strip
    result[0] = main_from_strip(state[0] + added, strip, 0, 1)[8:40]
    for a in range(1, 4):
        result[a] = state[a][8:40]
    copy_all([(result, out.at[pl.ds(0, 4)])], sem)


MICROSECONDS = {
    "start_rows_kernel": 3.2,
    "own_kernel": 4.0,
    "halo_kernel": 2.8,
    "first_kernel": 1.0,
    "rest_first_kernel": 4.3,
    "second_kernel": 1.0,
    "last_kernel": 0.5,
    "rest_second_kernel": 4.6,
}


def call(kernel, outs, args, specs, scratch=(), params=PARAMS, **more):
    cost = int(MICROSECONDS[kernel.__name__] * 3.5e6)
    return pl.pallas_call(
        kernel,
        out_shape=[jax.ShapeDtypeStruct(s, jnp.int32 if spec is SMEM else F32) for s, spec in outs],
        in_specs=specs,
        out_specs=[spec for _, spec in outs],
        scratch_shapes=list(scratch),
        compiler_params=params,
        cost_estimate=pl.CostEstimate(flops=0, bytes_accessed=cost, transcendentals=0),
        **more,
    )(*args)


def index(c, a, o):
    return (c * LAT + a) * LON + o % LON


def lon_pairs(do):
    return [(index(c, a, o), index(c, a, o + do)) for c in range(2) for a in range(LAT) for o in range(LON)]


def swap_pairs(start):
    pairs = []
    for c in range(2):
        for a in range(start, LAT - 1, 2):
            for o in range(LON):
                pairs += [(index(c, a, o), index(c, a + 1, o)), (index(c, a + 1, o), index(c, a, o))]
    return pairs


def fold_pairs(total, comps):
    return [(index(c, LAT - 1, o), index(c, LAT - 1, total - o)) for c in comps for o in range(LON)]


def body(
    adjoint_state,
    winds,
    block_inverse,
    flux_coef,
    sea_mask,
    intersection_cell,
    intersection_weight,
    fold_map,
):
    lam = adjoint_state[0]
    wind = winds[:, 0]
    inv = block_inverse[0]
    rows = (ROW_BUFFER, COLS)
    x, first, second, mirror, low, high, turn, half_turn = call(
        start_rows_kernel,
        [((4, 4, ROWS, COLS), VMEM)] + [(rows, VMEM)] * 3 + [((ROW_BUFFER // 2, COLS), VMEM)] * 2 + [((1,), SMEM)] * 2,
        (fold_map, lam, wind, inv, flux_coef[0], sea_mask, intersection_cell, intersection_weight),
        [SMEM] + [HBM] * 7,
        [
            pltpu.VMEM((3, *rows), F32),
            pltpu.VMEM((32, 16, COLS), F32),
            pltpu.VMEM((2, 32, 16, COLS), F32),
            pltpu.VMEM((1, 4, 4, 16, COLS), F32),
            pltpu.VMEM((4, ROWS, COLS), F32),
            pltpu.VMEM((ROWS, COLS), jnp.int32),
            pltpu.VMEM((2, 4, ROWS, COLS), jnp.int32),
            pltpu.VMEM((4, ROWS, COLS), F32),
            pltpu.SemaphoreType.DMA((10,)),
        ],
        FULL,
    )
    def swap(first, second):
        return lax.ppermute(first, AXES, swap_pairs(0)), lax.ppermute(second, AXES, swap_pairs(1))

    def around(to_west, to_east):
        return lax.ppermute(to_east, AXES, lon_pairs(1)), lax.ppermute(to_west, AXES, lon_pairs(-1))

    def across(value):
        return lax.ppermute(value, AXES, [(i, (i + LAT * LON) % (2 * LAT * LON)) for i in range(2 * LAT * LON)])

    def vmem(*shape):
        return ((*shape, COLS), VMEM)

    state_in = (lam, wind, inv)
    swapped = swap(first, second)

    def across_fold(step, mirror, low, high, lam, wind, inv, x):
        total, in_late_half = step // 2, step % 2
        whole = lax.ppermute(mirror, AXES, fold_pairs(total - 1 + in_late_half, (0, 1)))
        half = lax.ppermute(high if in_late_half else low, AXES, fold_pairs(total - in_late_half, (0, 1)))
        folded = (whole, half)
        own = call(
            own_kernel,
            [vmem(12, ROWS), vmem(3 * ROWS), vmem(3 * ROWS)]
            + [vmem(4, ROWS), vmem(2, 4, ROWS), vmem(1, 4, 4, ROWS)]
            + [vmem(8 * REST, ROWS), vmem(2 * REST * ROWS), vmem(2 * REST * ROWS)],
            (lam, wind, inv, x),
            [HBM] * 4,
            [
                pltpu.VMEM((32, ROWS, COLS), F32),
                pltpu.VMEM((2, 32, ROWS, COLS), F32),
                pltpu.VMEM((BLOCKS, 4, 4, ROWS, COLS), F32),
                pltpu.VMEM((4, 4, ROWS, COLS), F32),
                pltpu.SemaphoreType.DMA((4,)),
                pltpu.SemaphoreType.DMA((REST, 3)),
            ],
        )
        return *folded, *own

    *folded, own, mid_west, mid_east, lam0, wind0, inv0, rest_own, rest_mid_west, rest_mid_east = lax.switch(
        half_turn[0], [functools.partial(across_fold, step) for step in range(2 * LON)], mirror, low, high, lam, wind, inv, x
    )
    moved = (*swapped, *folded)
    brought = (own, lam0, wind0, inv0, rest_own)
    h, hx, own_halo, rest_h, rest_own_halo, to_west, to_east, own, lam0, wind0, inv0, rest_own = call(
        halo_kernel,
        [vmem(7, 4, 16), vmem(4, 4, 16), vmem(12, 16), vmem(REST, 3, 4, 16), vmem(3 * REST, 16)]
        + [vmem(COL_BUFFER)] * 2
        + [(value.shape, VMEM) for value in brought],
        (fold_map, *moved, mid_west, mid_east, rest_mid_west, rest_mid_east, *brought),
        [SMEM] + [VMEM] * (8 + BROUGHT),
        [pltpu.VMEM((ROW_BUFFER, COLS), F32)] * 2,
    )
    from_sides = around(to_west, to_east)
    five = vmem(5, EXT)
    tall = vmem(5 * EXT)
    payload, state, land, *tables = call(
        first_kernel,
        [five, five] + [tall] * 4 + [vmem(k, EXT) for k in (4, 9, 16, 4, 2)],
        (lam0, wind0, inv0, h, own, own_halo, *from_sides, x, hx),
        [VMEM] * (INPUTS + 2),
    )
    rest_args = (*state_in, rest_h, rest_own, rest_own_halo, *from_sides)
    whole = ((32, ROWS, COLS), HBM)
    done = pltpu.SemaphoreType.DMA((1,))
    rest_state, rest_coefs, strip_inverse, *rest_rows = call(
        rest_first_kernel,
        [vmem(REST, 5, ROWS), vmem(REST, 3, 5 * EXT), vmem(REST, 4, ROWS)] + [vmem(120)] * 3,
        (*rest_args, land),
        [VMEM] * (INPUTS + 1),
        [pltpu.VMEM((3, REST, 5, 8, COLS), F32), pltpu.VMEM((3, 120, COLS), F32)]
        + [pltpu.VMEM((5 * EXT, COLS), F32)] * 2,
    )
    def finish(total, rest_rows, payload, chain, rest_args):
        received = across(payload)
        folded = [lax.ppermute(rest_rows[2], AXES, fold_pairs(total - k, (1,))) for k in range(2)]
        swapped = swap(*rest_rows[:2])
        x, hx, land, *tables, state = chain
        payload, state = call(second_kernel, [five, five], (x, hx, land, *tables, received, state), [VMEM] * 13)
        payload, swapped, folded = lax.optimization_barrier((payload, swapped, folded))
        received = across(payload)
        (rest,) = call(
            rest_second_kernel,
            [whole],
            (*rest_args, *swapped, *folded),
            [SMEM] + [VMEM] * 9,
            [
                pltpu.VMEM((4 * REST, ROWS, COLS), F32),
                pltpu.VMEM((120, COLS), F32),
                pltpu.VMEM((120, COLS), F32),
                pltpu.VMEM((REST, 5, 16, COLS), F32),
                pltpu.SemaphoreType.DMA((REST,)),
            ],
        )
        return call(
            last_kernel,
            [whole],
            (x, hx, land, *tables[3:5], received, state, rest),
            [VMEM] * 7 + [HBM],
            [pltpu.VMEM((4, ROWS, COLS), F32), done],
            input_output_aliases={7: 0},
        )[0]

    out = lax.switch(
        turn[0],
        [functools.partial(finish, total) for total in range(LON)],
        rest_rows,
        payload,
        (x, hx, land, *tables, state),
        (fold_map, inv, strip_inverse, land, rest_state, rest_coefs),
    )
    return out[None]


def solution(mesh):
    return jax.shard_map(
        body,
        mesh=mesh,
        in_specs=(
            P("comp", None, "lat", "lon"),
            P(None, "comp", None, "lat", "lon"),
            P("comp", None, None, None, "lat", "lon"),
            P("comp", None, "lat", "lon"),
            P("lat", "lon"),
            P(None, None, "lat", "lon"),
            P(None, "lat", "lon"),
            P(),
        ),
        out_specs=P("comp", None, "lat", "lon"),
        check_vma=False,
    )
```
